32 devices in a mesh: section: 2 (over core), wide: 16 (over z, y, x).
Axes of the slice: x: 2, y: 2, z: 4, core: 2. Of those that a mesh axis runs over, the one named last changes fastest.
Arguments:
- frames: bfloat16 [1024, 48, 1024], P(('section', 'wide')), may hold values from -6 to 6
- qkv_weight: bfloat16 [1024, 3072], replicated, may hold values from -0.1875 to 0.1875
- out_weight: bfloat16 [1024, 1024], replicated, may hold values from -0.1875 to 0.1875
- proj_weight: bfloat16 [1024, 512], replicated, may hold values from -0.1875 to 0.1875
- mlp_weight: bfloat16 [1536, 1024], replicated, may hold values from -0.15625 to 0.15625
- logit_weight: bfloat16 [1024], replicated, may hold values from -0.1875 to 0.1875
- history: bfloat16 [128, 2048, 512], P(('section', 'wide')), may hold values from -6 to 6
- hist_len: int32 [128], P(('section', 'wide')), may hold values from 1 to 2048, as said below
- hist_mask: int32 [128, 2048], P(('section', 'wide')), may hold values 0 or 1
- req_owner: int32 [24576, 1], P(('section', 'wide')), may hold values from 0 to 31; in each aligned block of 768 rows (0 to 767, 768 to 1535, ...) at most 48 rows name the same one
- req_local: int32 [24576], P(('section', 'wide')), may hold values from 0 to 31
- labels: int32 [24576], P(('section', 'wide')), may hold values 0 or 1
Outputs:
- logits: float32 [24576], P(('section', 'wide'))
- grad_proj: float32 [1024, 512], P(('section', 'wide'))
The draws below stay inside these ranges and needn't reach their ends.
Inputs may be any that keep to these rules, and one draw needn't show every extreme that they name: `hist_len`: some user has 2048 events and some user has 1. `req_owner`: among the 768 requests of one device at most 48 name the same device, and exactly 48 do on some device.
All inputs are finite; a program needn't handle non-finite values. No bound on the sum of `hist_mask` or of `labels` on one device may be relied on, other than what follows from the above.
Results may differ from the reference program's by a relative error of at most 0.01.
Values may be sent and summed in bfloat16 or wider, within the bound.
No kernel may reach another device: no remote copies, remote signals or barrier semaphores. Data moves between devices by JAX's collectives and lax.ppermute only.
A program may use at most 128 MiB of HBM per device.

```python
import math
import jax
import jax.numpy as jnp
import numpy as np
from jax import lax

D = 1024
HEADS = 16
HD = 64
FRAMES = 3
PATCHES = 16
C_DEV = 32
DK = 512
H = 1024
HIST = 2048
U_DEV = 4
R_USER = 192
CANDS = 1024
USERS = 128
REQ_DEV = 768
REQS = 24576
CAP = 48
DEVICES = 32


def draw_hist_len(key, part):
    lengths = jax.random.randint(jax.random.fold_in(key, 11), (USERS,), 1, HIST + 1)
    longest = jax.random.randint(jax.random.fold_in(key, 12), (), 0, USERS)
    shortest = (longest + 1 + jax.random.randint(jax.random.fold_in(key, 13), (), 0, USERS - 1)) % USERS
    return lengths.at[longest].set(HIST).at[shortest].set(1).astype(jnp.int32)


def place_ends(array, rng, smallest, top_value):
    shape = array.shape
    spot = [jax.random.randint(jax.random.fold_in(rng, axis), (), 0, shape[axis]) for axis in range(len(shape))]
    array = array.at[tuple(spot)].set(smallest)
    longest = shape.index(max(shape))
    spot[longest] = (spot[longest] + 1) % shape[longest]
    return array.at[tuple(spot)].set(top_value)


def levels(rng, dims, split, least, top_value):
    gain, own = 1.0, jax.random.fold_in(rng, 6)
    for dim, shards_of in split:
        heights = jnp.exp(jax.random.uniform(jax.random.fold_in(own, dim), (shards_of,), jnp.float32, least / len(split), top_value / len(split)))
        gain = gain * jnp.repeat(heights, dims[dim] // shards_of).reshape([-1 if axis == dim else 1 for axis in range(len(dims))])
    return gain


def routed_block(own_key, own, number, rows, amount, top, bound, slope):
    sequence = jax.random.permutation(own_key, amount)
    crowded, ordinary = portions_of(amount, rows * top, bound, slope, True), portions_of(amount, rows * top, bound, slope, False)
    places = jnp.arange(amount)

    def named(sizes, rotation):
        used = int((sizes > 0).sum())
        fixed = max(1, used // 4)
        passed = fixed + (places - fixed + rotation * (used - fixed)) % max(1, amount - fixed)
        return jnp.zeros((amount,), jnp.int32).at[sequence[jnp.where(places < fixed, places, passed)]].set(jnp.asarray(sizes, jnp.int32))

    sizes = jnp.where(number % 4 == 0, named(crowded, number // 4), named(ordinary, number - number // 4 - 1))
    mixed = jax.random.permutation(jax.random.fold_in(own, 3), amount)
    donor, receiver = mixed[0:amount // 2 * 2:2], mixed[1:amount // 2 * 2:2]
    slack = jnp.minimum(sizes[donor] - 1, bound - sizes[receiver]) // 2
    slack = jnp.where((donor == sequence[0]) | (receiver == sequence[0]) | (sizes[receiver] == 0), 0, jnp.maximum(slack, 0))
    passed = jax.random.randint(jax.random.fold_in(own, 4), (amount // 2,), 0, 1 << 20) % (slack + 1)
    sizes = sizes.at[donor].add(-passed).at[receiver].add(passed)
    items = jnp.searchsorted(jnp.cumsum(sizes), jnp.arange(rows * top), side="right").astype(jnp.int32)
    listing = items.reshape(top, rows).T
    listing = listing[jax.random.permutation(jax.random.fold_in(own, 1), rows)]
    rotation = jax.random.randint(jax.random.fold_in(own, 2), (rows, 1), 0, top)
    return jnp.take_along_axis(listing, (jnp.arange(top)[None, :] + rotation) % top, axis=1)


def portions_of(number_of, total, bound, skew, full):
    portions = [(1 << 20) // math.isqrt(standing ** skew) + 1 for standing in range(1, number_of + 1)]
    largest = bound if full else min(bound, max(-(-total // number_of), total * portions[0] // sum(portions)))
    least = 1 if total - largest >= number_of - 1 else 0
    holding, surplus = [largest] + [least] * (number_of - 1), total - largest - least * (number_of - 1)
    while surplus > 0:
        movable = [i for i in range(1, number_of) if holding[i] < largest] or [i for i in range(1, number_of) if holding[i] < bound]
        mass, budget = sum([portions[i] for i in movable]), surplus
        for i in movable:
            extra = min(bound - holding[i], max(1, budget * portions[i] // mass), surplus)
            holding[i] = holding[i] + extra
            surplus = surplus - extra
    return np.array(holding)


def bell_draw(key, dims, scale, bound, cuts=(), kind=jnp.bfloat16):
    entries = jax.random.normal(key, dims, jnp.float32) * scale
    if len(cuts) > 0:
        entries = levels(key, dims, cuts, -0.22, 0.18) * entries
    return jnp.clip(entries, min=-bound, max=bound).astype(kind)


def setup_inputs(seed: int = 0) -> dict:
    seeds = jax.random.split(jax.random.key(seed), 13)
    frames = bell_draw(seeds[0], (CANDS, FRAMES * PATCHES, D), 1.0, 6.0, ((0, 32),))
    qkv_weight = bell_draw(seeds[1], (D, 3 * D), D ** -0.5, 0.1875)
    out_weight = bell_draw(seeds[2], (D, D), D ** -0.5, 0.1875)
    proj_weight = bell_draw(seeds[3], (D, DK), D ** -0.5, 0.1875)
    mlp_weight = bell_draw(seeds[4], (3 * DK, H), (3 * DK) ** -0.5, 0.15625)
    logit_weight = bell_draw(seeds[5], (H,), H ** -0.5, 0.1875)
    history = bell_draw(seeds[6], (USERS, HIST, DK), 1.0, 6.0, ((0, 32),))
    hist_len = draw_hist_len(jax.random.fold_in(seeds[12], 71), 0)
    hist_mask = place_ends((jax.random.randint(seeds[8], (USERS, HIST), 0, 4) < 3).astype(jnp.int32), jax.random.fold_in(seeds[8], 1), 0, 1)
    req_owner_keys = jax.random.split(jax.random.fold_in(seeds[9], 1), REQS // REQ_DEV)
    req_owner_turns = jax.random.permutation(jax.random.fold_in(seeds[9], 3), REQS // REQ_DEV)
    req_owner = jax.vmap(lambda own, number: routed_block(jax.random.fold_in(seeds[9], 2), own, number, REQ_DEV, DEVICES, 1, CAP, 2))(req_owner_keys, req_owner_turns).reshape((REQS, 1))
    req_local = place_ends(jax.random.randint(seeds[10], (REQS,), 0, C_DEV), jax.random.fold_in(seeds[10], 1), 0, C_DEV - 1).astype(jnp.int32)
    labels = place_ends((jax.random.randint(seeds[11], (REQS,), 0, 2) < 1).astype(jnp.int32), jax.random.fold_in(seeds[11], 1), 0, 1)
    return dict(frames=frames, qkv_weight=qkv_weight, out_weight=out_weight, proj_weight=proj_weight, mlp_weight=mlp_weight, logit_weight=logit_weight, history=history, hist_len=hist_len, hist_mask=hist_mask, req_owner=req_owner, req_local=req_local, labels=labels)


EPSILON = 1e-06

def layer_norm(values):
    center = values - lax.optimization_barrier(jnp.mean(values, axis=-1, keepdims=True))
    spread = lax.optimization_barrier(jnp.mean(jnp.square(center), axis=-1, keepdims=True))
    return center * lax.rsqrt(spread + EPSILON)

def encode_block(block_in, qkv_weight, out_weight, proj_weight):
    cand_count = block_in.shape[0]
    inputs = block_in.reshape(-1, D).astype(jnp.float32)
    normed = layer_norm(inputs).astype(jnp.bfloat16)
    packed = jnp.dot(normed, qkv_weight, preferred_element_type=jnp.float32).astype(jnp.bfloat16)
    packed = packed.reshape(cand_count * FRAMES, PATCHES, 3, HEADS, HD).astype(jnp.float32)
    scores = jnp.einsum('bphd,bqhd->bhpq', packed[:, :, 0], packed[:, :, 1]) * (1.0 / math.sqrt(HD))
    exp_scores = jnp.exp(scores)
    attn_probs = (exp_scores / lax.optimization_barrier(jnp.sum(exp_scores, axis=-1, keepdims=True))).astype(jnp.bfloat16)
    mixed_heads = jnp.einsum('bhpq,bqhd->bphd', attn_probs.astype(jnp.float32), packed[:, :, 2])
    mixed_heads = mixed_heads.astype(jnp.bfloat16).reshape(-1, D)
    hidden = inputs + jnp.dot(mixed_heads, out_weight, preferred_element_type=jnp.float32)
    pooled = layer_norm(lax.optimization_barrier(jnp.mean(hidden.reshape(cand_count, FRAMES * PATCHES, D), axis=1))).astype(jnp.bfloat16)
    embedded = jnp.dot(pooled, proj_weight, preferred_element_type=jnp.float32).astype(jnp.bfloat16)
    return (pooled, embedded)

def score_block(queries, history, usable, targets, mlp_weight, logit_weight):
    score_scale = 1.0 / math.sqrt(DK)
    query_f = queries.astype(jnp.float32)
    keys_f = history.astype(jnp.float32)
    inv_count = lax.rsqrt(lax.optimization_barrier(jnp.sum(usable, axis=1)))[:, None, None]
    scores = jnp.einsum('urd,ujd->urj', query_f, keys_f) * score_scale
    gate_sig = jax.nn.sigmoid(scores)
    weights = (gate_sig * usable[:, None, :]).astype(jnp.bfloat16)
    attended = jnp.einsum('urj,ujd->urd', weights.astype(jnp.float32), keys_f) * inv_count
    joined = jnp.concatenate([query_f, attended, query_f * attended], axis=-1).astype(jnp.bfloat16)
    pre_act = jnp.dot(joined.reshape(-1, 3 * DK), mlp_weight, preferred_element_type=jnp.float32)
    act_sig = jax.nn.sigmoid(pre_act)
    hidden_units = (pre_act * act_sig).astype(jnp.bfloat16)
    logits = jnp.dot(hidden_units, logit_weight, preferred_element_type=jnp.float32)
    dlogit = jax.nn.sigmoid(logits) - targets.reshape(-1)
    grad_pre = (dlogit[:, None] * logit_weight.astype(jnp.float32)[None, :] * (act_sig * (1.0 + pre_act * (1.0 - act_sig)))).astype(jnp.bfloat16)
    djoined = jnp.dot(grad_pre, mlp_weight.T, preferred_element_type=jnp.float32)
    djoined = djoined.reshape(queries.shape[0], queries.shape[1], 3 * DK)
    part_query = djoined[:, :, :DK]
    part_att = djoined[:, :, DK:2 * DK]
    part_prod = djoined[:, :, 2 * DK:]
    grad_att = ((part_att + part_prod * query_f) * inv_count).astype(jnp.bfloat16)
    grad_sig = jnp.einsum('urd,ujd->urj', grad_att.astype(jnp.float32), keys_f)
    grad_sig = (grad_sig * usable[:, None, :] * (gate_sig * (1.0 - gate_sig))).astype(jnp.bfloat16)
    grad_rows = part_query + part_prod * attended + jnp.einsum('urj,ujd->urd', grad_sig.astype(jnp.float32), keys_f) * score_scale
    return (logits, grad_rows)

def reference(frames, qkv_weight, out_weight, proj_weight, mlp_weight, logit_weight, history, hist_len, hist_mask, req_owner, req_local, labels):
    blocks = frames.reshape(CANDS // C_DEV, C_DEV, FRAMES * PATCHES, D)

    def encode_one(block_in):
        return encode_block(block_in, qkv_weight, out_weight, proj_weight)
    pooled, embedded = lax.map(encode_one, blocks)
    pooled = pooled.reshape(CANDS, D)
    embedded = embedded.reshape(CANDS, DK)
    cand_ids = (req_owner[:, 0] * C_DEV + req_local).astype(jnp.int32)
    queries = embedded[cand_ids]
    positions = jnp.arange(HIST, dtype=jnp.int32)
    usable = ((positions[None, :] < hist_len[:, None]) & ((hist_mask == 1) | (positions[None, :] == 0))).astype(jnp.float32)
    user_blocks = USERS // U_DEV
    targets = labels.astype(jnp.float32)

    def score_one(items):
        return score_block(items[0], items[1], items[2], items[3], mlp_weight, logit_weight)
    logits, grad_rows = lax.map(score_one, (queries.reshape(user_blocks, U_DEV, R_USER, DK), history.reshape(user_blocks, U_DEV, HIST, DK), usable.reshape(user_blocks, U_DEV, HIST), targets.reshape(user_blocks, U_DEV, R_USER)))
    cand_grad = jnp.zeros((CANDS, DK), jnp.float32).at[cand_ids].add(grad_rows.reshape(REQS, DK))
    grad_proj = jnp.dot(pooled.astype(jnp.float32).T, cand_grad, precision=lax.Precision.HIGHEST)
    return (logits.reshape(REQS), grad_proj)
```

```python
import math

import jax
import jax.numpy as jnp
from jax import lax
from jax.sharding import PartitionSpec as P

HEADS = 16
FRAMES = 3


EPSILON = 1e-06


def layer_norm(values):
    center = values - jnp.mean(values, axis=-1, keepdims=True)
    spread = jnp.mean(jnp.square(center), axis=-1, keepdims=True)
    return center * lax.rsqrt(spread + EPSILON)


def encode_block(frames, qkv_weight, out_weight, proj_weight):
    cand_count = frames.shape[0]
    tokens = frames.shape[1]
    model_width = frames.shape[2]
    head_dim = model_width // HEADS
    inputs = frames.reshape(-1, model_width).astype(jnp.float32)
    normed = layer_norm(inputs).astype(jnp.bfloat16)
    packed = jnp.dot(normed, qkv_weight, preferred_element_type=jnp.float32).astype(jnp.bfloat16)
    packed = packed.reshape(cand_count * FRAMES, tokens // FRAMES, 3, HEADS, head_dim)
    scores = jnp.einsum(
        "bphd,bqhd->bhpq", packed[:, :, 0], packed[:, :, 1], preferred_element_type=jnp.float32
    ) * (1.0 / math.sqrt(head_dim))
    exp_scores = jnp.exp(scores)
    attn_probs = (exp_scores / jnp.sum(exp_scores, axis=-1, keepdims=True)).astype(jnp.bfloat16)
    mixed_heads = jnp.einsum(
        "bhpq,bqhd->bphd", attn_probs, packed[:, :, 2], preferred_element_type=jnp.float32
    )
    mixed_heads = mixed_heads.astype(jnp.bfloat16).reshape(-1, model_width)
    hidden = inputs + jnp.dot(mixed_heads, out_weight, preferred_element_type=jnp.float32)
    pooled = layer_norm(jnp.mean(hidden.reshape(cand_count, tokens, model_width), axis=1)).astype(
        jnp.bfloat16
    )
    embedded = jnp.dot(pooled, proj_weight, preferred_element_type=jnp.float32).astype(jnp.bfloat16)
    return (pooled, embedded)


def score_block(queries, history, usable, targets, mlp_weight, logit_weight):
    key_width = queries.shape[2]
    score_scale = 1.0 / math.sqrt(key_width)
    query_f = queries.astype(jnp.float32)
    inv_count = lax.rsqrt(jnp.sum(usable, axis=1))[:, None, None]
    scores = (
        jnp.einsum("urd,ujd->urj", queries, history, preferred_element_type=jnp.float32)
        * score_scale
    )
    gate_sig = jax.nn.sigmoid(scores)
    weights = (gate_sig * usable[:, None, :]).astype(jnp.bfloat16)
    attended = (
        jnp.einsum("urj,ujd->urd", weights, history, preferred_element_type=jnp.float32) * inv_count
    )
    joined = jnp.concatenate([query_f, attended, query_f * attended], axis=-1).astype(jnp.bfloat16)
    pre_act = jnp.dot(
        joined.reshape(-1, 3 * key_width), mlp_weight, preferred_element_type=jnp.float32
    )
    act_sig = jax.nn.sigmoid(pre_act)
    hidden_units = (pre_act * act_sig).astype(jnp.bfloat16)
    logits = jnp.dot(hidden_units, logit_weight, preferred_element_type=jnp.float32)
    dlogit = jax.nn.sigmoid(logits) - targets.reshape(-1)
    grad_pre = (
        dlogit[:, None]
        * logit_weight.astype(jnp.float32)[None, :]
        * (act_sig * (1.0 + pre_act * (1.0 - act_sig)))
    ).astype(jnp.bfloat16)
    djoined = jnp.dot(grad_pre, mlp_weight.T, preferred_element_type=jnp.float32)
    djoined = djoined.reshape(queries.shape[0], queries.shape[1], 3 * key_width)
    part_query = djoined[:, :, :key_width]
    part_att = djoined[:, :, key_width : 2 * key_width]
    part_prod = djoined[:, :, 2 * key_width :]
    grad_att = ((part_att + part_prod * query_f) * inv_count).astype(jnp.bfloat16)
    grad_sig = jnp.einsum("urd,ujd->urj", grad_att, history, preferred_element_type=jnp.float32)
    grad_sig = (grad_sig * usable[:, None, :] * (gate_sig * (1.0 - gate_sig))).astype(jnp.bfloat16)
    grad_rows = (
        part_query
        + part_prod * attended
        + jnp.einsum("urj,ujd->urd", grad_sig, history, preferred_element_type=jnp.float32)
        * score_scale
    )
    return (logits, grad_rows)


def gather_rows(row_hot, rows):
    return jnp.dot(row_hot, rows, preferred_element_type=jnp.float32).astype(jnp.bfloat16)


def sum_scatter(terms, sections, wides):
    rows = terms.shape[0] // (sections * wides)
    part = terms.reshape(sections, wides * rows, terms.shape[1])
    mine = lax.axis_index("section")
    kept = lax.dynamic_index_in_dim(part, mine, 0, keepdims=False)
    sent = lax.dynamic_index_in_dim(part, 1 - mine, 0, keepdims=False)
    got = lax.ppermute(sent, "section", [(i, 1 - i) for i in range(sections)])
    total = kept.astype(jnp.float32) + got.astype(jnp.float32)
    part = total.astype(jnp.bfloat16).reshape(wides, rows, terms.shape[1])
    bit = 0
    while part.shape[0] > 1:
        groups = part.shape[0]
        mine = (lax.axis_index("wide") >> bit) & 1
        split = part.reshape(groups // 2, 2, rows, terms.shape[1])
        kept = lax.dynamic_index_in_dim(split, mine, 1, keepdims=False)
        sent = lax.dynamic_index_in_dim(split, 1 - mine, 1, keepdims=False)
        got = lax.ppermute(sent, "wide", [(i, i ^ (1 << bit)) for i in range(wides)])
        total = kept.astype(jnp.float32) + got.astype(jnp.float32)
        part = total if groups == 2 else total.astype(jnp.bfloat16)
        bit += 1
    return part[0]


def body(
    frames,
    qkv_weight,
    out_weight,
    proj_weight,
    mlp_weight,
    logit_weight,
    history,
    hist_len,
    hist_mask,
    req_owner,
    req_local,
    labels,
):
    pooled, embedded = encode_block(frames, qkv_weight, out_weight, proj_weight)
    sections, wides = lax.axis_size("section"), lax.axis_size("wide")
    requests = req_local.shape[0]
    cand_count = frames.shape[0]
    key_width = proj_weight.shape[1]
    all_embedded = lax.all_gather(embedded, ("section", "wide"), axis=0, tiled=True)
    all_pooled = lax.all_gather(pooled, ("section", "wide"), axis=0, tiled=True)
    cand_ids = req_owner[:, 0] * cand_count + req_local
    row_hot = (
        cand_ids[:, None] == jnp.arange(all_embedded.shape[0], dtype=jnp.int32)[None, :]
    ).astype(jnp.bfloat16)
    queries = gather_rows(row_hot, all_embedded)
    users = history.shape[0]
    positions = jnp.arange(history.shape[1], dtype=jnp.int32)
    usable = (
        (positions[None, :] < hist_len[:, None]) & ((hist_mask == 1) | (positions[None, :] == 0))
    ).astype(jnp.float32)
    targets = labels.astype(jnp.float32).reshape(users, requests // users)
    logits, grad_rows = score_block(
        queries.reshape(users, requests // users, key_width),
        history,
        usable,
        targets,
        mlp_weight,
        logit_weight,
    )
    grad_rows = grad_rows.reshape(requests, key_width)
    asked_rows = gather_rows(row_hot, all_pooled)
    terms = jnp.dot(
        asked_rows.T, grad_rows.astype(jnp.bfloat16), preferred_element_type=jnp.float32
    )
    grad_proj = sum_scatter(terms.astype(jnp.bfloat16), sections, wides)
    return (logits, grad_proj)


def solution(mesh):
    in_specs = (
        P(("section", "wide"), None, None),
        P(),
        P(),
        P(),
        P(),
        P(),
        P(("section", "wide"), None, None),
        P(("section", "wide")),
        P(("section", "wide"), None),
        P(("section", "wide"), None),
        P(("section", "wide")),
        P(("section", "wide")),
    )
    out_specs = (P(("section", "wide")), P(("section", "wide"), None))
    return jax.shard_map(body, mesh=mesh, in_specs=in_specs, out_specs=out_specs, check_vma=False)
```

```python
import functools
import math

import jax
import jax.numpy as jnp
from jax import lax
from jax.experimental import pallas as pl
from jax.experimental.pallas import tpu as pltpu
from jax.sharding import PartitionSpec as P

HEADS = 16
FRAMES = 3


EPSILON = 1e-06
VMEM_LIMIT = 60 * 1024 * 1024


def layer_norm(values):
    center = values - jnp.mean(values, axis=-1, keepdims=True)
    spread = jnp.mean(jnp.square(center), axis=-1, keepdims=True)
    return center * lax.rsqrt(spread + EPSILON)


def dot(left, right):
    return jnp.dot(left, right, preferred_element_type=jnp.float32)


def dot_rows(left, right):
    return lax.dot_general(left, right, (((1,), (1,)), ((), ())), preferred_element_type=jnp.float32)


def dot_columns(left, right):
    return lax.dot_general(left, right, (((0,), (0,)), ((), ())), preferred_element_type=jnp.float32)


def split_rows(values):
    high = values.astype(jnp.bfloat16)
    low = (values - high.astype(jnp.float32)).astype(jnp.bfloat16)
    return jnp.concatenate([high, low], axis=0)


def dot_split(values, right):
    both = dot(split_rows(values), right)
    rows = values.shape[0]
    return both[:rows] + both[rows:]


def encode_kernel(
    tokens,
    frames_ref,
    qkv_hbm,
    out_hbm,
    proj_hbm,
    pooled_ref,
    embedded_ref,
    qkv_ref,
    out_ref,
    proj_ref,
    sems,
    normed_ref,
    key_sums_ref,
    mixed_rows_ref,
    sums_ref,
):
    group = pl.program_id(0)
    rows, width = normed_ref.shape
    head_dim = width // HEADS
    patches = tokens // FRAMES
    cands = rows // tokens
    lanes = 2 * head_dim
    parts = 3
    copies = [
        pltpu.make_async_copy(
            qkv_hbm.at[:, pl.ds(part * width, width)],
            qkv_ref.at[:, pl.ds(part * width, width)],
            sems.at[part],
        )
        for part in range(parts)
    ]
    copies.append(pltpu.make_async_copy(out_hbm, out_ref, sems.at[parts]))
    copies.append(pltpu.make_async_copy(proj_hbm, proj_ref, sems.at[parts + 1]))

    @pl.when(group == 0)
    def _():
        for copy in copies:
            copy.start()

    inputs = frames_ref[...].astype(jnp.float32)
    sums_ref[pl.ds(pl.multiple_of(group * cands, cands), cands), :] = jnp.sum(
        inputs.reshape(cands, tokens, width), axis=1
    )
    normed_ref[...] = layer_norm(inputs).astype(jnp.bfloat16)

    @pl.when(group == 0)
    def _():
        copies[0].wait()
        copies[1].wait()

    exponent = math.log2(math.e) / math.sqrt(head_dim)
    lane = lax.broadcasted_iota(jnp.int32, (lanes, lanes), 1)
    first_head = lane < head_dim
    query_at = lax.broadcasted_iota(jnp.int32, (lanes, 2 * lanes), 0)
    key_at = lax.broadcasted_iota(jnp.int32, (lanes, 2 * lanes), 1) % lanes
    same_frame = (query_at // patches) == (key_at // patches)
    ones_row = lax.broadcasted_iota(jnp.int32, (2 * lanes, 2 * lanes), 0) // lanes
    ones_column = lax.broadcasted_iota(jnp.int32, (2 * lanes, 2 * lanes), 1) // lanes
    head_ones = (ones_row == ones_column).astype(jnp.bfloat16)

    def head_pair(pair):
        start = pl.multiple_of(pair * lanes, lanes)
        weight = jnp.concatenate(
            [qkv_ref[:, pl.ds(start, lanes)], qkv_ref[:, pl.ds(width + start, lanes)]], axis=1
        )
        packed = dot(normed_ref[...], weight).astype(jnp.bfloat16)
        found = []
        for block in range(rows // lanes):
            query = packed[block * lanes : (block + 1) * lanes, :lanes]
            key = packed[block * lanes : (block + 1) * lanes, lanes:]
            zero = jnp.zeros_like(key)
            keys = jnp.concatenate(
                [jnp.where(first_head, key, zero), jnp.where(first_head, zero, key)], axis=0
            )
            scores = dot_rows(query, keys)
            exp_scores = jnp.where(same_frame, jnp.exp2(scores * exponent), 0.0)
            totals = dot(exp_scores.astype(jnp.bfloat16), head_ones)
            found.append(jnp.sum(exp_scores / totals, axis=0, keepdims=True))
        for head in range(2):
            row = jnp.concatenate(
                [part[:, head * lanes : (head + 1) * lanes] for part in found], axis=1
            )
            key_sums_ref[2 * pair + head] = row

    for pair in range(HEADS // 2):
        head_pair(pair)

    own = lax.broadcasted_iota(jnp.int32, (cands, rows), 1) // tokens == lax.broadcasted_iota(
        jnp.int32, (cands, rows), 0
    )
    spread = jnp.concatenate(
        [jnp.where(own, key_sums_ref[head], 0.0) for head in range(HEADS)], axis=0
    ).astype(jnp.bfloat16)
    mixed_rows = dot(spread, normed_ref[...])
    for head in range(HEADS):
        mixed_rows_ref[head, pl.ds(pl.multiple_of(group * cands, cands), cands), :] = mixed_rows[
            head * cands : (head + 1) * cands
        ]

    @pl.when(group == pl.num_programs(0) - 1)
    def _():
        for copy in copies[2:]:
            copy.wait()
        total = pooled_ref.shape[0]
        quad = 4
        span = quad * head_dim
        pieces = []
        for part in range(HEADS // quad):
            left = mixed_rows_ref[pl.ds(part * quad, quad)].reshape(quad * total, width)
            both = dot_split(left, qkv_ref[:, pl.ds(2 * width + part * span, span)])
            head_at = lax.broadcasted_iota(jnp.int32, (total, span), 1) // head_dim
            piece = jnp.zeros((total, span), jnp.float32)
            for head in range(quad):
                piece = jnp.where(head_at == head, both[head * total : (head + 1) * total], piece)
            pieces.append(piece)
        mixed_mean = jnp.concatenate(pieces, axis=1) * (1.0 / tokens)
        hidden = sums_ref[...] * (1.0 / tokens) + dot_split(mixed_mean, out_ref[...])
        pooled = layer_norm(hidden).astype(jnp.bfloat16)
        pooled_ref[...] = pooled
        embedded_ref[...] = dot(pooled, proj_ref[...]).astype(jnp.bfloat16)


def encode_block(frames, qkv_weight, out_weight, proj_weight):
    cand_count, tokens, width = frames.shape
    key_width = proj_weight.shape[1]
    cands = 8
    rows = cands * tokens
    return pl.pallas_call(
        functools.partial(encode_kernel, tokens),
        grid=(cand_count // cands,),
        in_specs=[
            pl.BlockSpec((rows, width), lambda group: (group, 0)),
            pl.BlockSpec(memory_space=pl.ANY),
            pl.BlockSpec(memory_space=pl.ANY),
            pl.BlockSpec(memory_space=pl.ANY),
        ],
        out_specs=[
            pl.BlockSpec((cand_count, width), lambda group: (0, 0)),
            pl.BlockSpec((cand_count, key_width), lambda group: (0, 0)),
        ],
        out_shape=[
            jax.ShapeDtypeStruct((cand_count, width), jnp.bfloat16),
            jax.ShapeDtypeStruct((cand_count, key_width), jnp.bfloat16),
        ],
        scratch_shapes=[
            pltpu.VMEM(qkv_weight.shape, jnp.bfloat16),
            pltpu.VMEM(out_weight.shape, jnp.bfloat16),
            pltpu.VMEM(proj_weight.shape, jnp.bfloat16),
            pltpu.SemaphoreType.DMA((5,)),
            pltpu.VMEM((rows, width), jnp.bfloat16),
            pltpu.VMEM((HEADS, 1, rows), jnp.float32),
            pltpu.VMEM((HEADS, cand_count, width), jnp.float32),
            pltpu.VMEM((cand_count, width), jnp.float32),
        ],
        compiler_params=pltpu.CompilerParams(vmem_limit_bytes=VMEM_LIMIT),
        cost_estimate=pl.CostEstimate(
            flops=5 * cand_count * tokens * width * width, bytes_accessed=1 << 24, transcendentals=0
        ),
        name="encode",
    )(frames.reshape(cand_count * tokens, width), qkv_weight, out_weight, proj_weight)


def usable_row(user, length_ref, mask_ref):
    positions = lax.broadcasted_iota(jnp.int32, mask_ref.shape, 1)
    kept = (positions < length_ref[user]) & ((mask_ref[...] == 1) | (positions == 0))
    return kept.astype(jnp.float32)


def attend_kernel(
    length_ref,
    slots_ref,
    near_ref,
    far_ref,
    history_ref,
    mask_ref,
    queries_ref,
    attended_ref,
    gates_ref,
):
    usable = usable_row(pl.program_id(0), length_ref, mask_ref)
    inv_count = lax.rsqrt(jnp.sum(usable, axis=1, keepdims=True))
    slots = slots_ref[...]
    half, key_width = near_ref.shape
    places = lax.broadcasted_iota(jnp.int32, (slots.shape[0], half), 1)
    queries = dot((slots == places).astype(jnp.bfloat16), near_ref[...])
    queries += dot((slots == places + half).astype(jnp.bfloat16), far_ref[...])
    queries = queries.astype(jnp.bfloat16)
    queries_ref[...] = queries
    events = history_ref.shape[0]
    chunk = math.gcd(events, 512)
    attended = jnp.zeros(attended_ref.shape, jnp.float32)
    for at in range(0, events, chunk):
        keys = history_ref[at : at + chunk, :]
        gates = jnp.tanh(dot_rows(queries, keys) * (0.5 / math.sqrt(key_width)))
        gates_ref[:, at : at + chunk] = gates
        weights = ((0.5 * gates + 0.5) * usable[:, at : at + chunk]).astype(jnp.bfloat16)
        attended += dot(weights, keys)
    attended_ref[...] = attended * inv_count


def attend(hist_len, slots, near, far, history, hist_mask):
    users, events, key_width = history.shape
    requests = slots.shape[0]
    per_user = requests // users
    return pl.pallas_call(
        attend_kernel,
        grid=(users,),
        in_specs=[
            pl.BlockSpec(memory_space=pltpu.SMEM),
            pl.BlockSpec((per_user, 1), lambda user: (user, 0)),
            pl.BlockSpec(near.shape, lambda user: (0, 0)),
            pl.BlockSpec(far.shape, lambda user: (0, 0)),
            pl.BlockSpec((None, events, key_width), lambda user: (user, 0, 0)),
            pl.BlockSpec((None, 1, events), lambda user: (user, 0, 0)),
        ],
        out_specs=[
            pl.BlockSpec((per_user, key_width), lambda user: (user, 0)),
            pl.BlockSpec((per_user, key_width), lambda user: (user, 0)),
            pl.BlockSpec((per_user, events), lambda user: (user, 0)),
        ],
        out_shape=[
            jax.ShapeDtypeStruct((requests, key_width), jnp.bfloat16),
            jax.ShapeDtypeStruct((requests, key_width), jnp.float32),
            jax.ShapeDtypeStruct((requests, events), jnp.float32),
        ],
        compiler_params=pltpu.CompilerParams(vmem_limit_bytes=VMEM_LIMIT),
        cost_estimate=pl.CostEstimate(
            flops=4 * requests * events * key_width, bytes_accessed=1 << 24, transcendentals=0
        ),
        name="attend",
    )(hist_len, slots, near, far, history, hist_mask)


def score_kernel(
    length_ref,
    queries_ref,
    attended_ref,
    mask_ref,
    labels_ref,
    mlp_ref,
    logit_weight_ref,
    logits_ref,
    grad_att_ref,
    direct_ref,
):
    usable = usable_row(pl.program_id(0), length_ref, mask_ref)
    inv_count = lax.rsqrt(jnp.sum(usable, axis=1, keepdims=True))
    query_b = queries_ref[...]
    query_f = query_b.astype(jnp.float32)
    attended = attended_ref[...]
    key_width = query_f.shape[1]
    joined = jnp.concatenate(
        [query_b, attended.astype(jnp.bfloat16), (query_f * attended).astype(jnp.bfloat16)], axis=1
    )
    pre_act = dot(joined, mlp_ref[...])
    act_sig = 0.5 * jnp.tanh(0.5 * pre_act) + 0.5
    hidden_units = (pre_act * act_sig).astype(jnp.bfloat16)
    weight = logit_weight_ref[...].astype(jnp.float32)
    logits = jnp.sum(hidden_units.astype(jnp.float32) * weight, axis=1, keepdims=True)
    logits_ref[...] = logits
    dlogit = (0.5 * jnp.tanh(0.5 * logits) + 0.5) - labels_ref[...].astype(jnp.float32)
    grad_pre = (dlogit * weight * (act_sig * (1.0 + pre_act * (1.0 - act_sig)))).astype(jnp.bfloat16)
    djoined = dot_rows(grad_pre, mlp_ref[...])
    part_query = djoined[:, :key_width]
    part_att = djoined[:, key_width : 2 * key_width]
    part_prod = djoined[:, 2 * key_width :]
    grad_att_ref[...] = ((part_att + part_prod * query_f) * inv_count).astype(jnp.bfloat16)
    direct_ref[...] = part_query + part_prod * attended


def score(hist_len, queries, attended, hist_mask, labels, mlp_weight, logit_weight):
    users, _, events = hist_mask.shape
    requests, key_width = queries.shape
    per_user = requests // users
    block = pl.BlockSpec((per_user, key_width), lambda user: (user, 0))
    column = pl.BlockSpec((per_user, 1), lambda user: (user, 0))
    return pl.pallas_call(
        score_kernel,
        grid=(users,),
        in_specs=[
            pl.BlockSpec(memory_space=pltpu.SMEM),
            block,
            block,
            pl.BlockSpec((None, 1, events), lambda user: (user, 0, 0)),
            column,
            pl.BlockSpec(mlp_weight.shape, lambda user: (0, 0)),
            pl.BlockSpec(logit_weight.shape, lambda user: (0, 0)),
        ],
        out_specs=[column, block, block],
        out_shape=[
            jax.ShapeDtypeStruct((requests, 1), jnp.float32),
            jax.ShapeDtypeStruct((requests, key_width), jnp.bfloat16),
            jax.ShapeDtypeStruct((requests, key_width), jnp.float32),
        ],
        compiler_params=pltpu.CompilerParams(vmem_limit_bytes=VMEM_LIMIT),
        cost_estimate=pl.CostEstimate(
            flops=4 * requests * mlp_weight.shape[0] * mlp_weight.shape[1],
            bytes_accessed=1 << 23,
            transcendentals=0,
        ),
        name="score",
    )(hist_len, queries, attended, hist_mask, labels, mlp_weight, logit_weight)


def attend_back_kernel(
    length_ref, grad_att_ref, direct_ref, gates_ref, history_ref, mask_ref, grad_rows_ref
):
    usable = usable_row(pl.program_id(0), length_ref, mask_ref)
    grad_att = grad_att_ref[...]
    events, key_width = history_ref.shape
    chunk = math.gcd(events, 512)
    back = jnp.zeros(direct_ref.shape, jnp.float32)
    for at in range(0, events, chunk):
        keys = history_ref[at : at + chunk, :]
        gates = gates_ref[:, at : at + chunk]
        slope = (0.25 - 0.25 * gates * gates) * usable[:, at : at + chunk]
        grad_sig = (dot_rows(grad_att, keys) * slope).astype(jnp.bfloat16)
        back += dot(grad_sig, keys)
    grad_rows_ref[...] = (direct_ref[...] + back * (1.0 / math.sqrt(key_width))).astype(jnp.bfloat16)


def attend_back(hist_len, grad_att, direct, gates, history, hist_mask):
    users, events, key_width = history.shape
    requests = grad_att.shape[0]
    per_user = requests // users
    block = pl.BlockSpec((per_user, key_width), lambda user: (user, 0))
    return pl.pallas_call(
        attend_back_kernel,
        grid=(users,),
        in_specs=[
            pl.BlockSpec(memory_space=pltpu.SMEM),
            block,
            block,
            pl.BlockSpec((per_user, events), lambda user: (user, 0)),
            pl.BlockSpec((None, events, key_width), lambda user: (user, 0, 0)),
            pl.BlockSpec((None, 1, events), lambda user: (user, 0, 0)),
        ],
        out_specs=block,
        out_shape=jax.ShapeDtypeStruct((requests, key_width), jnp.bfloat16),
        compiler_params=pltpu.CompilerParams(vmem_limit_bytes=VMEM_LIMIT),
        cost_estimate=pl.CostEstimate(
            flops=4 * requests * events * key_width, bytes_accessed=1 << 24, transcendentals=0
        ),
        name="attend_back",
    )(hist_len, grad_att, direct, gates, history, hist_mask)


def terms_kernel(
    origins, me_ref, slots_ref, grad_rows_ref, near_ref, far_ref, keep_ref, send_ref, terms_ref
):
    half = near_ref.shape[0]
    requests = slots_ref.shape[1]
    grad_rows = grad_rows_ref[...]
    chunk = math.gcd(half, 512)
    steps = 0
    for offset, pooled_ref in ((0, near_ref), (half, far_ref)):
        for at in range(0, half, chunk):
            places = lax.broadcasted_iota(jnp.int32, (chunk, requests), 0) + (offset + at)
            row_hot = (places == slots_ref[...]).astype(jnp.bfloat16)
            cand_grad = dot(row_hot, grad_rows).astype(jnp.bfloat16)
            term = dot_columns(pooled_ref[at : at + chunk, :], cand_grad)
            if steps == 0:
                terms_ref[...] = term
            else:
                terms_ref[...] += term
            steps += 1
    rows = terms_ref.shape[0] // len(origins)
    me = me_ref[0]
    batch = max(1, 32 // rows)
    for slot in range(0, len(origins), batch):
        found = [
            terms_ref[pl.ds(pl.multiple_of((me ^ origins[slot + i]) * rows, rows), rows), :]
            for i in range(batch)
        ]
        found = found[0] if batch == 1 else jnp.concatenate(found, axis=0)
        out_ref, at = (keep_ref, slot) if slot < len(origins) // 2 else (send_ref, slot - len(origins) // 2)
        out_ref[at * rows : (at + batch) * rows, :] = found.astype(jnp.bfloat16)


def own_terms(origins, me, slots, grad_rows, near, far):
    width, key_width = near.shape[1], grad_rows.shape[1]
    whole = pl.BlockSpec(memory_space=pltpu.VMEM)
    return pl.pallas_call(
        functools.partial(terms_kernel, origins),
        in_specs=[pl.BlockSpec(memory_space=pltpu.SMEM), whole, whole, whole, whole],
        out_specs=[whole, whole],
        out_shape=[jax.ShapeDtypeStruct((width // 2, key_width), jnp.bfloat16)] * 2,
        scratch_shapes=[pltpu.VMEM((width, key_width), jnp.float32)],
        compiler_params=pltpu.CompilerParams(vmem_limit_bytes=VMEM_LIMIT),
        cost_estimate=pl.CostEstimate(
            flops=4 * near.shape[0] * key_width * (width + grad_rows.shape[0]),
            bytes_accessed=1 << 23,
            transcendentals=0,
        ),
        name="own_terms",
    )(me, slots, grad_rows, near, far)


def bit_groups(size):
    groups = []
    bit = 0
    while (1 << bit) < size:
        values = min(4, size >> bit)
        groups.append((bit, values))
        bit += values.bit_length() - 1
    return groups


def exchange(values, axis_name, size, distance):
    return lax.ppermute(values, axis_name, [(i, i ^ distance) for i in range(size)])


def gather_blocks(block, wides):
    rows = block
    for bit, values in reversed(bit_groups(wides)):
        found = [exchange(rows, "wide", wides, step << bit) for step in range(1, values)]
        rows = jnp.concatenate([rows] + found, axis=0)
    return rows, exchange(rows, "section", 2, 1)


def slot_of(distance, wides):
    slot = 0
    for bit, values in bit_groups(wides):
        slot = slot * values + ((distance >> bit) & (values - 1))
    return slot + (distance // wides) * wides


def sum_blocks(keep, send, wides):
    total = keep.astype(jnp.float32) + exchange(send, "section", 2, 1).astype(jnp.float32)
    for bit, values in bit_groups(wides):
        parts = total.astype(jnp.bfloat16).reshape((values, -1) + keep.shape[1:])
        found = [
            exchange(parts[step], "wide", wides, step << bit).astype(jnp.float32)
            for step in range(1, values)
        ]
        total = sum(found, parts[0].astype(jnp.float32))
    return total


def body(
    frames,
    qkv_weight,
    out_weight,
    proj_weight,
    mlp_weight,
    logit_weight,
    history,
    hist_len,
    hist_mask,
    req_owner,
    req_local,
    labels,
):
    wides = lax.axis_size("wide")
    devices = lax.axis_size("section") * wides
    me = lax.axis_index("section") * wides + lax.axis_index("wide")
    cand_count = frames.shape[0]
    requests = req_local.shape[0]
    users, events, _ = history.shape
    pooled, embedded = encode_block(frames, qkv_weight, out_weight, proj_weight)
    near_embedded, far_embedded = gather_blocks(embedded, wides)
    near_pooled, far_pooled = gather_blocks(pooled, wides)
    slots = slot_of(req_owner[:, 0] ^ me, wides) * cand_count + req_local
    masks = hist_mask.reshape(users, 1, events)
    queries, attended, gates = attend(
        hist_len, slots.reshape(requests, 1), near_embedded, far_embedded, history, masks
    )
    logits, grad_att, direct = score(
        hist_len,
        queries,
        attended,
        masks,
        labels.reshape(requests, 1),
        mlp_weight,
        logit_weight.reshape(1, -1),
    )
    grad_rows = attend_back(hist_len, grad_att, direct, gates, history, masks)
    origins = [0] * devices
    for distance in range(devices):
        origins[slot_of(distance, wides)] = distance
    keep, send = own_terms(
        origins, me.reshape(1), slots.reshape(1, requests), grad_rows, near_pooled, far_pooled
    )
    grad_proj = sum_blocks(keep, send, wides)
    return (logits.reshape(requests), grad_proj)


def solution(mesh):
    in_specs = (
        P(("section", "wide"), None, None),
        P(),
        P(),
        P(),
        P(),
        P(),
        P(("section", "wide"), None, None),
        P(("section", "wide")),
        P(("section", "wide"), None),
        P(("section", "wide"), None),
        P(("section", "wide")),
        P(("section", "wide")),
    )
    out_specs = (P(("section", "wide")), P(("section", "wide"), None))
    return jax.shard_map(body, mesh=mesh, in_specs=in_specs, out_specs=out_specs, check_vma=False)
```

```python
import functools
import math

import jax
import jax.numpy as jnp
from jax import lax
from jax.experimental import pallas as pl
from jax.experimental.pallas import tpu as pltpu
from jax.sharding import PartitionSpec as P

HEADS = 16
FRAMES = 3


EPSILON = 1e-06
MIB = 1024 * 1024


def layer_norm(values):
    center = values - jnp.mean(values, axis=-1, keepdims=True)
    spread = jnp.mean(jnp.square(center), axis=-1, keepdims=True)
    return center * lax.rsqrt(spread + EPSILON)


def dot(left, right):
    return jnp.dot(left, right, preferred_element_type=jnp.float32)


def dot_rows(left, right):
    return lax.dot_general(left, right, (((1,), (1,)), ((), ())), preferred_element_type=jnp.float32)


def dot_columns(left, right):
    return lax.dot_general(left, right, (((0,), (0,)), ((), ())), preferred_element_type=jnp.float32)


def split_rows(values):
    high = values.astype(jnp.bfloat16)
    low = (values - high.astype(jnp.float32)).astype(jnp.bfloat16)
    return jnp.concatenate([high, low], axis=0)


def dot_split(values, right):
    both = dot(split_rows(values), right)
    rows = values.shape[0]
    return both[:rows] + both[rows:]


def encode_kernel(
    tokens,
    frames_ref,
    qkv_hbm,
    out_hbm,
    proj_hbm,
    pooled_ref,
    embedded_ref,
    qkv_ref,
    out_ref,
    proj_ref,
    sems,
    normed_ref,
    scores_ref,
    mixed_rows_ref,
    sums_ref,
):
    group = pl.program_id(0)
    rows, width = normed_ref.shape
    head_dim = width // HEADS
    patches = tokens // FRAMES
    cands = rows // tokens
    lanes = 2 * head_dim
    parts = 3
    copies = [
        pltpu.make_async_copy(
            qkv_hbm.at[:, pl.ds(part * width, width)],
            qkv_ref.at[:, pl.ds(part * width, width)],
            sems.at[part],
        )
        for part in range(parts)
    ]
    copies.append(pltpu.make_async_copy(out_hbm, out_ref, sems.at[parts]))
    copies.append(pltpu.make_async_copy(proj_hbm, proj_ref, sems.at[parts + 1]))

    @pl.when(group == 0)
    def _():
        for copy in copies:
            copy.start()

    inputs = frames_ref[...].astype(jnp.float32)
    sums_ref[pl.ds(pl.multiple_of(group * cands, cands), cands), :] = jnp.sum(
        inputs.reshape(cands, tokens, width), axis=1
    )
    normed_ref[...] = layer_norm(inputs).astype(jnp.bfloat16)

    @pl.when(group == 0)
    def _():
        copies[0].wait()
        copies[1].wait()

    exponent = math.log2(math.e) / math.sqrt(head_dim)
    blocks = rows // lanes
    pairs = HEADS // 2
    first_head = lax.broadcasted_iota(jnp.int32, (lanes, lanes), 1) < head_dim
    frame_at = (lax.broadcasted_iota(jnp.int32, (patches, 2 * lanes), 1) % lanes) // patches
    for pair in range(pairs):
        start = pair * lanes
        weight = jnp.concatenate(
            [qkv_ref[:, start : start + lanes], qkv_ref[:, width + start : width + start + lanes]],
            axis=1,
        )
        packed = dot(normed_ref[...], weight).astype(jnp.bfloat16)
        for block in range(blocks):
            query = packed[block * lanes : (block + 1) * lanes, :lanes]
            key = packed[block * lanes : (block + 1) * lanes, lanes:]
            zero = jnp.zeros_like(key)
            keys = jnp.concatenate(
                [jnp.where(first_head, key, zero), jnp.where(first_head, zero, key)], axis=0
            )
            scores = dot_rows(query, keys)
            own_scores = scores[:patches]
            for frame in range(1, lanes // patches):
                own_scores = jnp.where(
                    frame_at == frame, scores[frame * patches : (frame + 1) * patches], own_scores
                )
            scores_ref[block, pair] = own_scores

    ones_row = lax.broadcasted_iota(jnp.int32, (2 * lanes, 2 * lanes), 0) // patches
    ones_column = lax.broadcasted_iota(jnp.int32, (2 * lanes, 2 * lanes), 1) // patches
    frame_ones = (ones_row == ones_column).astype(jnp.bfloat16)
    exp_scores = jnp.exp2(
        scores_ref[...].reshape(blocks * pairs * patches, 2 * lanes) * exponent
    )
    totals = dot(exp_scores.astype(jnp.bfloat16), frame_ones)
    probs = (exp_scores / totals).reshape(blocks * pairs, patches, 2 * lanes)
    sums = jnp.sum(probs, axis=1)
    key_sums = [
        jnp.concatenate(
            [
                sums[block * pairs : (block + 1) * pairs, side * lanes : (side + 1) * lanes]
                for block in range(blocks)
            ],
            axis=1,
        )
        for side in range(2)
    ]
    own = lax.broadcasted_iota(jnp.int32, (cands, rows), 1) // tokens == lax.broadcasted_iota(
        jnp.int32, (cands, rows), 0
    )
    spread = jnp.concatenate(
        [jnp.where(own, key_sums[head % 2][head // 2 : head // 2 + 1], 0.0) for head in range(HEADS)], axis=0
    ).astype(jnp.bfloat16)
    mixed_rows = dot(spread, normed_ref[...])
    for head in range(HEADS):
        mixed_rows_ref[head, pl.ds(pl.multiple_of(group * cands, cands), cands), :] = mixed_rows[
            head * cands : (head + 1) * cands
        ]

    @pl.when(group == pl.num_programs(0) - 1)
    def _():
        for copy in copies[2:]:
            copy.wait()
        total = pooled_ref.shape[0]
        quad = 4
        span = quad * head_dim
        pieces = []
        for part in range(HEADS // quad):
            left = mixed_rows_ref[pl.ds(part * quad, quad)].reshape(quad * total, width)
            both = dot_split(left, qkv_ref[:, pl.ds(2 * width + part * span, span)])
            head_at = lax.broadcasted_iota(jnp.int32, (total, span), 1) // head_dim
            piece = jnp.zeros((total, span), jnp.float32)
            for head in range(quad):
                piece = jnp.where(head_at == head, both[head * total : (head + 1) * total], piece)
            pieces.append(piece)
        mixed_mean = jnp.concatenate(pieces, axis=1) * (1.0 / tokens)
        hidden = sums_ref[...] * (1.0 / tokens) + dot_split(mixed_mean, out_ref[...])
        pooled = layer_norm(hidden).astype(jnp.bfloat16)
        pooled_ref[...] = pooled
        embedded_ref[...] = dot(pooled, proj_ref[...]).astype(jnp.bfloat16)


def encode_block(frames, qkv_weight, out_weight, proj_weight):
    cand_count, tokens, width = frames.shape
    key_width = proj_weight.shape[1]
    cands = 8
    rows = cands * tokens
    lanes = 2 * width // HEADS
    patches = tokens // FRAMES
    return pl.pallas_call(
        functools.partial(encode_kernel, tokens),
        grid=(cand_count // cands,),
        in_specs=[
            pl.BlockSpec((rows, width), lambda group: (group, 0)),
            pl.BlockSpec(memory_space=pl.ANY),
            pl.BlockSpec(memory_space=pl.ANY),
            pl.BlockSpec(memory_space=pl.ANY),
        ],
        out_specs=[
            pl.BlockSpec((cand_count, width), lambda group: (0, 0)),
            pl.BlockSpec((cand_count, key_width), lambda group: (0, 0)),
        ],
        out_shape=[
            jax.ShapeDtypeStruct((cand_count, width), jnp.bfloat16),
            jax.ShapeDtypeStruct((cand_count, key_width), jnp.bfloat16),
        ],
        scratch_shapes=[
            pltpu.VMEM(qkv_weight.shape, jnp.bfloat16),
            pltpu.VMEM(out_weight.shape, jnp.bfloat16),
            pltpu.VMEM(proj_weight.shape, jnp.bfloat16),
            pltpu.SemaphoreType.DMA((5,)),
            pltpu.VMEM((rows, width), jnp.bfloat16),
            pltpu.VMEM((rows * FRAMES // tokens * patches // lanes, HEADS // 2, patches, 2 * lanes), jnp.float32),
            pltpu.VMEM((HEADS, cand_count, width), jnp.float32),
            pltpu.VMEM((cand_count, width), jnp.float32),
        ],
        compiler_params=pltpu.CompilerParams(vmem_limit_bytes=60 * MIB),
        cost_estimate=pl.CostEstimate(
            flops=5 * cand_count * tokens * width * width, bytes_accessed=1 << 24, transcendentals=0
        ),
        name="encode",
    )(frames.reshape(cand_count * tokens, width), qkv_weight, out_weight, proj_weight)


def attend_kernel(
    inv_ref,
    slots_ref,
    near_ref,
    far_ref,
    history_ref,
    usable_ref,
    queries_ref,
    attended_ref,
    slope_ref,
):
    slots = slots_ref[...]
    half, key_width = near_ref.shape
    places = lax.broadcasted_iota(jnp.int32, (slots.shape[0], half), 1)
    queries = dot((slots == places).astype(jnp.bfloat16), near_ref[...])
    queries += dot((slots == places + half).astype(jnp.bfloat16), far_ref[...])
    queries = queries.astype(jnp.bfloat16)
    queries_ref[...] = queries
    events = history_ref.shape[0]
    chunk = math.gcd(events, 512)
    attended = jnp.zeros(attended_ref.shape, jnp.float32)
    for at in range(0, events, chunk):
        keys = history_ref[at : at + chunk, :]
        half_gate = 0.5 * jnp.tanh(dot_rows(queries, keys) * (0.5 / math.sqrt(key_width)))
        weights = (0.5 + half_gate) * usable_ref[:, at : at + chunk]
        slope_ref[:, at : at + chunk] = (weights * (0.5 - half_gate)).astype(jnp.bfloat16)
        attended += dot(weights.astype(jnp.bfloat16), keys)
    attended_ref[...] = attended * inv_ref[pl.program_id(0)]


def attend(inv_count, slots, near, far, history, usable):
    users, events, key_width = history.shape
    requests = slots.shape[0]
    per_user = requests // users
    return pl.pallas_call(
        attend_kernel,
        grid=(users,),
        in_specs=[
            pl.BlockSpec(memory_space=pltpu.SMEM),
            pl.BlockSpec((per_user, 1), lambda user: (user, 0)),
            pl.BlockSpec(near.shape, lambda user: (0, 0)),
            pl.BlockSpec(far.shape, lambda user: (0, 0)),
            pl.BlockSpec((None, events, key_width), lambda user: (user, 0, 0)),
            pl.BlockSpec((None, 1, events), lambda user: (user, 0, 0)),
        ],
        out_specs=[
            pl.BlockSpec((per_user, key_width), lambda user: (user, 0)),
            pl.BlockSpec((per_user, key_width), lambda user: (user, 0)),
            pl.BlockSpec((per_user, events), lambda user: (user, 0)),
        ],
        out_shape=[
            jax.ShapeDtypeStruct((requests, key_width), jnp.bfloat16),
            jax.ShapeDtypeStruct((requests, key_width), jnp.float32),
            jax.ShapeDtypeStruct((requests, events), jnp.bfloat16),
        ],
        compiler_params=pltpu.CompilerParams(vmem_limit_bytes=24 * MIB),
        cost_estimate=pl.CostEstimate(
            flops=4 * requests * events * key_width, bytes_accessed=1 << 24, transcendentals=0
        ),
        name="attend",
    )(inv_count, slots, near, far, history, usable)


def score_kernel(
    inv_ref,
    queries_ref,
    attended_ref,
    labels_ref,
    mlp_ref,
    logit_weight_ref,
    logits_ref,
    grad_att_ref,
    direct_ref,
):
    step_users = inv_ref.shape[0] // pl.num_programs(0)
    per_user = queries_ref.shape[0] // step_users
    query_b = queries_ref[...]
    query_f = query_b.astype(jnp.float32)
    attended = attended_ref[...]
    key_width = query_f.shape[1]
    joined = jnp.concatenate(
        [query_b, attended.astype(jnp.bfloat16), (query_f * attended).astype(jnp.bfloat16)], axis=1
    )
    pre_act = dot(joined, mlp_ref[...])
    act_sig = 0.5 * jnp.tanh(0.5 * pre_act) + 0.5
    hidden_units = (pre_act * act_sig).astype(jnp.bfloat16)
    weight = logit_weight_ref[...].astype(jnp.float32)
    logits = jnp.sum(hidden_units.astype(jnp.float32) * weight, axis=1, keepdims=True)
    logits_ref[...] = logits
    dlogit = (0.5 * jnp.tanh(0.5 * logits) + 0.5) - labels_ref[...].astype(jnp.float32)
    grad_pre = (dlogit * weight * (act_sig * (1.0 + pre_act * (1.0 - act_sig)))).astype(jnp.bfloat16)
    djoined = dot_rows(grad_pre, mlp_ref[...])
    part_query = djoined[:, :key_width]
    part_att = djoined[:, key_width : 2 * key_width]
    part_prod = djoined[:, 2 * key_width :]
    grad_att = part_att + part_prod * query_f
    for user in range(step_users):
        rows = slice(user * per_user, (user + 1) * per_user)
        inv_count = inv_ref[pl.program_id(0) * step_users + user]
        grad_att_ref[rows, :] = (grad_att[rows] * inv_count).astype(jnp.bfloat16)
    direct_ref[...] = part_query + part_prod * attended


def score(inv_count, queries, attended, labels, mlp_weight, logit_weight):
    users = inv_count.shape[0]
    requests, key_width = queries.shape
    steps = math.gcd(users, 2)
    step_rows = requests // steps
    block = pl.BlockSpec((step_rows, key_width), lambda step: (step, 0))
    column = pl.BlockSpec((step_rows, 1), lambda step: (step, 0))
    return pl.pallas_call(
        score_kernel,
        grid=(steps,),
        in_specs=[
            pl.BlockSpec(memory_space=pltpu.SMEM),
            block,
            block,
            column,
            pl.BlockSpec(mlp_weight.shape, lambda step: (0, 0)),
            pl.BlockSpec(logit_weight.shape, lambda step: (0, 0)),
        ],
        out_specs=[column, block, block],
        out_shape=[
            jax.ShapeDtypeStruct((requests, 1), jnp.float32),
            jax.ShapeDtypeStruct((requests, key_width), jnp.bfloat16),
            jax.ShapeDtypeStruct((requests, key_width), jnp.float32),
        ],
        compiler_params=pltpu.CompilerParams(vmem_limit_bytes=32 * MIB),
        cost_estimate=pl.CostEstimate(
            flops=4 * requests * mlp_weight.shape[0] * mlp_weight.shape[1],
            bytes_accessed=1 << 23,
            transcendentals=0,
        ),
        name="score",
    )(inv_count, queries, attended, labels, mlp_weight, logit_weight)


def attend_back_kernel(
    grad_att_ref, direct_ref, slope_ref, history_ref, grad_rows_ref
):
    grad_att = grad_att_ref[...]
    events, key_width = history_ref.shape
    chunk = math.gcd(events, 512)
    back = jnp.zeros(direct_ref.shape, jnp.float32)
    for at in range(0, events, chunk):
        keys = history_ref[at : at + chunk, :]
        slope = slope_ref[:, at : at + chunk].astype(jnp.float32)
        grad_sig = (dot_rows(grad_att, keys) * slope).astype(jnp.bfloat16)
        back += dot(grad_sig, keys)
    grad_rows_ref[...] = (direct_ref[...] + back * (1.0 / math.sqrt(key_width))).astype(jnp.bfloat16)


def attend_back(grad_att, direct, slope, history):
    users, events, key_width = history.shape
    requests = grad_att.shape[0]
    per_user = requests // users
    block = pl.BlockSpec((per_user, key_width), lambda user: (user, 0))
    return pl.pallas_call(
        attend_back_kernel,
        grid=(users,),
        in_specs=[
            block,
            block,
            pl.BlockSpec((per_user, events), lambda user: (user, 0)),
            pl.BlockSpec((None, events, key_width), lambda user: (user, 0, 0)),
        ],
        out_specs=block,
        out_shape=jax.ShapeDtypeStruct((requests, key_width), jnp.bfloat16),
        compiler_params=pltpu.CompilerParams(vmem_limit_bytes=20 * MIB),
        cost_estimate=pl.CostEstimate(
            flops=4 * requests * events * key_width, bytes_accessed=1 << 24, transcendentals=0
        ),
        name="attend_back",
    )(grad_att, direct, slope, history)


def terms_kernel(
    origins, me_ref, slots_ref, grad_rows_ref, near_ref, far_ref, keep_ref, send_ref, terms_ref
):
    half = near_ref.shape[0]
    requests = slots_ref.shape[1]
    grad_rows = grad_rows_ref[...]
    chunk = math.gcd(half, 512)
    steps = 0
    for offset, pooled_ref in ((0, near_ref), (half, far_ref)):
        for at in range(0, half, chunk):
            places = lax.broadcasted_iota(jnp.int32, (chunk, requests), 0) + (offset + at)
            row_hot = (places == slots_ref[...]).astype(jnp.bfloat16)
            cand_grad = dot(row_hot, grad_rows).astype(jnp.bfloat16)
            term = dot_columns(pooled_ref[at : at + chunk, :], cand_grad)
            if steps == 0:
                terms_ref[...] = term
            else:
                terms_ref[...] += term
            steps += 1
    rows = terms_ref.shape[0] // len(origins)
    me = me_ref[0]
    batch = max(1, 32 // rows)
    for slot in range(0, len(origins), batch):
        found = [
            terms_ref[pl.ds(pl.multiple_of((me ^ origins[slot + i]) * rows, rows), rows), :]
            for i in range(batch)
        ]
        found = found[0] if batch == 1 else jnp.concatenate(found, axis=0)
        out_ref, at = (keep_ref, slot) if slot < len(origins) // 2 else (send_ref, slot - len(origins) // 2)
        out_ref[at * rows : (at + batch) * rows, :] = found.astype(jnp.bfloat16)


def own_terms(origins, me, slots, grad_rows, near, far):
    width, key_width = near.shape[1], grad_rows.shape[1]
    whole = pl.BlockSpec(memory_space=pltpu.VMEM)
    return pl.pallas_call(
        functools.partial(terms_kernel, origins),
        in_specs=[pl.BlockSpec(memory_space=pltpu.SMEM), whole, whole, whole, whole],
        out_specs=[whole, whole],
        out_shape=[jax.ShapeDtypeStruct((width // 2, key_width), jnp.bfloat16)] * 2,
        scratch_shapes=[pltpu.VMEM((width, key_width), jnp.float32)],
        compiler_params=pltpu.CompilerParams(vmem_limit_bytes=20 * MIB),
        cost_estimate=pl.CostEstimate(
            flops=4 * near.shape[0] * key_width * (width + grad_rows.shape[0]),
            bytes_accessed=1 << 23,
            transcendentals=0,
        ),
        name="own_terms",
    )(me, slots, grad_rows, near, far)


def bit_groups(size):
    groups = []
    bit = 0
    while (1 << bit) < size:
        values = min(4, size >> bit)
        groups.append((bit, values))
        bit += values.bit_length() - 1
    return groups


def exchange(values, axis_name, size, distance):
    return lax.ppermute(values, axis_name, [(i, i ^ distance) for i in range(size)])


def gather_stage(rows, wides, bit, values):
    found = [exchange(rows, "wide", wides, step << bit) for step in range(1, values)]
    return jnp.concatenate([rows] + found, axis=0)


def after(values, *others):
    return lax.optimization_barrier((values,) + others)[0]


def slot_of(distance, wides):
    slot = 0
    for bit, values in bit_groups(wides):
        slot = slot * values + ((distance >> bit) & (values - 1))
    return slot + (distance // wides) * wides


def sum_blocks(keep, send, wides):
    total = keep.astype(jnp.float32) + exchange(send, "section", 2, 1).astype(jnp.float32)
    for bit, values in bit_groups(wides):
        parts = total.astype(jnp.bfloat16).reshape((values, -1) + keep.shape[1:])
        found = [
            exchange(parts[step], "wide", wides, step << bit).astype(jnp.float32)
            for step in range(1, values)
        ]
        total = sum(found, parts[0].astype(jnp.float32))
    return total


def body(
    frames,
    qkv_weight,
    out_weight,
    proj_weight,
    mlp_weight,
    logit_weight,
    history,
    hist_len,
    hist_mask,
    req_owner,
    req_local,
    labels,
):
    wides = lax.axis_size("wide")
    devices = lax.axis_size("section") * wides
    me = lax.axis_index("section") * wides + lax.axis_index("wide")
    cand_count = frames.shape[0]
    requests = req_local.shape[0]
    users, events, _ = history.shape
    pooled, embedded = encode_block(frames, qkv_weight, out_weight, proj_weight)
    positions = jnp.arange(events, dtype=jnp.int32)[None, :]
    usable = (
        (positions < hist_len[:, None]) & ((hist_mask == 1) | (positions == 0))
    ).astype(jnp.float32)
    inv_count = lax.rsqrt(jnp.sum(usable, axis=1))
    usable = usable.reshape(users, 1, events)
    slots = slot_of(req_owner[:, 0] ^ me, wides) * cand_count + req_local
    stages = list(reversed(bit_groups(wides)))
    near_embedded = embedded
    for bit, values in stages:
        near_embedded = gather_stage(near_embedded, wides, bit, values)
    far_embedded = exchange(near_embedded, "section", 2, 1)
    near_pooled = gather_stage(after(pooled, near_embedded), wides, *stages[0])
    queries, attended, slope = attend(
        inv_count, slots.reshape(requests, 1), near_embedded, far_embedded, history, usable
    )
    near_pooled = after(near_pooled, attended)
    for bit, values in stages[1:]:
        near_pooled = gather_stage(near_pooled, wides, bit, values)
    logits, grad_att, direct = score(
        inv_count,
        queries,
        attended,
        labels.reshape(requests, 1),
        mlp_weight,
        logit_weight.reshape(1, -1),
    )
    far_pooled = exchange(after(near_pooled, grad_att), "section", 2, 1)
    grad_rows = attend_back(grad_att, direct, slope, history)
    origins = [0] * devices
    for distance in range(devices):
        origins[slot_of(distance, wides)] = distance
    keep, send = own_terms(
        origins, me.reshape(1), slots.reshape(1, requests), grad_rows, near_pooled, far_pooled
    )
    grad_proj = sum_blocks(keep, send, wides)
    return (logits.reshape(requests), grad_proj)


def solution(mesh):
    in_specs = (
        P(("section", "wide"), None, None),
        P(),
        P(),
        P(),
        P(),
        P(),
        P(("section", "wide"), None, None),
        P(("section", "wide")),
        P(("section", "wide"), None),
        P(("section", "wide"), None),
        P(("section", "wide")),
        P(("section", "wide")),
    )
    out_specs = (P(("section", "wide")), P(("section", "wide"), None))
    return jax.shard_map(body, mesh=mesh, in_specs=in_specs, out_specs=out_specs, check_vma=False)
```

```python
import functools
import math

import jax
import jax.numpy as jnp
from jax import lax
from jax.experimental import pallas as pl
from jax.experimental.pallas import tpu as pltpu
from jax.sharding import PartitionSpec as P

HEADS = 16
FRAMES = 3


EPSILON = 1e-06
MIB = 1024 * 1024


def layer_norm(values):
    center = values - jnp.mean(values, axis=-1, keepdims=True)
    spread = jnp.mean(jnp.square(center), axis=-1, keepdims=True)
    return center * lax.rsqrt(spread + EPSILON)


def dot(left, right):
    return jnp.dot(left, right, preferred_element_type=jnp.float32)


def dot_rows(left, right):
    return lax.dot_general(left, right, (((1,), (1,)), ((), ())), preferred_element_type=jnp.float32)


def dot_columns(left, right):
    return lax.dot_general(left, right, (((0,), (0,)), ((), ())), preferred_element_type=jnp.float32)


def split_rows(values):
    high = values.astype(jnp.bfloat16)
    low = (values - high.astype(jnp.float32)).astype(jnp.bfloat16)
    return jnp.concatenate([high, low], axis=0)


def dot_split(values, right):
    both = dot(split_rows(values), right)
    rows = values.shape[0]
    return both[:rows] + both[rows:]


def encode_kernel(
    tokens,
    first_ref,
    next_ref,
    qkv_hbm,
    out_hbm,
    proj_hbm,
    pooled_ref,
    embedded_ref,
    qkv_ref,
    out_ref,
    proj_ref,
    sems,
    normed_ref,
    scores_ref,
    mixed_rows_ref,
    sums_ref,
):
    group = pl.program_id(0)
    rows, width = next_ref.shape
    head_dim = width // HEADS
    patches = tokens // FRAMES
    cands = rows // tokens
    lanes = 2 * head_dim
    parts = 3
    copies = [
        pltpu.make_async_copy(
            qkv_hbm.at[:, pl.ds(part * width, width)],
            qkv_ref.at[:, pl.ds(part * width, width)],
            sems.at[part],
        )
        for part in range(parts)
    ]
    copies.append(pltpu.make_async_copy(out_hbm, out_ref, sems.at[parts]))
    copies.append(pltpu.make_async_copy(proj_hbm, proj_ref, sems.at[parts + 1]))

    @pl.when(group == 0)
    def _():
        for copy in copies:
            copy.start()

    def norm_cand(source_ref, half, cand_group, cand):
        at = cand * tokens
        inputs = source_ref[at : at + tokens, :].astype(jnp.float32)
        start = pl.multiple_of(half * rows, rows) + at
        normed_ref[pl.ds(pl.multiple_of(start, tokens), tokens), :] = layer_norm(inputs).astype(
            jnp.bfloat16
        )
        sums_ref[cand_group * cands + cand] = jnp.sum(inputs, axis=0, keepdims=True)

    @pl.when(group == 0)
    def _():
        for cand in range(cands):
            norm_cand(first_ref, 0, 0, cand)
        copies[0].wait()
        copies[1].wait()

    place = pl.multiple_of((group % 2) * rows, rows)
    following = jnp.minimum(group + 1, pl.num_programs(0) - 1)
    exponent = math.log2(math.e) / math.sqrt(head_dim)
    blocks = rows // lanes
    pairs = HEADS // 2
    first_head = lax.broadcasted_iota(jnp.int32, (lanes, lanes), 1) < head_dim
    frame_at = (lax.broadcasted_iota(jnp.int32, (patches, 2 * lanes), 1) % lanes) // patches
    for pair in range(pairs):
        start = pair * lanes
        weight = jnp.concatenate(
            [qkv_ref[:, start : start + lanes], qkv_ref[:, width + start : width + start + lanes]],
            axis=1,
        )
        packed = dot(normed_ref[pl.ds(place, rows), :], weight).astype(jnp.bfloat16)
        for block in range(blocks):
            query = packed[block * lanes : (block + 1) * lanes, :lanes]
            key = packed[block * lanes : (block + 1) * lanes, lanes:]
            zero = jnp.zeros_like(key)
            keys = jnp.concatenate(
                [jnp.where(first_head, key, zero), jnp.where(first_head, zero, key)], axis=0
            )
            scores = dot_rows(query, keys)
            own_scores = scores[:patches]
            for frame in range(1, lanes // patches):
                own_scores = jnp.where(
                    frame_at == frame, scores[frame * patches : (frame + 1) * patches], own_scores
                )
            scores_ref[block, pair] = own_scores
        if pair < cands:
            norm_cand(next_ref, 1 - group % 2, following, pair)

    ones_row = lax.broadcasted_iota(jnp.int32, (2 * lanes, 2 * lanes), 0) // patches
    ones_column = lax.broadcasted_iota(jnp.int32, (2 * lanes, 2 * lanes), 1) // patches
    frame_ones = (ones_row == ones_column).astype(jnp.bfloat16)
    exp_scores = jnp.exp2(
        scores_ref[...].reshape(blocks * pairs * patches, 2 * lanes) * exponent
    )
    totals = dot(exp_scores.astype(jnp.bfloat16), frame_ones)
    probs = (exp_scores / totals).reshape(blocks * pairs, patches, 2 * lanes)
    sums = jnp.sum(probs, axis=1)
    key_sums = [
        jnp.concatenate(
            [
                sums[block * pairs : (block + 1) * pairs, side * lanes : (side + 1) * lanes]
                for block in range(blocks)
            ],
            axis=1,
        )
        for side in range(2)
    ]
    own = lax.broadcasted_iota(jnp.int32, (cands, rows), 1) // tokens == lax.broadcasted_iota(
        jnp.int32, (cands, rows), 0
    )
    spread = jnp.concatenate(
        [jnp.where(own, key_sums[head % 2][head // 2 : head // 2 + 1], 0.0) for head in range(HEADS)], axis=0
    ).astype(jnp.bfloat16)
    mixed_rows = dot(spread, normed_ref[pl.ds(place, rows), :])
    for head in range(HEADS):
        mixed_rows_ref[head, pl.ds(pl.multiple_of(group * cands, cands), cands), :] = mixed_rows[
            head * cands : (head + 1) * cands
        ]

    @pl.when(group == pl.num_programs(0) - 1)
    def _():
        for copy in copies[2:]:
            copy.wait()
        total = pooled_ref.shape[0]
        quad = 4
        span = quad * head_dim
        pieces = []
        for part in range(HEADS // quad):
            left = mixed_rows_ref[pl.ds(part * quad, quad)].reshape(quad * total, width)
            both = dot_split(left, qkv_ref[:, pl.ds(2 * width + part * span, span)])
            head_at = lax.broadcasted_iota(jnp.int32, (total, span), 1) // head_dim
            piece = jnp.zeros((total, span), jnp.float32)
            for head in range(quad):
                piece = jnp.where(head_at == head, both[head * total : (head + 1) * total], piece)
            pieces.append(piece)
        mixed_mean = jnp.concatenate(pieces, axis=1) * (1.0 / tokens)
        hidden = sums_ref[...].reshape(total, width) * (1.0 / tokens) + dot_split(mixed_mean, out_ref[...])
        pooled = layer_norm(hidden).astype(jnp.bfloat16)
        pooled_ref[...] = pooled
        embedded_ref[...] = dot(pooled, proj_ref[...]).astype(jnp.bfloat16)


def encode_block(frames, qkv_weight, out_weight, proj_weight):
    cand_count, tokens, width = frames.shape
    key_width = proj_weight.shape[1]
    cands = 8
    rows = cands * tokens
    last = cand_count // cands - 1
    rows_in = frames.reshape(cand_count * tokens, width)
    lanes = 2 * width // HEADS
    patches = tokens // FRAMES
    return pl.pallas_call(
        functools.partial(encode_kernel, tokens),
        grid=(cand_count // cands,),
        in_specs=[
            pl.BlockSpec((rows, width), lambda group: (0, 0)),
            pl.BlockSpec((rows, width), lambda group: (jnp.minimum(group + 1, last), 0)),
            pl.BlockSpec(memory_space=pl.ANY),
            pl.BlockSpec(memory_space=pl.ANY),
            pl.BlockSpec(memory_space=pl.ANY),
        ],
        out_specs=[
            pl.BlockSpec((cand_count, width), lambda group: (0, 0)),
            pl.BlockSpec((cand_count, key_width), lambda group: (0, 0)),
        ],
        out_shape=[
            jax.ShapeDtypeStruct((cand_count, width), jnp.bfloat16),
            jax.ShapeDtypeStruct((cand_count, key_width), jnp.bfloat16),
        ],
        scratch_shapes=[
            pltpu.VMEM(qkv_weight.shape, jnp.bfloat16),
            pltpu.VMEM(out_weight.shape, jnp.bfloat16),
            pltpu.VMEM(proj_weight.shape, jnp.bfloat16),
            pltpu.SemaphoreType.DMA((5,)),
            pltpu.VMEM((2 * rows, width), jnp.bfloat16),
            pltpu.VMEM((rows * FRAMES // tokens * patches // lanes, HEADS // 2, patches, 2 * lanes), jnp.float32),
            pltpu.VMEM((HEADS, cand_count, width), jnp.float32),
            pltpu.VMEM((cand_count, 1, width), jnp.float32),
        ],
        compiler_params=pltpu.CompilerParams(vmem_limit_bytes=60 * MIB),
        cost_estimate=pl.CostEstimate(
            flops=5 * cand_count * tokens * width * width, bytes_accessed=1 << 24, transcendentals=0
        ),
        name="encode",
    )(rows_in, rows_in, qkv_weight, out_weight, proj_weight)


def attend_kernel(
    inv_ref,
    slots_ref,
    near_ref,
    far_ref,
    history_ref,
    usable_ref,
    queries_ref,
    attended_ref,
    slope_ref,
):
    slots = slots_ref[...]
    half, key_width = near_ref.shape
    places = lax.broadcasted_iota(jnp.int32, (slots.shape[0], half), 1)
    queries = dot((slots == places).astype(jnp.bfloat16), near_ref[...])
    queries += dot((slots == places + half).astype(jnp.bfloat16), far_ref[...])
    queries = queries.astype(jnp.bfloat16)
    queries_ref[...] = queries
    events = history_ref.shape[0]
    chunk = math.gcd(events, 512)
    attended = jnp.zeros(attended_ref.shape, jnp.float32)
    for at in range(0, events, chunk):
        keys = history_ref[at : at + chunk, :]
        half_gate = 0.5 * jnp.tanh(dot_rows(queries, keys) * (0.5 / math.sqrt(key_width)))
        weights = (0.5 + half_gate) * usable_ref[:, at : at + chunk]
        slope_ref[:, at : at + chunk] = (weights * (0.5 - half_gate)).astype(jnp.bfloat16)
        attended += dot(weights.astype(jnp.bfloat16), keys)
    attended_ref[...] = attended * inv_ref[pl.program_id(0)]


def attend(inv_count, slots, near, far, history, usable):
    users, events, key_width = history.shape
    requests = slots.shape[0]
    per_user = requests // users
    return pl.pallas_call(
        attend_kernel,
        grid=(users,),
        in_specs=[
            pl.BlockSpec(memory_space=pltpu.SMEM),
            pl.BlockSpec((per_user, 1), lambda user: (user, 0)),
            pl.BlockSpec(near.shape, lambda user: (0, 0)),
            pl.BlockSpec(far.shape, lambda user: (0, 0)),
            pl.BlockSpec((None, events, key_width), lambda user: (user, 0, 0)),
            pl.BlockSpec((None, 1, events), lambda user: (user, 0, 0)),
        ],
        out_specs=[
            pl.BlockSpec((per_user, key_width), lambda user: (user, 0)),
            pl.BlockSpec((per_user, key_width), lambda user: (user, 0)),
            pl.BlockSpec((per_user, events), lambda user: (user, 0)),
        ],
        out_shape=[
            jax.ShapeDtypeStruct((requests, key_width), jnp.bfloat16),
            jax.ShapeDtypeStruct((requests, key_width), jnp.float32),
            jax.ShapeDtypeStruct((requests, events), jnp.bfloat16),
        ],
        compiler_params=pltpu.CompilerParams(vmem_limit_bytes=60 * MIB),
        cost_estimate=pl.CostEstimate(
            flops=4 * requests * events * key_width, bytes_accessed=1 << 24, transcendentals=0
        ),
        name="attend",
    )(inv_count, slots, near, far, history, usable)


def score_kernel(
    inv_ref,
    queries_ref,
    attended_ref,
    labels_ref,
    mlp_ref,
    logit_weight_ref,
    logits_ref,
    grad_att_ref,
    direct_ref,
):
    step_users = inv_ref.shape[0] // pl.num_programs(0)
    per_user = queries_ref.shape[0] // step_users
    query_b = queries_ref[...]
    query_f = query_b.astype(jnp.float32)
    attended = attended_ref[...]
    key_width = query_f.shape[1]
    joined = jnp.concatenate(
        [query_b, attended.astype(jnp.bfloat16), (query_f * attended).astype(jnp.bfloat16)], axis=1
    )
    pre_act = dot(joined, mlp_ref[...])
    act_sig = 0.5 * jnp.tanh(0.5 * pre_act) + 0.5
    hidden_units = (pre_act * act_sig).astype(jnp.bfloat16)
    weight = logit_weight_ref[...].astype(jnp.float32)
    logits = jnp.sum(hidden_units.astype(jnp.float32) * weight, axis=1, keepdims=True)
    logits_ref[...] = logits
    dlogit = (0.5 * jnp.tanh(0.5 * logits) + 0.5) - labels_ref[...].astype(jnp.float32)
    grad_pre = (dlogit * weight * (act_sig * (1.0 + pre_act * (1.0 - act_sig)))).astype(jnp.bfloat16)
    djoined = dot_rows(grad_pre, mlp_ref[...])
    part_query = djoined[:, :key_width]
    part_att = djoined[:, key_width : 2 * key_width]
    part_prod = djoined[:, 2 * key_width :]
    grad_att = part_att + part_prod * query_f
    for user in range(step_users):
        rows = slice(user * per_user, (user + 1) * per_user)
        inv_count = inv_ref[pl.program_id(0) * step_users + user]
        grad_att_ref[rows, :] = (grad_att[rows] * inv_count).astype(jnp.bfloat16)
    direct_ref[...] = part_query + part_prod * attended


def score(inv_count, queries, attended, labels, mlp_weight, logit_weight):
    users = inv_count.shape[0]
    requests, key_width = queries.shape
    steps = math.gcd(users, 2)
    step_rows = requests // steps
    block = pl.BlockSpec((step_rows, key_width), lambda step: (step, 0))
    column = pl.BlockSpec((step_rows, 1), lambda step: (step, 0))
    return pl.pallas_call(
        score_kernel,
        grid=(steps,),
        in_specs=[
            pl.BlockSpec(memory_space=pltpu.SMEM),
            block,
            block,
            column,
            pl.BlockSpec(mlp_weight.shape, lambda step: (0, 0)),
            pl.BlockSpec(logit_weight.shape, lambda step: (0, 0)),
        ],
        out_specs=[column, block, block],
        out_shape=[
            jax.ShapeDtypeStruct((requests, 1), jnp.float32),
            jax.ShapeDtypeStruct((requests, key_width), jnp.bfloat16),
            jax.ShapeDtypeStruct((requests, key_width), jnp.float32),
        ],
        compiler_params=pltpu.CompilerParams(vmem_limit_bytes=32 * MIB),
        cost_estimate=pl.CostEstimate(
            flops=4 * requests * mlp_weight.shape[0] * mlp_weight.shape[1],
            bytes_accessed=1 << 23,
            transcendentals=0,
        ),
        name="score",
    )(inv_count, queries, attended, labels, mlp_weight, logit_weight)


def attend_back_kernel(
    grad_att_ref, direct_ref, slope_ref, history_ref, grad_rows_ref
):
    grad_att = grad_att_ref[...]
    events, key_width = history_ref.shape
    chunk = math.gcd(events, 512)
    back = jnp.zeros(direct_ref.shape, jnp.float32)
    for at in range(0, events, chunk):
        keys = history_ref[at : at + chunk, :]
        slope = slope_ref[:, at : at + chunk].astype(jnp.float32)
        grad_sig = (dot_rows(grad_att, keys) * slope).astype(jnp.bfloat16)
        back += dot(grad_sig, keys)
    grad_rows_ref[...] = (direct_ref[...] + back * (1.0 / math.sqrt(key_width))).astype(jnp.bfloat16)


def attend_back(grad_att, direct, slope, history):
    users, events, key_width = history.shape
    requests = grad_att.shape[0]
    per_user = requests // users
    block = pl.BlockSpec((per_user, key_width), lambda user: (user, 0))
    return pl.pallas_call(
        attend_back_kernel,
        grid=(users,),
        in_specs=[
            block,
            block,
            pl.BlockSpec((per_user, events), lambda user: (user, 0)),
            pl.BlockSpec((None, events, key_width), lambda user: (user, 0, 0)),
        ],
        out_specs=block,
        out_shape=jax.ShapeDtypeStruct((requests, key_width), jnp.bfloat16),
        compiler_params=pltpu.CompilerParams(vmem_limit_bytes=20 * MIB),
        cost_estimate=pl.CostEstimate(
            flops=4 * requests * events * key_width, bytes_accessed=1 << 24, transcendentals=0
        ),
        name="attend_back",
    )(grad_att, direct, slope, history)


def terms_kernel(
    origins, core_ref, slots_ref, grad_rows_ref, near_ref, far_ref, keep_ref, send_ref, terms_ref
):
    half = near_ref.shape[0]
    requests = slots_ref.shape[1]
    grad_rows = grad_rows_ref[...]
    chunk = math.gcd(half, 512)
    steps = 0
    for offset, pooled_ref in ((0, near_ref), (half, far_ref)):
        for at in range(0, half, chunk):
            places = lax.broadcasted_iota(jnp.int32, (chunk, requests), 0) + (offset + at)
            row_hot = (places == slots_ref[...]).astype(jnp.bfloat16)
            cand_grad = dot(row_hot, grad_rows).astype(jnp.bfloat16)
            term = dot_columns(pooled_ref[at : at + chunk, :], cand_grad)
            if steps == 0:
                terms_ref[...] = term
            else:
                terms_ref[...] += term
            steps += 1
    rows = terms_ref.shape[0] // len(origins)
    core = core_ref[0]
    batch = max(1, 32 // rows)
    for slot in range(0, len(origins), batch):
        found = [
            terms_ref[pl.ds(pl.multiple_of((core ^ origins[slot + i]) * rows, rows), rows), :]
            for i in range(batch)
        ]
        found = found[0] if batch == 1 else jnp.concatenate(found, axis=0)
        out_ref, at = (keep_ref, slot) if slot < len(origins) // 2 else (send_ref, slot - len(origins) // 2)
        out_ref[at * rows : (at + batch) * rows, :] = found.astype(jnp.bfloat16)


def own_terms(origins, core, slots, grad_rows, near, far):
    width, key_width = near.shape[1], grad_rows.shape[1]
    whole = pl.BlockSpec(memory_space=pltpu.VMEM)
    return pl.pallas_call(
        functools.partial(terms_kernel, origins),
        in_specs=[pl.BlockSpec(memory_space=pltpu.SMEM), whole, whole, whole, whole],
        out_specs=[whole, whole],
        out_shape=[jax.ShapeDtypeStruct((width // 2, key_width), jnp.bfloat16)] * 2,
        scratch_shapes=[pltpu.VMEM((width, key_width), jnp.float32)],
        compiler_params=pltpu.CompilerParams(vmem_limit_bytes=20 * MIB),
        cost_estimate=pl.CostEstimate(
            flops=4 * near.shape[0] * key_width * (width + grad_rows.shape[0]),
            bytes_accessed=1 << 23,
            transcendentals=0,
        ),
        name="own_terms",
    )(core, slots, grad_rows, near, far)


def bit_groups(size):
    groups = []
    bit = 0
    while (1 << bit) < size:
        values = min(4, size >> bit)
        groups.append((bit, values))
        bit += values.bit_length() - 1
    return groups


def exchange(values, axis_name, size, distance):
    return lax.ppermute(values, axis_name, [(i, i ^ distance) for i in range(size)])


def stage_groups(wides, bit, values):
    mask = (values - 1) << bit
    return [[i | (step << bit) for step in range(values)] for i in range(wides) if not i & mask]


def swap_blocks(rows, wides, bit, values):
    return lax.all_to_all(
        rows,
        "wide",
        split_axis=0,
        concat_axis=0,
        axis_index_groups=stage_groups(wides, bit, values),
        tiled=True,
    )


def gather_stage(rows, wides, bit, values):
    return swap_blocks(jnp.concatenate([rows] * values, axis=0), wides, bit, values)


def after(values, *others):
    return lax.optimization_barrier((values,) + others)[0]


def slot_of(distance, wides):
    slot = 0
    for bit, values in bit_groups(wides):
        slot = slot * values + ((distance >> bit) & (values - 1))
    return slot + (distance // wides) * wides


def sum_blocks(keep, send, wides):
    total = keep.astype(jnp.float32) + exchange(send, "section", 2, 1).astype(jnp.float32)
    for bit, values in bit_groups(wides):
        parts = swap_blocks(total.astype(jnp.bfloat16), wides, bit, values)
        total = jnp.sum(parts.astype(jnp.float32).reshape((values, -1) + keep.shape[1:]), axis=0)
    return total


def body(
    frames,
    qkv_weight,
    out_weight,
    proj_weight,
    mlp_weight,
    logit_weight,
    history,
    hist_len,
    hist_mask,
    req_owner,
    req_local,
    labels,
):
    wides = lax.axis_size("wide")
    devices = lax.axis_size("section") * wides
    core = lax.axis_index("section") * wides
    cand_count = frames.shape[0]
    requests = req_local.shape[0]
    users, events, _ = history.shape
    pooled, embedded = encode_block(frames, qkv_weight, out_weight, proj_weight)
    positions = jnp.arange(events, dtype=jnp.int32)[None, :]
    usable = (
        (positions < hist_len[:, None]) & ((hist_mask == 1) | (positions == 0))
    ).astype(jnp.float32)
    inv_count = lax.rsqrt(jnp.sum(usable, axis=1))
    usable = usable.reshape(users, 1, events)
    slots = slot_of(req_owner[:, 0] ^ core, wides) * cand_count + req_local
    stages = list(reversed(bit_groups(wides)))
    near_embedded = embedded
    for bit, values in stages:
        near_embedded = gather_stage(near_embedded, wides, bit, values)
    far_embedded = exchange(near_embedded, "section", 2, 1)
    near_pooled = gather_stage(after(pooled, near_embedded), wides, *stages[0])
    queries, attended, slope = attend(
        inv_count, slots.reshape(requests, 1), near_embedded, far_embedded, history, usable
    )
    near_pooled = after(near_pooled, attended)
    for bit, values in stages[1:]:
        near_pooled = gather_stage(near_pooled, wides, bit, values)
    logits, grad_att, direct = score(
        inv_count,
        queries,
        attended,
        labels.reshape(requests, 1),
        mlp_weight,
        logit_weight.reshape(1, -1),
    )
    far_pooled = exchange(after(near_pooled, grad_att), "section", 2, 1)
    grad_rows = attend_back(grad_att, direct, slope, history)
    origins = [0] * devices
    for distance in range(devices):
        origins[slot_of(distance, wides)] = distance
    keep, send = own_terms(
        origins, core.reshape(1), slots.reshape(1, requests), grad_rows, near_pooled, far_pooled
    )
    grad_proj = sum_blocks(keep, send, wides)
    return (logits.reshape(requests), grad_proj)


def solution(mesh):
    in_specs = (
        P(("section", "wide"), None, None),
        P(),
        P(),
        P(),
        P(),
        P(),
        P(("section", "wide"), None, None),
        P(("section", "wide")),
        P(("section", "wide"), None),
        P(("section", "wide"), None),
        P(("section", "wide")),
        P(("section", "wide")),
    )
    out_specs = (P(("section", "wide")), P(("section", "wide"), None))
    return jax.shard_map(body, mesh=mesh, in_specs=in_specs, out_specs=out_specs, check_vma=False)
```

```python
import functools
import math

import jax
import jax.numpy as jnp
from jax import lax
from jax.experimental import pallas as pl
from jax.experimental.pallas import tpu as pltpu
from jax.sharding import PartitionSpec as P

HEADS = 16
FRAMES = 3


EPSILON = 1e-06
MIB = 1024 * 1024


def layer_norm(values):
    center = values - jnp.mean(values, axis=-1, keepdims=True)
    spread = jnp.mean(jnp.square(center), axis=-1, keepdims=True)
    return center * lax.rsqrt(spread + EPSILON)


def dot(left, right):
    return jnp.dot(left, right, preferred_element_type=jnp.float32)


def dot_rows(left, right):
    return lax.dot_general(left, right, (((1,), (1,)), ((), ())), preferred_element_type=jnp.float32)


def dot_columns(left, right):
    return lax.dot_general(left, right, (((0,), (0,)), ((), ())), preferred_element_type=jnp.float32)


def split_rows(values):
    high = values.astype(jnp.bfloat16)
    low = (values - high.astype(jnp.float32)).astype(jnp.bfloat16)
    return jnp.concatenate([high, low], axis=0)


def dot_split(values, right):
    both = dot(split_rows(values), right)
    rows = values.shape[0]
    return both[:rows] + both[rows:]


def encode_kernel(
    tokens,
    core_ref,
    first_ref,
    next_ref,
    qkv_hbm,
    out_hbm,
    proj_hbm,
    keep_ref,
    send_ref,
    embedded_ref,
    qkv_ref,
    out_ref,
    proj_ref,
    sems,
    normed_ref,
    packed_ref,
    scores_ref,
    mixed_rows_ref,
    sums_ref,
):
    group = pl.program_id(0)
    rows, width = next_ref.shape
    head_dim = width // HEADS
    patches = tokens // FRAMES
    cands = rows // tokens
    lanes = 2 * head_dim
    parts = 3
    copies = [
        pltpu.make_async_copy(
            qkv_hbm.at[:, pl.ds(part * width, width)],
            qkv_ref.at[:, pl.ds(part * width, width)],
            sems.at[part],
        )
        for part in range(parts)
    ]
    copies.append(pltpu.make_async_copy(out_hbm, out_ref, sems.at[parts]))
    copies.append(pltpu.make_async_copy(proj_hbm, proj_ref, sems.at[parts + 1]))

    @pl.when(group == 0)
    def _():
        for copy in copies:
            copy.start()

    def norm_cand(source_ref, half, cand_group, cand):
        at = cand * tokens
        inputs = source_ref[at : at + tokens, :].astype(jnp.float32)
        start = pl.multiple_of(half * rows, rows) + at
        normed_ref[pl.ds(pl.multiple_of(start, tokens), tokens), :] = layer_norm(inputs).astype(
            jnp.bfloat16
        )
        sums_ref[cand_group * cands + cand] = jnp.sum(inputs, axis=0, keepdims=True)

    @pl.when(group == 0)
    def _():
        for cand in range(cands):
            norm_cand(first_ref, 0, 0, cand)
        copies[0].wait()
        copies[1].wait()

    place = pl.multiple_of((group % 2) * rows, rows)
    following = jnp.minimum(group + 1, pl.num_programs(0) - 1)
    exponent = math.log2(math.e) / math.sqrt(head_dim)
    blocks = rows // lanes
    pairs = HEADS // 2
    quad = 4
    span = quad * head_dim
    frame_at = (lax.broadcasted_iota(jnp.int32, (patches, quad * lanes), 1) % lanes) // patches
    nothing = jnp.zeros((head_dim, lanes), jnp.bfloat16)
    for part in range(2):
        packed_ref[:, part * width : (part + 1) * width] = dot(
            normed_ref[pl.ds(place, rows), :], qkv_ref[:, part * width : (part + 1) * width]
        ).astype(jnp.bfloat16)
    for group_heads in range(HEADS // quad):
        start = group_heads * span
        for block in range(blocks):
            block_rows = slice(block * lanes, (block + 1) * lanes)
            query = packed_ref[block_rows, start : start + span]
            keys = packed_ref[block_rows, width + start : width + start + span].T
            keys = jnp.concatenate(
                [
                    jnp.concatenate(
                        [nothing] * head
                        + [keys[head * head_dim : (head + 1) * head_dim]]
                        + [nothing] * (quad - 1 - head),
                        axis=1,
                    )
                    for head in range(quad)
                ],
                axis=0,
            )
            scores = dot(query, keys)
            own_scores = scores[:patches]
            for frame in range(1, lanes // patches):
                own_scores = jnp.where(
                    frame_at == frame, scores[frame * patches : (frame + 1) * patches], own_scores
                )
            for side in range(quad // 2):
                scores_ref[block, group_heads * (quad // 2) + side] = own_scores[
                    :, side * 2 * lanes : (side + 1) * 2 * lanes
                ]
        for cand in range(group_heads * cands * quad // HEADS, (group_heads + 1) * cands * quad // HEADS):
            norm_cand(next_ref, 1 - group % 2, following, cand)

    ones_row = lax.broadcasted_iota(jnp.int32, (2 * lanes, 2 * lanes), 0) // patches
    ones_column = lax.broadcasted_iota(jnp.int32, (2 * lanes, 2 * lanes), 1) // patches
    frame_ones = (ones_row == ones_column).astype(jnp.bfloat16)
    exp_scores = jnp.exp2(
        scores_ref[...].reshape(blocks * pairs * patches, 2 * lanes) * exponent
    )
    totals = dot(exp_scores.astype(jnp.bfloat16), frame_ones)
    probs = (exp_scores / totals).reshape(blocks * pairs, patches, 2 * lanes)
    sums = jnp.sum(probs, axis=1)
    key_sums = [
        jnp.concatenate(
            [
                sums[block * pairs : (block + 1) * pairs, side * lanes : (side + 1) * lanes]
                for block in range(blocks)
            ],
            axis=1,
        )
        for side in range(2)
    ]
    own = lax.broadcasted_iota(jnp.int32, (cands, rows), 1) // tokens == lax.broadcasted_iota(
        jnp.int32, (cands, rows), 0
    )
    spread = jnp.concatenate(
        [jnp.where(own, key_sums[head % 2][head // 2 : head // 2 + 1], 0.0) for head in range(HEADS)], axis=0
    ).astype(jnp.bfloat16)
    mixed_rows = dot(spread, normed_ref[pl.ds(place, rows), :])
    for head in range(HEADS):
        mixed_rows_ref[head, pl.ds(pl.multiple_of(group * cands, cands), cands), :] = mixed_rows[
            head * cands : (head + 1) * cands
        ]

    @pl.when(group == pl.num_programs(0) - 1)
    def _():
        for copy in copies[2:]:
            copy.wait()
        total = embedded_ref.shape[0]
        pieces = []
        for part in range(HEADS // quad):
            left = mixed_rows_ref[pl.ds(part * quad, quad)].reshape(quad * total, width)
            both = dot_split(left, qkv_ref[:, pl.ds(2 * width + part * span, span)])
            head_at = lax.broadcasted_iota(jnp.int32, (total, span), 1) // head_dim
            piece = jnp.zeros((total, span), jnp.float32)
            for head in range(quad):
                piece = jnp.where(head_at == head, both[head * total : (head + 1) * total], piece)
            pieces.append(piece)
        mixed_mean = jnp.concatenate(pieces, axis=1) * (1.0 / tokens)
        hidden = sums_ref[...].reshape(total, width) * (1.0 / tokens) + dot_split(mixed_mean, out_ref[...])
        pooled = layer_norm(hidden).astype(jnp.bfloat16)
        first, second = pooled[:, : width // 2], pooled[:, width // 2 :]
        keep_ref[...] = jnp.where(core_ref[0] == 0, first, second)
        send_ref[...] = jnp.where(core_ref[0] == 0, second, first)
        embedded_ref[...] = dot(pooled, proj_ref[...]).astype(jnp.bfloat16)


def encode_block(core, frames, qkv_weight, out_weight, proj_weight):
    cand_count, tokens, width = frames.shape
    key_width = proj_weight.shape[1]
    cands = 8
    rows = cands * tokens
    last = cand_count // cands - 1
    rows_in = frames.reshape(cand_count * tokens, width)
    lanes = 2 * width // HEADS
    patches = tokens // FRAMES
    return pl.pallas_call(
        functools.partial(encode_kernel, tokens),
        grid=(cand_count // cands,),
        in_specs=[
            pl.BlockSpec(memory_space=pltpu.SMEM),
            pl.BlockSpec((rows, width), lambda group: (0, 0)),
            pl.BlockSpec((rows, width), lambda group: (jnp.minimum(group + 1, last), 0)),
            pl.BlockSpec(memory_space=pltpu.HBM),
            pl.BlockSpec(memory_space=pltpu.HBM),
            pl.BlockSpec(memory_space=pltpu.HBM),
        ],
        out_specs=[
            pl.BlockSpec((cand_count, width // 2), lambda group: (0, 0)),
            pl.BlockSpec((cand_count, width // 2), lambda group: (0, 0)),
            pl.BlockSpec((cand_count, key_width), lambda group: (0, 0)),
        ],
        out_shape=[
            jax.ShapeDtypeStruct((cand_count, width // 2), jnp.bfloat16),
            jax.ShapeDtypeStruct((cand_count, width // 2), jnp.bfloat16),
            jax.ShapeDtypeStruct((cand_count, key_width), jnp.bfloat16),
        ],
        scratch_shapes=[
            pltpu.VMEM(qkv_weight.shape, jnp.bfloat16),
            pltpu.VMEM(out_weight.shape, jnp.bfloat16),
            pltpu.VMEM(proj_weight.shape, jnp.bfloat16),
            pltpu.SemaphoreType.DMA((5,)),
            pltpu.VMEM((2 * rows, width), jnp.bfloat16),
            pltpu.VMEM((rows, 2 * width), jnp.bfloat16),
            pltpu.VMEM((rows * FRAMES // tokens * patches // lanes, HEADS // 2, patches, 2 * lanes), jnp.float32),
            pltpu.VMEM((HEADS, cand_count, width), jnp.float32),
            pltpu.VMEM((cand_count, 1, width), jnp.float32),
        ],
        compiler_params=pltpu.CompilerParams(vmem_limit_bytes=53 * MIB),
        cost_estimate=pl.CostEstimate(
            flops=5 * cand_count * tokens * width * width, bytes_accessed=1 << 24, transcendentals=0
        ),
        name="encode",
    )(core, rows_in, rows_in, qkv_weight, out_weight, proj_weight)


def attend_kernel(
    inv_ref,
    slots_ref,
    near_ref,
    far_ref,
    history_ref,
    usable_ref,
    queries_ref,
    attended_ref,
    slope_ref,
):
    slots = slots_ref[...]
    half, key_width = near_ref.shape
    places = lax.broadcasted_iota(jnp.int32, (slots.shape[0], half), 1)
    queries = dot((slots == places).astype(jnp.bfloat16), near_ref[...])
    queries += dot((slots == places + half).astype(jnp.bfloat16), far_ref[...])
    queries = queries.astype(jnp.bfloat16)
    queries_ref[...] = queries
    events = history_ref.shape[0]
    chunk = math.gcd(events, 1024)
    attended = jnp.zeros(attended_ref.shape, jnp.float32)
    for at in range(0, events, chunk):
        keys = history_ref[at : at + chunk, :]
        half_gate = 0.5 * jnp.tanh(dot_rows(queries, keys) * (0.5 / math.sqrt(key_width)))
        weights = (0.5 + half_gate) * usable_ref[:, at : at + chunk]
        slope_ref[:, at : at + chunk] = (weights * (0.5 - half_gate)).astype(jnp.bfloat16)
        attended += dot(weights.astype(jnp.bfloat16), keys)
    attended_ref[...] = attended * inv_ref[pl.program_id(0)]


def attend(inv_count, slots, near, far, history, usable):
    users, events, key_width = history.shape
    requests = slots.shape[0]
    per_user = requests // users
    return pl.pallas_call(
        attend_kernel,
        grid=(users,),
        in_specs=[
            pl.BlockSpec(memory_space=pltpu.SMEM),
            pl.BlockSpec((per_user, 1), lambda user: (user, 0)),
            pl.BlockSpec(near.shape, lambda user: (0, 0)),
            pl.BlockSpec(far.shape, lambda user: (0, 0)),
            pl.BlockSpec((None, events, key_width), lambda user: (user, 0, 0)),
            pl.BlockSpec((None, 1, events), lambda user: (user, 0, 0)),
        ],
        out_specs=[
            pl.BlockSpec((per_user, key_width), lambda user: (user, 0)),
            pl.BlockSpec((per_user, key_width), lambda user: (user, 0)),
            pl.BlockSpec((per_user, events), lambda user: (user, 0)),
        ],
        out_shape=[
            jax.ShapeDtypeStruct((requests, key_width), jnp.bfloat16),
            jax.ShapeDtypeStruct((requests, key_width), jnp.float32),
            jax.ShapeDtypeStruct((requests, events), jnp.bfloat16),
        ],
        compiler_params=pltpu.CompilerParams(vmem_limit_bytes=28 * MIB),
        cost_estimate=pl.CostEstimate(
            flops=4 * requests * events * key_width, bytes_accessed=1 << 24, transcendentals=0
        ),
        name="attend",
    )(inv_count, slots, near, far, history, usable)


def score_kernel(
    inv_ref,
    queries_ref,
    attended_ref,
    labels_ref,
    mlp_ref,
    logit_weight_ref,
    logits_ref,
    grad_att_ref,
    direct_ref,
):
    step_users = inv_ref.shape[0] // pl.num_programs(0)
    per_user = queries_ref.shape[0] // step_users
    query_b = queries_ref[...]
    query_f = query_b.astype(jnp.float32)
    attended = attended_ref[...]
    key_width = query_f.shape[1]
    joined = jnp.concatenate(
        [query_b, attended.astype(jnp.bfloat16), (query_f * attended).astype(jnp.bfloat16)], axis=1
    )
    pre_act = dot(joined, mlp_ref[...])
    act_sig = 0.5 * jnp.tanh(0.5 * pre_act) + 0.5
    hidden_units = (pre_act * act_sig).astype(jnp.bfloat16)
    weight = logit_weight_ref[...].astype(jnp.float32)
    logits = jnp.sum(hidden_units.astype(jnp.float32) * weight, axis=1, keepdims=True)
    logits_ref[...] = logits
    dlogit = (0.5 * jnp.tanh(0.5 * logits) + 0.5) - labels_ref[...].astype(jnp.float32)
    grad_pre = (dlogit * weight * (act_sig * (1.0 + pre_act * (1.0 - act_sig)))).astype(jnp.bfloat16)
    djoined = dot_rows(grad_pre, mlp_ref[...])
    part_query = djoined[:, :key_width]
    part_att = djoined[:, key_width : 2 * key_width]
    part_prod = djoined[:, 2 * key_width :]
    grad_att = part_att + part_prod * query_f
    for user in range(step_users):
        rows = slice(user * per_user, (user + 1) * per_user)
        inv_count = inv_ref[pl.program_id(0) * step_users + user]
        grad_att_ref[rows, :] = (grad_att[rows] * inv_count).astype(jnp.bfloat16)
    direct_ref[...] = part_query + part_prod * attended


def score(inv_count, queries, attended, labels, mlp_weight, logit_weight):
    users = inv_count.shape[0]
    requests, key_width = queries.shape
    steps = math.gcd(users, 2)
    step_rows = requests // steps
    block = pl.BlockSpec((step_rows, key_width), lambda step: (step, 0))
    column = pl.BlockSpec((step_rows, 1), lambda step: (step, 0))
    return pl.pallas_call(
        score_kernel,
        grid=(steps,),
        in_specs=[
            pl.BlockSpec(memory_space=pltpu.SMEM),
            block,
            block,
            column,
            pl.BlockSpec(mlp_weight.shape, lambda step: (0, 0)),
            pl.BlockSpec(logit_weight.shape, lambda step: (0, 0)),
        ],
        out_specs=[column, block, block],
        out_shape=[
            jax.ShapeDtypeStruct((requests, 1), jnp.float32),
            jax.ShapeDtypeStruct((requests, key_width), jnp.bfloat16),
            jax.ShapeDtypeStruct((requests, key_width), jnp.float32),
        ],
        compiler_params=pltpu.CompilerParams(vmem_limit_bytes=32 * MIB),
        cost_estimate=pl.CostEstimate(
            flops=4 * requests * mlp_weight.shape[0] * mlp_weight.shape[1],
            bytes_accessed=1 << 23,
            transcendentals=0,
        ),
        name="score",
    )(inv_count, queries, attended, labels, mlp_weight, logit_weight)


def attend_back_kernel(
    grad_att_ref, direct_ref, slope_ref, history_ref, grad_rows_ref
):
    grad_att = grad_att_ref[...]
    events, key_width = history_ref.shape
    chunk = math.gcd(events, 512)
    back = jnp.zeros(direct_ref.shape, jnp.float32)
    for at in range(0, events, chunk):
        keys = history_ref[at : at + chunk, :]
        slope = slope_ref[:, at : at + chunk].astype(jnp.float32)
        grad_sig = (dot_rows(grad_att, keys) * slope).astype(jnp.bfloat16)
        back += dot(grad_sig, keys)
    grad_rows_ref[...] = (direct_ref[...] + back * (1.0 / math.sqrt(key_width))).astype(jnp.bfloat16)


def attend_back(first, count, grad_att, direct, slope, history):
    users, events, key_width = history.shape
    requests = grad_att.shape[0]
    per_user = requests // users
    block = pl.BlockSpec((per_user, key_width), lambda user: (first + user, 0))
    return pl.pallas_call(
        attend_back_kernel,
        grid=(count,),
        in_specs=[
            block,
            block,
            pl.BlockSpec((per_user, events), lambda user: (first + user, 0)),
            pl.BlockSpec((None, events, key_width), lambda user: (first + user, 0, 0)),
        ],
        out_specs=pl.BlockSpec((per_user, key_width), lambda user: (user, 0)),
        out_shape=jax.ShapeDtypeStruct((count * per_user, key_width), jnp.bfloat16),
        compiler_params=pltpu.CompilerParams(vmem_limit_bytes=20 * MIB),
        cost_estimate=pl.CostEstimate(
            flops=4 * count * per_user * events * key_width, bytes_accessed=1 << 24, transcendentals=0
        ),
        name="attend_back",
    )(grad_att, direct, slope, history)


def terms_kernel(origins, wide_ref, slots_ref, *refs):
    grad_refs = refs[:-4]
    pooled_ref, out_ref, grad_rows_ref, terms_ref = refs[-4:]
    at = 0
    for grad_ref in grad_refs:
        grad_rows_ref[at : at + grad_ref.shape[0], :] = grad_ref[...]
        at += grad_ref.shape[0]
    cands = pooled_ref.shape[0]
    requests = slots_ref.shape[1]
    chunk = math.gcd(cands, 512)
    for at in range(0, cands, chunk):
        places = lax.broadcasted_iota(jnp.int32, (chunk, requests), 0) + at
        row_hot = (places == slots_ref[...]).astype(jnp.bfloat16)
        cand_grad = dot(row_hot, grad_rows_ref[...]).astype(jnp.bfloat16)
        term = dot_columns(pooled_ref[at : at + chunk, :], cand_grad)
        if at == 0:
            terms_ref[...] = term
        else:
            terms_ref[...] += term
    rows = terms_ref.shape[0] // len(origins)
    wide = wide_ref[0]
    batch = max(1, 32 // rows)
    for slot in range(0, len(origins), batch):
        found = [
            terms_ref[pl.ds(pl.multiple_of((wide ^ origins[slot + i]) * rows, rows), rows), :]
            for i in range(batch)
        ]
        found = found[0] if batch == 1 else jnp.concatenate(found, axis=0)
        out_ref[slot * rows : (slot + batch) * rows, :] = found.astype(jnp.bfloat16)


def chip_terms(origins, wide, slots, grad_parts, pooled):
    cands, width = pooled.shape
    requests = slots.shape[1]
    key_width = grad_parts[0].shape[1]
    whole = pl.BlockSpec(memory_space=pltpu.VMEM)
    return pl.pallas_call(
        functools.partial(terms_kernel, origins),
        in_specs=[pl.BlockSpec(memory_space=pltpu.SMEM)] + [whole] * (len(grad_parts) + 2),
        out_specs=whole,
        out_shape=jax.ShapeDtypeStruct((width, key_width), jnp.bfloat16),
        scratch_shapes=[
            pltpu.VMEM((requests, key_width), jnp.bfloat16),
            pltpu.VMEM((width, key_width), jnp.float32),
        ],
        compiler_params=pltpu.CompilerParams(vmem_limit_bytes=20 * MIB),
        cost_estimate=pl.CostEstimate(
            flops=2 * cands * key_width * (width + requests),
            bytes_accessed=1 << 22,
            transcendentals=0,
        ),
        name="chip_terms",
    )(wide, slots, *grad_parts, pooled)


def bit_groups(size):
    groups = []
    bit = 0
    while (1 << bit) < size:
        values = min(4, size >> bit)
        groups.append((bit, values))
        bit += values.bit_length() - 1
    return groups


def exchange(values, axis_name, size, distance):
    return lax.ppermute(values, axis_name, [(i, i ^ distance) for i in range(size)])


def send_stage(rows, wides, bit, values):
    return [exchange(rows, "wide", wides, step << bit) for step in range(1, values)]


def after(values, *others):
    return lax.optimization_barrier((tuple(values),) + others)[0]


def slot_of(distance, wides):
    slot = 0
    for bit, values in bit_groups(wides):
        slot = slot * values + ((distance >> bit) & (values - 1))
    return slot


def sum_blocks(blocks, wides):
    total = blocks
    for bit, values in bit_groups(wides):
        parts = total.astype(jnp.bfloat16).reshape((values, -1) + blocks.shape[1:])
        found = [
            exchange(parts[step], "wide", wides, step << bit).astype(jnp.float32)
            for step in range(1, values)
        ]
        total = sum(found, parts[0].astype(jnp.float32))
    return total


def body(
    frames,
    qkv_weight,
    out_weight,
    proj_weight,
    mlp_weight,
    logit_weight,
    history,
    hist_len,
    hist_mask,
    req_owner,
    req_local,
    labels,
):
    wides = lax.axis_size("wide")
    core, wide = lax.axis_index("section"), lax.axis_index("wide")
    cand_count = frames.shape[0]
    requests = req_local.shape[0]
    users, events, _ = history.shape
    keep, send, embedded = encode_block(
        core.reshape(1), frames, qkv_weight, out_weight, proj_weight
    )
    positions = jnp.arange(events, dtype=jnp.int32)[None, :]
    usable = (
        (positions < hist_len[:, None]) & ((hist_mask == 1) | (positions == 0))
    ).astype(jnp.float32)
    inv_count = lax.rsqrt(jnp.sum(usable, axis=1))
    usable = usable.reshape(users, 1, events)
    owner_core = req_owner[:, 0] // wides
    owner_slot = slot_of((req_owner[:, 0] % wides) ^ wide, wides)
    slots = ((owner_core ^ core) * wides + owner_slot) * cand_count + req_local
    pooled_slots = (owner_slot * 2 + owner_core) * cand_count + req_local
    stages = list(reversed(bit_groups(wides)))
    near = embedded
    for bit, values in stages:
        near = jnp.concatenate([near] + send_stage(near, wides, bit, values), axis=0)
    far = exchange(near, "section", 2, 1)
    far_slots = exchange(pooled_slots, "section", 2, 1)
    keep, send = after((keep, send), near)
    got = exchange(send, "section", 2, 1)
    pooled = jnp.where(
        core == 0, jnp.concatenate([keep, got], axis=0), jnp.concatenate([got, keep], axis=0)
    )
    found = send_stage(pooled, wides, *stages[0])
    queries, attended, slope = attend(
        inv_count, slots.reshape(requests, 1), near, far, history, usable
    )
    for stage in stages[1:]:
        pooled = jnp.concatenate(after([pooled] + found, attended), axis=0)
        found = send_stage(pooled, wides, *stage)
    logits, grad_att, direct = score(
        inv_count,
        queries,
        attended,
        labels.reshape(requests, 1),
        mlp_weight,
        logit_weight.reshape(1, -1),
    )
    half = users // 2
    grad_parts = [
        attend_back(0, half, grad_att, direct, slope, history),
        attend_back(half, users - half, grad_att, direct, slope, history),
    ]
    far_parts = [exchange(part, "section", 2, 1) for part in grad_parts]
    pooled = jnp.concatenate(after([pooled] + found, grad_parts[1]), axis=0)
    origins = [0] * wides
    for distance in range(wides):
        origins[slot_of(distance, wides)] = distance
    terms = chip_terms(
        origins,
        wide.reshape(1),
        jnp.concatenate([pooled_slots, far_slots]).reshape(1, 2 * requests),
        grad_parts + far_parts,
        pooled,
    )
    grad_proj = sum_blocks(terms, wides)
    return (logits.reshape(requests), grad_proj)


def solution(mesh):
    in_specs = (
        P(("section", "wide"), None, None),
        P(),
        P(),
        P(),
        P(),
        P(),
        P(("section", "wide"), None, None),
        P(("section", "wide")),
        P(("section", "wide"), None),
        P(("section", "wide"), None),
        P(("section", "wide")),
        P(("section", "wide")),
    )
    out_specs = (P(("section", "wide")), P(("section", "wide"), None))
    return jax.shard_map(body, mesh=mesh, in_specs=in_specs, out_specs=out_specs, check_vma=False)
```

```python
import functools
import math

import jax
import jax.numpy as jnp
from jax import lax
from jax.experimental import pallas as pl
from jax.experimental.pallas import tpu as pltpu
from jax.sharding import PartitionSpec as P

HEADS = 16
FRAMES = 3


EPSILON = 1e-06
MIB = 1024 * 1024


def layer_norm(values):
    center = values - jnp.mean(values, axis=-1, keepdims=True)
    spread = jnp.mean(jnp.square(center), axis=-1, keepdims=True)
    return center * lax.rsqrt(spread + EPSILON)


def dot(left, right):
    return jnp.dot(left, right, preferred_element_type=jnp.float32)


def dot_rows(left, right):
    return lax.dot_general(left, right, (((1,), (1,)), ((), ())), preferred_element_type=jnp.float32)


def dot_columns(left, right):
    return lax.dot_general(left, right, (((0,), (0,)), ((), ())), preferred_element_type=jnp.float32)


def split_rows(values):
    high = values.astype(jnp.bfloat16)
    low = (values - high.astype(jnp.float32)).astype(jnp.bfloat16)
    return jnp.concatenate([high, low], axis=0)


def dot_split(values, right):
    both = dot(split_rows(values), right)
    rows = values.shape[0]
    return both[:rows] + both[rows:]


def encode_kernel(
    tokens,
    core_ref,
    first_ref,
    next_ref,
    qkv_hbm,
    out_hbm,
    proj_hbm,
    history_hbm,
    keep_ref,
    send_ref,
    embedded_ref,
    history_ref,
    qkv_ref,
    out_ref,
    proj_ref,
    sems,
    normed_ref,
    packed_ref,
    scores_ref,
    mixed_rows_ref,
    sums_ref,
):
    group = pl.program_id(0)
    rows, width = next_ref.shape
    head_dim = width // HEADS
    patches = tokens // FRAMES
    cands = rows // tokens
    lanes = 2 * head_dim
    parts = 3
    copies = [
        pltpu.make_async_copy(
            qkv_hbm.at[:, pl.ds(part * width, width)],
            qkv_ref.at[:, pl.ds(part * width, width)],
            sems.at[part],
        )
        for part in range(parts)
    ]
    copies.append(pltpu.make_async_copy(out_hbm, out_ref, sems.at[parts]))
    copies.append(pltpu.make_async_copy(proj_hbm, proj_ref, sems.at[parts + 1]))
    copies.append(pltpu.make_async_copy(history_hbm, history_ref, sems.at[parts + 2]))

    @pl.when(group == 0)
    def _():
        for copy in copies:
            copy.start()

    def norm_cand(source_ref, half, cand_group, cand):
        at = cand * tokens
        inputs = source_ref[at : at + tokens, :].astype(jnp.float32)
        start = pl.multiple_of(half * rows, rows) + at
        normed_ref[pl.ds(pl.multiple_of(start, tokens), tokens), :] = layer_norm(inputs).astype(
            jnp.bfloat16
        )
        sums_ref[cand_group * cands + cand] = jnp.sum(inputs, axis=0, keepdims=True)

    @pl.when(group == 0)
    def _():
        for cand in range(cands):
            norm_cand(first_ref, 0, 0, cand)
        copies[0].wait()
        copies[1].wait()

    place = pl.multiple_of((group % 2) * rows, rows)
    following = jnp.minimum(group + 1, pl.num_programs(0) - 1)
    exponent = math.log2(math.e) / math.sqrt(head_dim)
    blocks = rows // lanes
    pairs = HEADS // 2
    quad = 4
    span = quad * head_dim
    frame_at = (lax.broadcasted_iota(jnp.int32, (patches, quad * lanes), 1) % lanes) // patches
    nothing = jnp.zeros((head_dim, lanes), jnp.bfloat16)
    for part in range(2):
        packed_ref[:, part * width : (part + 1) * width] = dot(
            normed_ref[pl.ds(place, rows), :], qkv_ref[:, part * width : (part + 1) * width]
        ).astype(jnp.bfloat16)
    for group_heads in range(HEADS // quad):
        start = group_heads * span
        for block in range(blocks):
            block_rows = slice(block * lanes, (block + 1) * lanes)
            query = packed_ref[block_rows, start : start + span]
            keys = packed_ref[block_rows, width + start : width + start + span].T
            keys = jnp.concatenate(
                [
                    jnp.concatenate(
                        [nothing] * head
                        + [keys[head * head_dim : (head + 1) * head_dim]]
                        + [nothing] * (quad - 1 - head),
                        axis=1,
                    )
                    for head in range(quad)
                ],
                axis=0,
            )
            scores = dot(query, keys)
            own_scores = scores[:patches]
            for frame in range(1, lanes // patches):
                own_scores = jnp.where(
                    frame_at == frame, scores[frame * patches : (frame + 1) * patches], own_scores
                )
            for side in range(quad // 2):
                scores_ref[block, group_heads * (quad // 2) + side] = own_scores[
                    :, side * 2 * lanes : (side + 1) * 2 * lanes
                ]
        for cand in range(group_heads * cands * quad // HEADS, (group_heads + 1) * cands * quad // HEADS):
            norm_cand(next_ref, 1 - group % 2, following, cand)

    ones_row = lax.broadcasted_iota(jnp.int32, (2 * lanes, 2 * lanes), 0) // patches
    ones_column = lax.broadcasted_iota(jnp.int32, (2 * lanes, 2 * lanes), 1) // patches
    frame_ones = (ones_row == ones_column).astype(jnp.bfloat16)
    exp_scores = jnp.exp2(
        scores_ref[...].reshape(blocks * pairs * patches, 2 * lanes) * exponent
    )
    totals = dot(exp_scores.astype(jnp.bfloat16), frame_ones)
    probs = (exp_scores / totals).reshape(blocks * pairs, patches, 2 * lanes)
    sums = jnp.sum(probs, axis=1)
    key_sums = [
        jnp.concatenate(
            [
                sums[block * pairs : (block + 1) * pairs, side * lanes : (side + 1) * lanes]
                for block in range(blocks)
            ],
            axis=1,
        )
        for side in range(2)
    ]
    own = lax.broadcasted_iota(jnp.int32, (cands, rows), 1) // tokens == lax.broadcasted_iota(
        jnp.int32, (cands, rows), 0
    )
    spread = jnp.concatenate(
        [jnp.where(own, key_sums[head % 2][head // 2 : head // 2 + 1], 0.0) for head in range(HEADS)], axis=0
    ).astype(jnp.bfloat16)
    mixed_rows = dot(spread, normed_ref[pl.ds(place, rows), :])
    for head in range(HEADS):
        mixed_rows_ref[head, pl.ds(pl.multiple_of(group * cands, cands), cands), :] = mixed_rows[
            head * cands : (head + 1) * cands
        ]

    @pl.when(group == pl.num_programs(0) - 1)
    def _():
        for copy in copies[2:]:
            copy.wait()
        total = embedded_ref.shape[0]
        pieces = []
        for part in range(HEADS // quad):
            left = mixed_rows_ref[pl.ds(part * quad, quad)].reshape(quad * total, width)
            both = dot_split(left, qkv_ref[:, pl.ds(2 * width + part * span, span)])
            head_at = lax.broadcasted_iota(jnp.int32, (total, span), 1) // head_dim
            piece = jnp.zeros((total, span), jnp.float32)
            for head in range(quad):
                piece = jnp.where(head_at == head, both[head * total : (head + 1) * total], piece)
            pieces.append(piece)
        mixed_mean = jnp.concatenate(pieces, axis=1) * (1.0 / tokens)
        hidden = sums_ref[...].reshape(total, width) * (1.0 / tokens) + dot_split(mixed_mean, out_ref[...])
        pooled = layer_norm(hidden).astype(jnp.bfloat16)
        first, second = pooled[:, : width // 2], pooled[:, width // 2 :]
        keep_ref[...] = jnp.where(core_ref[0] == 0, first, second)
        send_ref[...] = jnp.where(core_ref[0] == 0, second, first)
        embedded_ref[...] = dot(pooled, proj_ref[...]).astype(jnp.bfloat16)


def in_hbm(*arrays):
    return [pltpu.with_memory_space_constraint(array, pltpu.HBM) for array in arrays]


def encode_block(core, frames, qkv_weight, out_weight, proj_weight, history):
    cand_count, tokens, width = frames.shape
    key_width = proj_weight.shape[1]
    cands = 8
    rows = cands * tokens
    last = cand_count // cands - 1
    rows_in = in_hbm(frames.reshape(cand_count * tokens, width))[0]
    lanes = 2 * width // HEADS
    patches = tokens // FRAMES
    return pl.pallas_call(
        functools.partial(encode_kernel, tokens),
        grid=(cand_count // cands,),
        in_specs=[
            pl.BlockSpec(memory_space=pltpu.SMEM),
            pl.BlockSpec((rows, width), lambda group: (0, 0)),
            pl.BlockSpec((rows, width), lambda group: (jnp.minimum(group + 1, last), 0)),
            pl.BlockSpec(memory_space=pltpu.HBM),
            pl.BlockSpec(memory_space=pltpu.HBM),
            pl.BlockSpec(memory_space=pltpu.HBM),
            pl.BlockSpec(memory_space=pltpu.HBM),
        ],
        out_specs=[
            pl.BlockSpec((cand_count, width // 2), lambda group: (0, 0)),
            pl.BlockSpec((cand_count, width // 2), lambda group: (0, 0)),
            pl.BlockSpec((cand_count, key_width), lambda group: (0, 0)),
            pl.BlockSpec(memory_space=pltpu.VMEM),
        ],
        out_shape=[
            jax.ShapeDtypeStruct((cand_count, width // 2), jnp.bfloat16),
            jax.ShapeDtypeStruct((cand_count, width // 2), jnp.bfloat16),
            jax.ShapeDtypeStruct((cand_count, key_width), jnp.bfloat16),
            pltpu.VMEM(history.shape, history.dtype),
        ],
        scratch_shapes=[
            pltpu.VMEM(qkv_weight.shape, jnp.bfloat16),
            pltpu.VMEM(out_weight.shape, jnp.bfloat16),
            pltpu.VMEM(proj_weight.shape, jnp.bfloat16),
            pltpu.SemaphoreType.DMA((6,)),
            pltpu.VMEM((2 * rows, width), jnp.bfloat16),
            pltpu.VMEM((rows, 2 * width), jnp.bfloat16),
            pltpu.VMEM((rows * FRAMES // tokens * patches // lanes, HEADS // 2, patches, 2 * lanes), jnp.float32),
            pltpu.VMEM((HEADS, cand_count, width), jnp.float32),
            pltpu.VMEM((cand_count, 1, width), jnp.float32),
        ],
        compiler_params=pltpu.CompilerParams(vmem_limit_bytes=40 * MIB),
        cost_estimate=pl.CostEstimate(
            flops=5 * cand_count * tokens * width * width, bytes_accessed=1 << 24, transcendentals=0
        ),
        name="encode",
    )(core, rows_in, rows_in, *in_hbm(qkv_weight, out_weight, proj_weight, history))


def attend_kernel(
    inv_ref,
    slots_ref,
    near_ref,
    far_ref,
    history_ref,
    usable_ref,
    queries_ref,
    attended_ref,
    slope_ref,
):
    slots = slots_ref[...]
    half, key_width = near_ref.shape
    places = lax.broadcasted_iota(jnp.int32, (slots.shape[0], half), 1)
    queries = dot((slots == places).astype(jnp.bfloat16), near_ref[...])
    queries += dot((slots == places + half).astype(jnp.bfloat16), far_ref[...])
    queries_ref[...] = queries.astype(jnp.bfloat16)
    users, events, _ = history_ref.shape
    per_user = slots.shape[0] // users
    chunk = math.gcd(events, 1024)
    for user in range(users):
        rows = slice(user * per_user, (user + 1) * per_user)
        attended = jnp.zeros((per_user, key_width), jnp.float32)
        for at in range(0, events, chunk):
            keys = history_ref[user, at : at + chunk, :]
            usable = usable_ref[user, :, at : at + chunk]
            scores = dot_rows(queries_ref[rows, :], keys)
            half_gate = 0.5 * jnp.tanh(scores * (0.5 / math.sqrt(key_width)))
            weights = (0.5 + half_gate) * usable
            slope_ref[rows, at : at + chunk] = (weights * (0.5 - half_gate)).astype(jnp.bfloat16)
            attended += dot(weights.astype(jnp.bfloat16), keys)
        attended_ref[rows, :] = attended * inv_ref[user]


def attend(inv_count, slots, near, far, history, usable):
    users, events, key_width = history.shape
    requests = slots.shape[0]
    whole = pl.BlockSpec(memory_space=pltpu.VMEM)
    return pl.pallas_call(
        attend_kernel,
        in_specs=[pl.BlockSpec(memory_space=pltpu.SMEM)] + [whole] * 5,
        out_specs=[whole] * 3,
        out_shape=[
            jax.ShapeDtypeStruct((requests, key_width), jnp.bfloat16),
            jax.ShapeDtypeStruct((requests, key_width), jnp.float32),
            jax.ShapeDtypeStruct((requests, events), jnp.bfloat16),
        ],
        compiler_params=pltpu.CompilerParams(vmem_limit_bytes=28 * MIB),
        cost_estimate=pl.CostEstimate(
            flops=4 * requests * events * key_width, bytes_accessed=1 << 24, transcendentals=0
        ),
        name="attend",
    )(inv_count, slots, near, far, history, usable)


def score_kernel(
    inv_ref,
    queries_ref,
    attended_ref,
    labels_ref,
    mlp_ref,
    logit_weight_ref,
    logits_ref,
    grad_att_ref,
    direct_ref,
):
    step_users = inv_ref.shape[0] // pl.num_programs(0)
    per_user = queries_ref.shape[0] // step_users
    query_b = queries_ref[...]
    query_f = query_b.astype(jnp.float32)
    attended = attended_ref[...]
    key_width = query_f.shape[1]
    joined = jnp.concatenate(
        [query_b, attended.astype(jnp.bfloat16), (query_f * attended).astype(jnp.bfloat16)], axis=1
    )
    pre_act = dot(joined, mlp_ref[...])
    act_sig = 0.5 * jnp.tanh(0.5 * pre_act) + 0.5
    hidden_units = (pre_act * act_sig).astype(jnp.bfloat16)
    weight = logit_weight_ref[...].astype(jnp.float32)
    logits = jnp.sum(hidden_units.astype(jnp.float32) * weight, axis=1, keepdims=True)
    logits_ref[...] = logits
    dlogit = (0.5 * jnp.tanh(0.5 * logits) + 0.5) - labels_ref[...].astype(jnp.float32)
    grad_pre = (dlogit * weight * (act_sig * (1.0 + pre_act * (1.0 - act_sig)))).astype(jnp.bfloat16)
    djoined = dot_rows(grad_pre, mlp_ref[...])
    part_query = djoined[:, :key_width]
    part_att = djoined[:, key_width : 2 * key_width]
    part_prod = djoined[:, 2 * key_width :]
    grad_att = part_att + part_prod * query_f
    for user in range(step_users):
        rows = slice(user * per_user, (user + 1) * per_user)
        inv_count = inv_ref[pl.program_id(0) * step_users + user]
        grad_att_ref[rows, :] = (grad_att[rows] * inv_count).astype(jnp.bfloat16)
    direct_ref[...] = part_query + part_prod * attended


def score(inv_count, queries, attended, labels, mlp_weight, logit_weight):
    users = inv_count.shape[0]
    requests, key_width = queries.shape
    steps = math.gcd(users, 2)
    step_rows = requests // steps
    block = pl.BlockSpec((step_rows, key_width), lambda step: (step, 0))
    column = pl.BlockSpec((step_rows, 1), lambda step: (step, 0))
    return pl.pallas_call(
        score_kernel,
        grid=(steps,),
        in_specs=[
            pl.BlockSpec(memory_space=pltpu.SMEM),
            block,
            block,
            column,
            pl.BlockSpec(mlp_weight.shape, lambda step: (0, 0)),
            pl.BlockSpec(logit_weight.shape, lambda step: (0, 0)),
        ],
        out_specs=[column, block, block],
        out_shape=[
            jax.ShapeDtypeStruct((requests, 1), jnp.float32),
            jax.ShapeDtypeStruct((requests, key_width), jnp.bfloat16),
            jax.ShapeDtypeStruct((requests, key_width), jnp.float32),
        ],
        compiler_params=pltpu.CompilerParams(vmem_limit_bytes=32 * MIB),
        cost_estimate=pl.CostEstimate(
            flops=4 * requests * mlp_weight.shape[0] * mlp_weight.shape[1],
            bytes_accessed=1 << 23,
            transcendentals=0,
        ),
        name="score",
    )(inv_count, queries, attended, labels, mlp_weight, logit_weight)


def attend_back_kernel(first, grad_att_ref, direct_ref, slope_ref, history_ref, grad_rows_ref):
    users, events, key_width = history_ref.shape
    per_user = grad_att_ref.shape[0] // users
    chunk = math.gcd(events, 1024)
    for user in range(grad_rows_ref.shape[0] // per_user):
        rows = slice((first + user) * per_user, (first + user + 1) * per_user)
        back = jnp.zeros((per_user, key_width), jnp.float32)
        for at in range(0, events, chunk):
            keys = history_ref[first + user, at : at + chunk, :]
            slope = slope_ref[rows, at : at + chunk].astype(jnp.float32)
            grad_sig = (dot_rows(grad_att_ref[rows, :], keys) * slope).astype(jnp.bfloat16)
            back += dot(grad_sig, keys)
        grad_rows = direct_ref[rows, :] + back * (1.0 / math.sqrt(key_width))
        grad_rows_ref[user * per_user : (user + 1) * per_user, :] = grad_rows.astype(jnp.bfloat16)


def attend_back(first, count, grad_att, direct, slope, history):
    users, events, key_width = history.shape
    per_user = grad_att.shape[0] // users
    whole = pl.BlockSpec(memory_space=pltpu.VMEM)
    return pl.pallas_call(
        functools.partial(attend_back_kernel, first),
        in_specs=[whole] * 4,
        out_specs=whole,
        out_shape=jax.ShapeDtypeStruct((count * per_user, key_width), jnp.bfloat16),
        compiler_params=pltpu.CompilerParams(vmem_limit_bytes=20 * MIB),
        cost_estimate=pl.CostEstimate(
            flops=4 * count * per_user * events * key_width,
            bytes_accessed=1 << 23,
            transcendentals=0,
        ),
        name="attend_back",
    )(grad_att, direct, slope, history)


def terms_kernel(origins, wide_ref, slots_ref, *refs):
    grad_refs = refs[:-4]
    pooled_ref, out_ref, grad_rows_ref, terms_ref = refs[-4:]
    at = 0
    for grad_ref in grad_refs:
        grad_rows_ref[at : at + grad_ref.shape[0], :] = grad_ref[...]
        at += grad_ref.shape[0]
    cands = pooled_ref.shape[0]
    requests = slots_ref.shape[1]
    chunk = math.gcd(cands, 512)
    for at in range(0, cands, chunk):
        places = lax.broadcasted_iota(jnp.int32, (chunk, requests), 0) + at
        row_hot = (places == slots_ref[...]).astype(jnp.bfloat16)
        cand_grad = dot(row_hot, grad_rows_ref[...]).astype(jnp.bfloat16)
        term = dot_columns(pooled_ref[at : at + chunk, :], cand_grad)
        if at == 0:
            terms_ref[...] = term
        else:
            terms_ref[...] += term
    rows = terms_ref.shape[0] // len(origins)
    wide = wide_ref[0]
    batch = max(1, 32 // rows)
    for slot in range(0, len(origins), batch):
        found = [
            terms_ref[pl.ds(pl.multiple_of((wide ^ origins[slot + i]) * rows, rows), rows), :]
            for i in range(batch)
        ]
        found = found[0] if batch == 1 else jnp.concatenate(found, axis=0)
        out_ref[slot * rows : (slot + batch) * rows, :] = found.astype(jnp.bfloat16)


def chip_terms(origins, wide, slots, grad_parts, pooled):
    cands, width = pooled.shape
    requests = slots.shape[1]
    key_width = grad_parts[0].shape[1]
    whole = pl.BlockSpec(memory_space=pltpu.VMEM)
    return pl.pallas_call(
        functools.partial(terms_kernel, origins),
        in_specs=[pl.BlockSpec(memory_space=pltpu.SMEM)] + [whole] * (len(grad_parts) + 2),
        out_specs=whole,
        out_shape=jax.ShapeDtypeStruct((width, key_width), jnp.bfloat16),
        scratch_shapes=[
            pltpu.VMEM((requests, key_width), jnp.bfloat16),
            pltpu.VMEM((width, key_width), jnp.float32),
        ],
        compiler_params=pltpu.CompilerParams(vmem_limit_bytes=20 * MIB),
        cost_estimate=pl.CostEstimate(
            flops=2 * cands * key_width * (width + requests),
            bytes_accessed=1 << 22,
            transcendentals=0,
        ),
        name="chip_terms",
    )(wide, slots, *grad_parts, pooled)


def bit_groups(size):
    groups = []
    bit = 0
    while (1 << bit) < size:
        values = min(4, size >> bit)
        groups.append((bit, values))
        bit += values.bit_length() - 1
    return groups


def exchange(values, axis_name, size, distance):
    return lax.ppermute(values, axis_name, [(i, i ^ distance) for i in range(size)])


def send_stage(rows, wides, bit, values):
    return [exchange(rows, "wide", wides, step << bit) for step in range(1, values)]


def after(values, *others):
    return lax.optimization_barrier((tuple(values),) + others)[0]


def slot_of(distance, wides):
    slot = 0
    for bit, values in bit_groups(wides):
        slot = slot * values + ((distance >> bit) & (values - 1))
    return slot


def sum_blocks(blocks, wides):
    total = blocks
    for bit, values in bit_groups(wides):
        parts = total.astype(jnp.bfloat16).reshape((values, -1) + blocks.shape[1:])
        found = [
            exchange(parts[step], "wide", wides, step << bit).astype(jnp.float32)
            for step in range(1, values)
        ]
        total = sum(found, parts[0].astype(jnp.float32))
    return total


def body(
    frames,
    qkv_weight,
    out_weight,
    proj_weight,
    mlp_weight,
    logit_weight,
    history,
    hist_len,
    hist_mask,
    req_owner,
    req_local,
    labels,
):
    wides = lax.axis_size("wide")
    core, wide = lax.axis_index("section"), lax.axis_index("wide")
    cand_count = frames.shape[0]
    requests = req_local.shape[0]
    users, events, _ = history.shape
    keep, send, embedded, history = encode_block(
        core.reshape(1), frames, qkv_weight, out_weight, proj_weight, history
    )
    positions = jnp.arange(events, dtype=jnp.int32)[None, :]
    usable = (
        (positions < hist_len[:, None]) & ((hist_mask == 1) | (positions == 0))
    ).astype(jnp.float32)
    inv_count = lax.rsqrt(jnp.sum(usable, axis=1))
    usable = usable.reshape(users, 1, events)
    owner_core = req_owner[:, 0] // wides
    owner_slot = slot_of((req_owner[:, 0] % wides) ^ wide, wides)
    slots = ((owner_core ^ core) * wides + owner_slot) * cand_count + req_local
    pooled_slots = (owner_slot * 2 + owner_core) * cand_count + req_local
    stages = list(reversed(bit_groups(wides)))
    near = embedded
    for bit, values in stages:
        near = jnp.concatenate([near] + send_stage(near, wides, bit, values), axis=0)
        if bit == stages[0][0]:
            keep, send = after((keep, send), near)
    far = exchange(near, "section", 2, 1)
    far_slots = exchange(pooled_slots, "section", 2, 1)
    got = exchange(send, "section", 2, 1)
    pooled = jnp.where(
        core == 0, jnp.concatenate([keep, got], axis=0), jnp.concatenate([got, keep], axis=0)
    )
    found = send_stage(pooled, wides, *stages[0])
    queries, attended, slope = attend(
        inv_count, slots.reshape(requests, 1), near, far, history, usable
    )
    for stage in stages[1:]:
        pooled = jnp.concatenate(after([pooled] + found, attended), axis=0)
        found = send_stage(pooled, wides, *stage)
    logits, grad_att, direct = score(
        inv_count,
        queries,
        attended,
        labels.reshape(requests, 1),
        mlp_weight,
        logit_weight.reshape(1, -1),
    )
    half = users // 2
    grad_parts = [
        attend_back(0, half, grad_att, direct, slope, history),
        attend_back(half, users - half, grad_att, direct, slope, history),
    ]
    far_parts = [exchange(part, "section", 2, 1) for part in grad_parts]
    pooled = jnp.concatenate(after([pooled] + found, grad_parts[1]), axis=0)
    origins = [0] * wides
    for distance in range(wides):
        origins[slot_of(distance, wides)] = distance
    terms = chip_terms(
        origins,
        wide.reshape(1),
        jnp.concatenate([pooled_slots, far_slots]).reshape(1, 2 * requests),
        grad_parts + far_parts,
        pooled,
    )
    grad_proj = sum_blocks(terms, wides)
    return (logits.reshape(requests), grad_proj)


def solution(mesh):
    in_specs = (
        P(("section", "wide"), None, None),
        P(),
        P(),
        P(),
        P(),
        P(),
        P(("section", "wide"), None, None),
        P(("section", "wide")),
        P(("section", "wide"), None),
        P(("section", "wide"), None),
        P(("section", "wide")),
        P(("section", "wide")),
    )
    out_specs = (P(("section", "wide")), P(("section", "wide"), None))
    return jax.shard_map(body, mesh=mesh, in_specs=in_specs, out_specs=out_specs, check_vma=False)
```

```python
import functools
import math

import jax
import jax.numpy as jnp
from jax import lax
from jax.experimental import pallas as pl
from jax.experimental.pallas import tpu as pltpu
from jax.sharding import PartitionSpec as P

HEADS = 16
FRAMES = 3


EPSILON = 1e-06
MIB = 1024 * 1024


def layer_norm(values):
    center = values - jnp.mean(values, axis=-1, keepdims=True)
    spread = jnp.mean(jnp.square(center), axis=-1, keepdims=True)
    return center * lax.rsqrt(spread + EPSILON)


def dot(left, right):
    return jnp.dot(left, right, preferred_element_type=jnp.float32)


def dot_rows(left, right):
    return lax.dot_general(left, right, (((1,), (1,)), ((), ())), preferred_element_type=jnp.float32)


def dot_columns(left, right):
    return lax.dot_general(left, right, (((0,), (0,)), ((), ())), preferred_element_type=jnp.float32)


def split_rows(values):
    high = values.astype(jnp.bfloat16)
    low = (values - high.astype(jnp.float32)).astype(jnp.bfloat16)
    return jnp.concatenate([high, low], axis=0)


def dot_split(values, right):
    both = dot(split_rows(values), right)
    rows = values.shape[0]
    return both[:rows] + both[rows:]


def encode_kernel(
    tokens,
    core_ref,
    frames_hbm,
    qkv_hbm,
    out_hbm,
    proj_hbm,
    keep_ref,
    send_ref,
    embedded_ref,
    frames_ref,
    qkv_ref,
    out_ref,
    proj_ref,
    sems,
    normed_ref,
    packed_ref,
    scores_ref,
    mixed_rows_ref,
    sums_ref,
):
    total = embedded_ref.shape[0]
    rows, width = packed_ref.shape[0], packed_ref.shape[1] // 2
    cands = rows // tokens
    groups = total // cands
    head_dim = width // HEADS
    patches = tokens // FRAMES
    lanes = 2 * head_dim
    blocks = rows // lanes
    pairs = HEADS // 2
    quad = 4
    span = quad * head_dim

    def group_rows(group):
        return pl.ds(group * rows, rows)

    def columns(part):
        return pl.ds(part * width, width)

    pieces = [(frames_hbm.at[group_rows(0)], frames_ref.at[group_rows(0)])]
    pieces += [(qkv_hbm.at[:, columns(part)], qkv_ref.at[:, columns(part)]) for part in range(2)]
    pieces += [
        (frames_hbm.at[group_rows(group)], frames_ref.at[group_rows(group)])
        for group in range(1, groups)
    ]
    pieces += [(qkv_hbm.at[:, columns(2)], qkv_ref.at[:, columns(2)])]
    pieces += [(out_hbm, out_ref), (proj_hbm, proj_ref)]
    copies = [
        pltpu.make_async_copy(source, target, sems.at[place])
        for place, (source, target) in enumerate(pieces)
    ]
    for copy in copies:
        copy.start()

    def norm_cand(cand):
        at = slice(cand * tokens, (cand + 1) * tokens)
        inputs = frames_ref[at, :].astype(jnp.float32)
        normed_ref[at, :] = layer_norm(inputs).astype(jnp.bfloat16)
        sums_ref[cand] = jnp.sum(inputs, axis=0, keepdims=True)

    exponent = math.log2(math.e) / math.sqrt(head_dim)
    frame_at = (lax.broadcasted_iota(jnp.int32, (patches, quad * lanes), 1) % lanes) // patches
    nothing = jnp.zeros((head_dim, lanes), jnp.bfloat16)
    ones_row = lax.broadcasted_iota(jnp.int32, (2 * lanes, 2 * lanes), 0) // patches
    ones_column = lax.broadcasted_iota(jnp.int32, (2 * lanes, 2 * lanes), 1) // patches
    frame_ones = (ones_row == ones_column).astype(jnp.bfloat16)
    own = lax.broadcasted_iota(jnp.int32, (cands, rows), 1) // tokens == lax.broadcasted_iota(
        jnp.int32, (cands, rows), 0
    )

    def own_scores(block, head):
        block_rows = slice(block * lanes, (block + 1) * lanes)
        start = head * head_dim
        query = packed_ref[block_rows, start : start + span]
        keys = packed_ref[block_rows, width + start : width + start + span].T
        keys = jnp.concatenate(
            [
                jnp.concatenate(
                    [nothing] * place
                    + [keys[place * head_dim : (place + 1) * head_dim]]
                    + [nothing] * (quad - 1 - place),
                    axis=1,
                )
                for place in range(quad)
            ],
            axis=0,
        )
        scores = dot(query, keys)
        found = scores[:patches]
        for frame in range(1, lanes // patches):
            found = jnp.where(
                frame_at == frame, scores[frame * patches : (frame + 1) * patches], found
            )
        for side in range(quad // 2):
            scores_ref[block, head // 2 + side] = found[
                :, side * 2 * lanes : (side + 1) * 2 * lanes
            ]

    copies[0].wait()
    for cand in range(cands):
        norm_cand(cand)
    copies[1].wait()
    copies[2].wait()
    for group in range(groups):
        at = slice(group * rows, (group + 1) * rows)
        for part in range(2):
            part_columns = slice(part * width, (part + 1) * width)
            packed_ref[:, part_columns] = dot(normed_ref[at, :], qkv_ref[:, part_columns]).astype(
                jnp.bfloat16
            )
        if group + 1 < groups:
            copies[3 + group].wait()
        for head in range(0, HEADS, quad):
            for block in range(blocks):
                own_scores(block, head)
            if group + 1 < groups:
                for cand in range(head * cands // HEADS, (head + quad) * cands // HEADS):
                    norm_cand((group + 1) * cands + cand)
        exp_scores = jnp.exp2(
            scores_ref[...].reshape(blocks * pairs * patches, 2 * lanes) * exponent
        )
        totals = dot(exp_scores.astype(jnp.bfloat16), frame_ones)
        probs = (exp_scores / totals).reshape(blocks * pairs, patches, 2 * lanes)
        sums = jnp.sum(probs, axis=1)
        key_sums = [
            jnp.concatenate(
                [
                    sums[block * pairs : (block + 1) * pairs, side * lanes : (side + 1) * lanes]
                    for block in range(blocks)
                ],
                axis=1,
            )
            for side in range(2)
        ]
        spread = jnp.concatenate(
            [
                jnp.where(own, key_sums[head % 2][head // 2 : head // 2 + 1], 0.0)
                for head in range(HEADS)
            ],
            axis=0,
        ).astype(jnp.bfloat16)
        mixed_rows = dot(spread, normed_ref[at, :])
        for head in range(HEADS):
            mixed_rows_ref[head, group * cands : (group + 1) * cands, :] = mixed_rows[
                head * cands : (head + 1) * cands
            ]

    for copy in copies[2 + groups :]:
        copy.wait()
    mixed = []
    for head in range(0, HEADS, quad):
        left = mixed_rows_ref[head : head + quad].reshape(quad * total, width)
        start = 2 * width + head * head_dim
        both = dot_split(left, qkv_ref[:, start : start + span])
        head_at = lax.broadcasted_iota(jnp.int32, (total, span), 1) // head_dim
        piece = jnp.zeros((total, span), jnp.float32)
        for place in range(quad):
            piece = jnp.where(head_at == place, both[place * total : (place + 1) * total], piece)
        mixed.append(piece)
    mixed_mean = jnp.concatenate(mixed, axis=1) * (1.0 / tokens)
    hidden = sums_ref[...].reshape(total, width) * (1.0 / tokens)
    hidden += dot_split(mixed_mean, out_ref[...])
    pooled = layer_norm(hidden).astype(jnp.bfloat16)
    first, second = pooled[:, : width // 2], pooled[:, width // 2 :]
    keep_ref[...] = jnp.where(core_ref[0] == 0, first, second)
    send_ref[...] = jnp.where(core_ref[0] == 0, second, first)
    embedded_ref[...] = dot(pooled, proj_ref[...]).astype(jnp.bfloat16)


def in_hbm(*arrays):
    return [pltpu.with_memory_space_constraint(array, pltpu.HBM) for array in arrays]


def encode_block(core, frames, qkv_weight, out_weight, proj_weight):
    cand_count, tokens, width = frames.shape
    key_width = proj_weight.shape[1]
    groups = 2
    rows = cand_count * tokens // groups
    lanes = 2 * width // HEADS
    patches = tokens // FRAMES
    flat = frames.reshape(cand_count * tokens, width)
    whole = pl.BlockSpec(memory_space=pltpu.VMEM)
    return pl.pallas_call(
        functools.partial(encode_kernel, tokens),
        in_specs=[pl.BlockSpec(memory_space=pltpu.SMEM)]
        + [pl.BlockSpec(memory_space=pltpu.HBM)] * 4,
        out_specs=[whole] * 3,
        out_shape=[
            jax.ShapeDtypeStruct((cand_count, width // 2), jnp.bfloat16),
            jax.ShapeDtypeStruct((cand_count, width // 2), jnp.bfloat16),
            jax.ShapeDtypeStruct((cand_count, key_width), jnp.bfloat16),
        ],
        scratch_shapes=[
            pltpu.VMEM(flat.shape, jnp.bfloat16),
            pltpu.VMEM(qkv_weight.shape, jnp.bfloat16),
            pltpu.VMEM(out_weight.shape, jnp.bfloat16),
            pltpu.VMEM(proj_weight.shape, jnp.bfloat16),
            pltpu.SemaphoreType.DMA((groups + 5,)),
            pltpu.VMEM(flat.shape, jnp.bfloat16),
            pltpu.VMEM((rows, 2 * width), jnp.bfloat16),
            pltpu.VMEM((rows // lanes, HEADS // 2, patches, 2 * lanes), jnp.float32),
            pltpu.VMEM((HEADS, cand_count, width), jnp.float32),
            pltpu.VMEM((cand_count, 1, width), jnp.float32),
        ],
        compiler_params=pltpu.CompilerParams(vmem_limit_bytes=44 * MIB),
        cost_estimate=pl.CostEstimate(
            flops=5 * cand_count * tokens * width * width, bytes_accessed=1 << 24, transcendentals=0
        ),
        name="encode",
    )(core, *in_hbm(flat, qkv_weight, out_weight, proj_weight))


def attend_kernel(
    inv_ref,
    slots_ref,
    near_ref,
    far_ref,
    usable_ref,
    history_hbm,
    queries_ref,
    attended_ref,
    slope_ref,
    history_ref,
    sems,
):
    users, events, _ = history_ref.shape
    chunk = math.gcd(events, 1024)
    copies = [
        [
            pltpu.make_async_copy(
                history_hbm.at[user, pl.ds(at, chunk)],
                history_ref.at[user, pl.ds(at, chunk)],
                sems.at[user, at // chunk],
            )
            for at in range(0, events, chunk)
        ]
        for user in range(users)
    ]
    for user_copies in copies:
        for copy in user_copies:
            copy.start()
    slots = slots_ref[...]
    half, key_width = near_ref.shape
    places = lax.broadcasted_iota(jnp.int32, (slots.shape[0], half), 1)
    queries = dot((slots == places).astype(jnp.bfloat16), near_ref[...])
    queries += dot((slots == places + half).astype(jnp.bfloat16), far_ref[...])
    queries_ref[...] = queries.astype(jnp.bfloat16)
    per_user = slots.shape[0] // users
    for user in range(users):
        rows = slice(user * per_user, (user + 1) * per_user)
        attended = jnp.zeros((per_user, key_width), jnp.float32)
        for at in range(0, events, chunk):
            copies[user][at // chunk].wait()
            keys = history_ref[user, at : at + chunk, :]
            usable = usable_ref[user, :, at : at + chunk]
            scores = dot_rows(queries_ref[rows, :], keys)
            half_gate = 0.5 * jnp.tanh(scores * (0.5 / math.sqrt(key_width)))
            weights = (0.5 + half_gate) * usable
            slope_ref[rows, at : at + chunk] = (weights * (0.5 - half_gate)).astype(jnp.bfloat16)
            attended += dot(weights.astype(jnp.bfloat16), keys)
        attended_ref[rows, :] = attended * inv_ref[user]


def attend(inv_count, slots, near, far, history, usable):
    users, events, key_width = history.shape
    requests = slots.shape[0]
    whole = pl.BlockSpec(memory_space=pltpu.VMEM)
    return pl.pallas_call(
        attend_kernel,
        in_specs=[pl.BlockSpec(memory_space=pltpu.SMEM)]
        + [whole] * 4
        + [pl.BlockSpec(memory_space=pltpu.HBM)],
        out_specs=[whole] * 3,
        out_shape=[
            jax.ShapeDtypeStruct((requests, key_width), jnp.bfloat16),
            jax.ShapeDtypeStruct((requests, key_width), jnp.float32),
            jax.ShapeDtypeStruct((requests, events), jnp.bfloat16),
        ],
        scratch_shapes=[
            pltpu.VMEM(history.shape, history.dtype),
            pltpu.SemaphoreType.DMA((users, events // math.gcd(events, 1024))),
        ],
        compiler_params=pltpu.CompilerParams(vmem_limit_bytes=32 * MIB),
        cost_estimate=pl.CostEstimate(
            flops=4 * requests * events * key_width, bytes_accessed=1 << 24, transcendentals=0
        ),
        name="attend",
    )(inv_count, slots, near, far, usable, *in_hbm(history))


def score_kernel(
    inv_ref,
    queries_ref,
    attended_ref,
    labels_ref,
    mlp_ref,
    logit_weight_ref,
    logits_ref,
    grad_att_ref,
    direct_ref,
):
    users = inv_ref.shape[0]
    per_user = queries_ref.shape[0] // users
    step_users = math.gcd(users, 2)
    step_rows = step_users * per_user
    weight = logit_weight_ref[...].astype(jnp.float32)
    for first in range(0, users, step_users):
        at = slice(first * per_user, first * per_user + step_rows)
        query_b = queries_ref[at, :]
        query_f = query_b.astype(jnp.float32)
        attended = attended_ref[at, :]
        key_width = query_f.shape[1]
        joined = jnp.concatenate(
            [query_b, attended.astype(jnp.bfloat16), (query_f * attended).astype(jnp.bfloat16)],
            axis=1,
        )
        pre_act = dot(joined, mlp_ref[...])
        act_sig = 0.5 * jnp.tanh(0.5 * pre_act) + 0.5
        hidden_units = (pre_act * act_sig).astype(jnp.bfloat16)
        logits = jnp.sum(hidden_units.astype(jnp.float32) * weight, axis=1, keepdims=True)
        logits_ref[at, :] = logits
        dlogit = (0.5 * jnp.tanh(0.5 * logits) + 0.5) - labels_ref[at, :].astype(jnp.float32)
        slope = act_sig * (1.0 + pre_act * (1.0 - act_sig))
        grad_pre = (dlogit * weight * slope).astype(jnp.bfloat16)
        djoined = dot_rows(grad_pre, mlp_ref[...])
        part_query = djoined[:, :key_width]
        part_att = djoined[:, key_width : 2 * key_width]
        part_prod = djoined[:, 2 * key_width :]
        grad_att = part_att + part_prod * query_f
        for user in range(step_users):
            grad_att_ref[pl.ds((first + user) * per_user, per_user), :] = (
                grad_att[user * per_user : (user + 1) * per_user] * inv_ref[first + user]
            ).astype(jnp.bfloat16)
        direct_ref[at, :] = part_query + part_prod * attended


def score(inv_count, queries, attended, labels, mlp_weight, logit_weight):
    requests, key_width = queries.shape
    whole = pl.BlockSpec(memory_space=pltpu.VMEM)
    return pl.pallas_call(
        score_kernel,
        in_specs=[pl.BlockSpec(memory_space=pltpu.SMEM)] + [whole] * 5,
        out_specs=[whole] * 3,
        out_shape=[
            jax.ShapeDtypeStruct((requests, 1), jnp.float32),
            jax.ShapeDtypeStruct((requests, key_width), jnp.bfloat16),
            jax.ShapeDtypeStruct((requests, key_width), jnp.float32),
        ],
        compiler_params=pltpu.CompilerParams(vmem_limit_bytes=32 * MIB),
        cost_estimate=pl.CostEstimate(
            flops=4 * requests * mlp_weight.shape[0] * mlp_weight.shape[1],
            bytes_accessed=1 << 23,
            transcendentals=0,
        ),
        name="score",
    )(inv_count, queries, attended, labels, mlp_weight, logit_weight)


def attend_back_kernel(first, grad_att_ref, direct_ref, slope_ref, history_ref, grad_rows_ref):
    users, events, key_width = history_ref.shape
    per_user = grad_att_ref.shape[0] // users
    chunk = math.gcd(events, 1024)
    for user in range(grad_rows_ref.shape[0] // per_user):
        rows = slice((first + user) * per_user, (first + user + 1) * per_user)
        back = jnp.zeros((per_user, key_width), jnp.float32)
        for at in range(0, events, chunk):
            keys = history_ref[first + user, at : at + chunk, :]
            slope = slope_ref[rows, at : at + chunk].astype(jnp.float32)
            grad_sig = (dot_rows(grad_att_ref[rows, :], keys) * slope).astype(jnp.bfloat16)
            back += dot(grad_sig, keys)
        grad_rows = direct_ref[rows, :] + back * (1.0 / math.sqrt(key_width))
        grad_rows_ref[user * per_user : (user + 1) * per_user, :] = grad_rows.astype(jnp.bfloat16)


def attend_back(first, count, grad_att, direct, slope, history):
    users, events, key_width = history.shape
    per_user = grad_att.shape[0] // users
    whole = pl.BlockSpec(memory_space=pltpu.VMEM)
    return pl.pallas_call(
        functools.partial(attend_back_kernel, first),
        in_specs=[whole] * 4,
        out_specs=whole,
        out_shape=jax.ShapeDtypeStruct((count * per_user, key_width), jnp.bfloat16),
        compiler_params=pltpu.CompilerParams(vmem_limit_bytes=20 * MIB),
        cost_estimate=pl.CostEstimate(
            flops=4 * count * per_user * events * key_width,
            bytes_accessed=1 << 23,
            transcendentals=0,
        ),
        name="attend_back",
    )(grad_att, direct, slope, history)


def terms_kernel(origins, wide_ref, slots_ref, *refs):
    grad_refs = refs[:-4]
    pooled_ref, out_ref, grad_rows_ref, terms_ref = refs[-4:]
    at = 0
    for grad_ref in grad_refs:
        grad_rows_ref[at : at + grad_ref.shape[0], :] = grad_ref[...]
        at += grad_ref.shape[0]
    cands = pooled_ref.shape[0]
    requests = slots_ref.shape[1]
    chunk = math.gcd(cands, 512)
    for at in range(0, cands, chunk):
        places = lax.broadcasted_iota(jnp.int32, (chunk, requests), 0) + at
        row_hot = (places == slots_ref[...]).astype(jnp.bfloat16)
        cand_grad = dot(row_hot, grad_rows_ref[...]).astype(jnp.bfloat16)
        term = dot_columns(pooled_ref[at : at + chunk, :], cand_grad)
        if at == 0:
            terms_ref[...] = term
        else:
            terms_ref[...] += term
    rows = terms_ref.shape[0] // len(origins)
    wide = wide_ref[0]
    batch = max(1, 32 // rows)
    for slot in range(0, len(origins), batch):
        found = [
            terms_ref[pl.ds(pl.multiple_of((wide ^ origins[slot + i]) * rows, rows), rows), :]
            for i in range(batch)
        ]
        found = found[0] if batch == 1 else jnp.concatenate(found, axis=0)
        out_ref[slot * rows : (slot + batch) * rows, :] = found.astype(jnp.bfloat16)


def chip_terms(origins, wide, slots, grad_parts, pooled):
    cands, width = pooled.shape
    requests = slots.shape[1]
    key_width = grad_parts[0].shape[1]
    whole = pl.BlockSpec(memory_space=pltpu.VMEM)
    return pl.pallas_call(
        functools.partial(terms_kernel, origins),
        in_specs=[pl.BlockSpec(memory_space=pltpu.SMEM)] + [whole] * (len(grad_parts) + 2),
        out_specs=whole,
        out_shape=jax.ShapeDtypeStruct((width, key_width), jnp.bfloat16),
        scratch_shapes=[
            pltpu.VMEM((requests, key_width), jnp.bfloat16),
            pltpu.VMEM((width, key_width), jnp.float32),
        ],
        compiler_params=pltpu.CompilerParams(vmem_limit_bytes=20 * MIB),
        cost_estimate=pl.CostEstimate(
            flops=2 * cands * key_width * (width + requests),
            bytes_accessed=1 << 22,
            transcendentals=0,
        ),
        name="chip_terms",
    )(wide, slots, *grad_parts, pooled)


def bit_groups(size):
    groups = []
    bit = 0
    while (1 << bit) < size:
        values = min(4, size >> bit)
        groups.append((bit, values))
        bit += values.bit_length() - 1
    return groups


def exchange(values, axis_name, size, distance):
    return lax.ppermute(values, axis_name, [(i, i ^ distance) for i in range(size)])


def send_stage(rows, wides, bit, values):
    return [exchange(rows, "wide", wides, step << bit) for step in range(1, values)]


def after(values, *others):
    return lax.optimization_barrier((tuple(values),) + others)[0]


def slot_of(distance, wides):
    slot = 0
    for bit, values in bit_groups(wides):
        slot = slot * values + ((distance >> bit) & (values - 1))
    return slot


def sum_blocks(blocks, wides, logits):
    total = blocks
    for bit, values in bit_groups(wides):
        if bit > 0:
            total, logits = lax.optimization_barrier((total, logits))
        parts = total.astype(jnp.bfloat16).reshape((values, -1) + blocks.shape[1:])
        found = [
            exchange(parts[step], "wide", wides, step << bit).astype(jnp.float32)
            for step in range(1, values)
        ]
        total = sum(found, parts[0].astype(jnp.float32))
    return total, logits


def body(
    frames,
    qkv_weight,
    out_weight,
    proj_weight,
    mlp_weight,
    logit_weight,
    history,
    hist_len,
    hist_mask,
    req_owner,
    req_local,
    labels,
):
    wides = lax.axis_size("wide")
    core, wide = lax.axis_index("section"), lax.axis_index("wide")
    cand_count = frames.shape[0]
    requests = req_local.shape[0]
    users, events, _ = history.shape
    keep, send, embedded = encode_block(
        core.reshape(1), frames, qkv_weight, out_weight, proj_weight
    )
    positions = jnp.arange(events, dtype=jnp.int32)[None, :]
    usable = (
        (positions < hist_len[:, None]) & ((hist_mask == 1) | (positions == 0))
    ).astype(jnp.float32)
    inv_count = lax.rsqrt(jnp.sum(usable, axis=1))
    usable = usable.reshape(users, 1, events)
    owner_core = req_owner[:, 0] // wides
    owner_slot = slot_of((req_owner[:, 0] % wides) ^ wide, wides)
    slots = ((owner_core ^ core) * wides + owner_slot) * cand_count + req_local
    pooled_slots = (owner_slot * 2 + owner_core) * cand_count + req_local
    stages = list(reversed(bit_groups(wides)))
    near = embedded
    for bit, values in stages:
        near = jnp.concatenate([near] + send_stage(near, wides, bit, values), axis=0)
        if bit == stages[0][0]:
            keep, send = after((keep, send), near)
    far = exchange(near, "section", 2, 1)
    far_slots = exchange(pooled_slots, "section", 2, 1)
    got = exchange(send, "section", 2, 1)
    pooled = jnp.where(
        core == 0, jnp.concatenate([keep, got], axis=0), jnp.concatenate([got, keep], axis=0)
    )
    found = send_stage(pooled, wides, *stages[0])
    queries, attended, slope = attend(
        inv_count, slots.reshape(requests, 1), near, far, history, usable
    )
    for stage in stages[1:]:
        pooled = jnp.concatenate(after([pooled] + found, attended), axis=0)
        found = send_stage(pooled, wides, *stage)
    logits, grad_att, direct = score(
        inv_count,
        queries,
        attended,
        labels.reshape(requests, 1),
        mlp_weight,
        logit_weight.reshape(1, -1),
    )
    half = users // 2
    grad_parts = [
        attend_back(0, half, grad_att, direct, slope, history),
        attend_back(half, users - half, grad_att, direct, slope, history),
    ]
    far_parts = [exchange(part, "section", 2, 1) for part in grad_parts]
    pooled = jnp.concatenate(after([pooled] + found, grad_parts[1]), axis=0)
    origins = [0] * wides
    for distance in range(wides):
        origins[slot_of(distance, wides)] = distance
    terms = chip_terms(
        origins,
        wide.reshape(1),
        jnp.concatenate([pooled_slots, far_slots]).reshape(1, 2 * requests),
        grad_parts + far_parts,
        pooled,
    )
    grad_proj, logits = sum_blocks(terms, wides, logits.reshape(requests))
    return (logits, grad_proj)


def solution(mesh):
    in_specs = (
        P(("section", "wide"), None, None),
        P(),
        P(),
        P(),
        P(),
        P(),
        P(("section", "wide"), None, None),
        P(("section", "wide")),
        P(("section", "wide"), None),
        P(("section", "wide"), None),
        P(("section", "wide")),
        P(("section", "wide")),
    )
    out_specs = (P(("section", "wide")), P(("section", "wide"), None))
    return jax.shard_map(body, mesh=mesh, in_specs=in_specs, out_specs=out_specs, check_vma=False)
```

```python
import functools
import math

import jax
import jax.numpy as jnp
from jax import lax
from jax.experimental import pallas as pl
from jax.experimental.pallas import tpu as pltpu
from jax.sharding import PartitionSpec as P

HEADS = 16
FRAMES = 3


EPSILON = 1e-06
MIB = 1024 * 1024


def layer_norm(values):
    center = values - jnp.mean(values, axis=-1, keepdims=True)
    spread = jnp.mean(jnp.square(center), axis=-1, keepdims=True)
    return center * lax.rsqrt(spread + EPSILON)


def dot(left, right):
    return jnp.dot(left, right, preferred_element_type=jnp.float32)


def dot_rows(left, right):
    return lax.dot_general(left, right, (((1,), (1,)), ((), ())), preferred_element_type=jnp.float32)


def dot_columns(left, right):
    return lax.dot_general(left, right, (((0,), (0,)), ((), ())), preferred_element_type=jnp.float32)


def split_rows(values):
    high = values.astype(jnp.bfloat16)
    low = (values - high.astype(jnp.float32)).astype(jnp.bfloat16)
    return jnp.concatenate([high, low], axis=0)


def dot_split(values, right):
    both = dot(split_rows(values), right)
    rows = values.shape[0]
    return both[:rows] + both[rows:]


def encode_kernel(
    tokens,
    core_ref,
    frames_hbm,
    qkv_hbm,
    out_hbm,
    proj_hbm,
    keep_ref,
    send_ref,
    embedded_ref,
    frames_ref,
    qkv_ref,
    out_ref,
    proj_ref,
    sems,
    normed_ref,
    packed_ref,
    scores_ref,
    mixed_rows_ref,
    sums_ref,
):
    total = embedded_ref.shape[0]
    rows, width = packed_ref.shape[0], packed_ref.shape[1] // 2
    cands = rows // tokens
    groups = total // cands
    head_dim = width // HEADS
    patches = tokens // FRAMES
    lanes = 2 * head_dim
    blocks = rows // lanes
    pairs = HEADS // 2
    quad = 4
    span = quad * head_dim

    def group_rows(group):
        return pl.ds(group * rows, rows)

    def columns(part):
        return pl.ds(part * width, width)

    pieces = [(frames_hbm.at[group_rows(0)], frames_ref.at[group_rows(0)])]
    pieces += [(qkv_hbm.at[:, columns(part)], qkv_ref.at[:, columns(part)]) for part in range(2)]
    pieces += [
        (frames_hbm.at[group_rows(group)], frames_ref.at[group_rows(group)])
        for group in range(1, groups)
    ]
    pieces += [(qkv_hbm.at[:, columns(2)], qkv_ref.at[:, columns(2)])]
    pieces += [(out_hbm, out_ref), (proj_hbm, proj_ref)]
    copies = [
        pltpu.make_async_copy(source, target, sems.at[place])
        for place, (source, target) in enumerate(pieces)
    ]
    for copy in copies:
        copy.start()

    def norm_cand(cand):
        at = slice(cand * tokens, (cand + 1) * tokens)
        inputs = frames_ref[at, :].astype(jnp.float32)
        normed_ref[at, :] = layer_norm(inputs).astype(jnp.bfloat16)
        sums_ref[cand] = jnp.sum(inputs, axis=0, keepdims=True)

    exponent = math.log2(math.e) / math.sqrt(head_dim)
    frame_at = (lax.broadcasted_iota(jnp.int32, (patches, quad * lanes), 1) % lanes) // patches
    nothing = jnp.zeros((head_dim, lanes), jnp.bfloat16)
    ones_row = lax.broadcasted_iota(jnp.int32, (2 * lanes, 2 * lanes), 0) // patches
    ones_column = lax.broadcasted_iota(jnp.int32, (2 * lanes, 2 * lanes), 1) // patches
    frame_ones = (ones_row == ones_column).astype(jnp.bfloat16)
    own = lax.broadcasted_iota(jnp.int32, (cands, rows), 1) // tokens == lax.broadcasted_iota(
        jnp.int32, (cands, rows), 0
    )

    def own_scores(block, head):
        block_rows = slice(block * lanes, (block + 1) * lanes)
        start = head * head_dim
        query = packed_ref[block_rows, start : start + span]
        keys = packed_ref[block_rows, width + start : width + start + span].T
        keys = jnp.concatenate(
            [
                jnp.concatenate(
                    [nothing] * place
                    + [keys[place * head_dim : (place + 1) * head_dim]]
                    + [nothing] * (quad - 1 - place),
                    axis=1,
                )
                for place in range(quad)
            ],
            axis=0,
        )
        scores = dot(query, keys)
        found = scores[:patches]
        for frame in range(1, lanes // patches):
            found = jnp.where(
                frame_at == frame, scores[frame * patches : (frame + 1) * patches], found
            )
        for side in range(quad // 2):
            scores_ref[block, head // 2 + side] = found[
                :, side * 2 * lanes : (side + 1) * 2 * lanes
            ]

    copies[0].wait()
    for cand in range(cands):
        norm_cand(cand)
    copies[1].wait()
    copies[2].wait()
    for group in range(groups):
        at = slice(group * rows, (group + 1) * rows)
        for part in range(2):
            part_columns = slice(part * width, (part + 1) * width)
            packed_ref[:, part_columns] = dot(normed_ref[at, :], qkv_ref[:, part_columns]).astype(
                jnp.bfloat16
            )
        if group + 1 < groups:
            copies[3 + group].wait()
        for head in range(0, HEADS, quad):
            for block in range(blocks):
                own_scores(block, head)
            if group + 1 < groups:
                for cand in range(head * cands // HEADS, (head + quad) * cands // HEADS):
                    norm_cand((group + 1) * cands + cand)
        exp_scores = jnp.exp2(
            scores_ref[...].reshape(blocks * pairs * patches, 2 * lanes) * exponent
        )
        totals = dot(exp_scores.astype(jnp.bfloat16), frame_ones)
        probs = (exp_scores / totals).reshape(blocks * pairs, patches, 2 * lanes)
        sums = jnp.sum(probs, axis=1)
        key_sums = [
            jnp.concatenate(
                [
                    sums[block * pairs : (block + 1) * pairs, side * lanes : (side + 1) * lanes]
                    for block in range(blocks)
                ],
                axis=1,
            )
            for side in range(2)
        ]
        spread = jnp.concatenate(
            [
                jnp.where(own, key_sums[head % 2][head // 2 : head // 2 + 1], 0.0)
                for head in range(HEADS)
            ],
            axis=0,
        ).astype(jnp.bfloat16)
        mixed_rows = dot(spread, normed_ref[at, :])
        for head in range(HEADS):
            mixed_rows_ref[head, group * cands : (group + 1) * cands, :] = mixed_rows[
                head * cands : (head + 1) * cands
            ]

    for copy in copies[2 + groups :]:
        copy.wait()
    mixed = []
    for head in range(0, HEADS, quad):
        left = mixed_rows_ref[head : head + quad].reshape(quad * total, width)
        start = 2 * width + head * head_dim
        both = dot_split(left, qkv_ref[:, start : start + span])
        head_at = lax.broadcasted_iota(jnp.int32, (total, span), 1) // head_dim
        piece = jnp.zeros((total, span), jnp.float32)
        for place in range(quad):
            piece = jnp.where(head_at == place, both[place * total : (place + 1) * total], piece)
        mixed.append(piece)
    mixed_mean = jnp.concatenate(mixed, axis=1) * (1.0 / tokens)
    hidden = sums_ref[...].reshape(total, width) * (1.0 / tokens)
    hidden += dot_split(mixed_mean, out_ref[...])
    pooled = layer_norm(hidden).astype(jnp.bfloat16)
    first, second = pooled[:, : width // 2], pooled[:, width // 2 :]
    keep_ref[...] = jnp.where(core_ref[0] == 0, first, second)
    send_ref[...] = jnp.where(core_ref[0] == 0, second, first)
    embedded_ref[...] = dot(pooled, proj_ref[...]).astype(jnp.bfloat16)


def in_hbm(*arrays):
    return [pltpu.with_memory_space_constraint(array, pltpu.HBM) for array in arrays]


def encode_block(core, frames, qkv_weight, out_weight, proj_weight):
    cand_count, tokens, width = frames.shape
    key_width = proj_weight.shape[1]
    groups = 2
    rows = cand_count * tokens // groups
    lanes = 2 * width // HEADS
    patches = tokens // FRAMES
    flat = frames.reshape(cand_count * tokens, width)
    whole = pl.BlockSpec(memory_space=pltpu.VMEM)
    return pl.pallas_call(
        functools.partial(encode_kernel, tokens),
        in_specs=[pl.BlockSpec(memory_space=pltpu.SMEM)]
        + [pl.BlockSpec(memory_space=pltpu.HBM)] * 4,
        out_specs=[whole] * 3,
        out_shape=[
            jax.ShapeDtypeStruct((cand_count, width // 2), jnp.bfloat16),
            jax.ShapeDtypeStruct((cand_count, width // 2), jnp.bfloat16),
            jax.ShapeDtypeStruct((cand_count, key_width), jnp.bfloat16),
        ],
        scratch_shapes=[
            pltpu.VMEM(flat.shape, jnp.bfloat16),
            pltpu.VMEM(qkv_weight.shape, jnp.bfloat16),
            pltpu.VMEM(out_weight.shape, jnp.bfloat16),
            pltpu.VMEM(proj_weight.shape, jnp.bfloat16),
            pltpu.SemaphoreType.DMA((groups + 5,)),
            pltpu.VMEM(flat.shape, jnp.bfloat16),
            pltpu.VMEM((rows, 2 * width), jnp.bfloat16),
            pltpu.VMEM((rows // lanes, HEADS // 2, patches, 2 * lanes), jnp.float32),
            pltpu.VMEM((HEADS, cand_count, width), jnp.float32),
            pltpu.VMEM((cand_count, 1, width), jnp.float32),
        ],
        compiler_params=pltpu.CompilerParams(vmem_limit_bytes=44 * MIB),
        cost_estimate=pl.CostEstimate(
            flops=5 * cand_count * tokens * width * width, bytes_accessed=1 << 24, transcendentals=0
        ),
        name="encode",
    )(core, *in_hbm(flat, qkv_weight, out_weight, proj_weight))


def attend_kernel(
    inv_ref,
    slots_ref,
    near_ref,
    far_ref,
    usable_ref,
    history_hbm,
    queries_ref,
    attended_ref,
    slope_ref,
    history_ref,
    sems,
):
    users, events, _ = history_ref.shape
    chunk = math.gcd(events, 1024)
    half_users = max(1, users // 2)
    copies = [
        pltpu.make_async_copy(
            history_hbm.at[pl.ds(user, half_users)],
            history_ref.at[pl.ds(user, half_users)],
            sems.at[user],
        )
        for user in range(0, users, half_users)
    ]
    for copy in copies:
        copy.start()
    slots = slots_ref[...]
    half, key_width = near_ref.shape
    places = lax.broadcasted_iota(jnp.int32, (slots.shape[0], half), 1)
    queries = dot((slots == places).astype(jnp.bfloat16), near_ref[...])
    queries += dot((slots == places + half).astype(jnp.bfloat16), far_ref[...])
    queries_ref[...] = queries.astype(jnp.bfloat16)
    per_user = slots.shape[0] // users
    for user in range(users):
        if user % half_users == 0:
            copies[user // half_users].wait()
        rows = slice(user * per_user, (user + 1) * per_user)
        attended = jnp.zeros((per_user, key_width), jnp.float32)
        for at in range(0, events, chunk):
            keys = history_ref[user, at : at + chunk, :]
            usable = usable_ref[user, :, at : at + chunk]
            scores = dot_rows(queries_ref[rows, :], keys)
            half_gate = 0.5 * jnp.tanh(scores * (0.5 / math.sqrt(key_width)))
            weights = (0.5 + half_gate) * usable
            slope_ref[rows, at : at + chunk] = (weights * (0.5 - half_gate)).astype(jnp.bfloat16)
            attended += dot(weights.astype(jnp.bfloat16), keys)
        attended_ref[rows, :] = attended * inv_ref[user]


def attend(inv_count, slots, near, far, history, usable):
    users, events, key_width = history.shape
    requests = slots.shape[0]
    whole = pl.BlockSpec(memory_space=pltpu.VMEM)
    return pl.pallas_call(
        attend_kernel,
        in_specs=[pl.BlockSpec(memory_space=pltpu.SMEM)]
        + [whole] * 4
        + [pl.BlockSpec(memory_space=pltpu.HBM)],
        out_specs=[whole] * 3,
        out_shape=[
            jax.ShapeDtypeStruct((requests, key_width), jnp.bfloat16),
            jax.ShapeDtypeStruct((requests, key_width), jnp.float32),
            jax.ShapeDtypeStruct((requests, events), jnp.bfloat16),
        ],
        scratch_shapes=[
            pltpu.VMEM(history.shape, history.dtype),
            pltpu.SemaphoreType.DMA((users,)),
        ],
        compiler_params=pltpu.CompilerParams(vmem_limit_bytes=32 * MIB),
        cost_estimate=pl.CostEstimate(
            flops=4 * requests * events * key_width, bytes_accessed=1 << 24, transcendentals=0
        ),
        name="attend",
    )(inv_count, slots, near, far, usable, *in_hbm(history))


def score_kernel(
    inv_ref,
    queries_ref,
    attended_ref,
    labels_ref,
    mlp_ref,
    logit_weight_ref,
    logits_ref,
    grad_att_ref,
    direct_ref,
    grad_pre_ref,
):
    users = inv_ref.shape[0]
    per_user = queries_ref.shape[0] // users
    step_users = math.gcd(users, 2)
    step_rows = step_users * per_user
    key_width = queries_ref.shape[1]
    weight = logit_weight_ref[...].astype(jnp.float32)
    for first in range(0, users, step_users):
        at = slice(first * per_user, first * per_user + step_rows)
        query_b = queries_ref[at, :]
        query_f = query_b.astype(jnp.float32)
        attended = attended_ref[at, :]
        joined = jnp.concatenate(
            [query_b, attended.astype(jnp.bfloat16), (query_f * attended).astype(jnp.bfloat16)],
            axis=1,
        )
        pre_act = dot(joined, mlp_ref[...])
        act_sig = 0.5 * jnp.tanh(0.5 * pre_act) + 0.5
        hidden_units = (pre_act * act_sig).astype(jnp.bfloat16)
        logits = jnp.sum(hidden_units.astype(jnp.float32) * weight, axis=1, keepdims=True)
        logits_ref[at, :] = logits
        dlogit = (0.5 * jnp.tanh(0.5 * logits) + 0.5) - labels_ref[at, :].astype(jnp.float32)
        slope = act_sig * (1.0 + pre_act * (1.0 - act_sig))
        grad_pre = (dlogit * weight * slope).astype(jnp.bfloat16)
        grad_pre_ref[at, :] = grad_pre
    djoined = dot_rows(grad_pre_ref[...], mlp_ref[...])
    part_att = djoined[:, key_width : 2 * key_width]
    part_prod = djoined[:, 2 * key_width :]
    for user in range(users):
        at = slice(user * per_user, (user + 1) * per_user)
        grad_att = part_att[at] + part_prod[at] * queries_ref[at, :].astype(jnp.float32)
        grad_att_ref[at, :] = (grad_att * inv_ref[user]).astype(jnp.bfloat16)
    direct_ref[...] = djoined[:, :key_width] + part_prod * attended_ref[...]


def score(inv_count, queries, attended, labels, mlp_weight, logit_weight):
    requests, key_width = queries.shape
    whole = pl.BlockSpec(memory_space=pltpu.VMEM)
    return pl.pallas_call(
        score_kernel,
        in_specs=[pl.BlockSpec(memory_space=pltpu.SMEM)] + [whole] * 5,
        out_specs=[whole] * 3,
        out_shape=[
            jax.ShapeDtypeStruct((requests, 1), jnp.float32),
            jax.ShapeDtypeStruct((requests, key_width), jnp.bfloat16),
            jax.ShapeDtypeStruct((requests, key_width), jnp.float32),
        ],
        scratch_shapes=[pltpu.VMEM((requests, mlp_weight.shape[1]), jnp.bfloat16)],
        compiler_params=pltpu.CompilerParams(vmem_limit_bytes=32 * MIB),
        cost_estimate=pl.CostEstimate(
            flops=4 * requests * mlp_weight.shape[0] * mlp_weight.shape[1],
            bytes_accessed=1 << 23,
            transcendentals=0,
        ),
        name="score",
    )(inv_count, queries, attended, labels, mlp_weight, logit_weight)


def attend_back_kernel(grad_att_ref, direct_ref, slope_ref, history_ref, grad_rows_ref):
    users, events, key_width = history_ref.shape
    per_user = grad_att_ref.shape[0] // users
    chunk = math.gcd(events, 1024)
    for user in range(users):
        rows = slice(user * per_user, (user + 1) * per_user)
        back = jnp.zeros((per_user, key_width), jnp.float32)
        for at in range(0, events, chunk):
            keys = history_ref[user, at : at + chunk, :]
            slope = slope_ref[rows, at : at + chunk].astype(jnp.float32)
            grad_sig = (dot_rows(grad_att_ref[rows, :], keys) * slope).astype(jnp.bfloat16)
            back += dot(grad_sig, keys)
        grad_rows = direct_ref[rows, :] + back * (1.0 / math.sqrt(key_width))
        grad_rows_ref[rows, :] = grad_rows.astype(jnp.bfloat16)


def attend_back(grad_att, direct, slope, history):
    _, events, key_width = history.shape
    requests = grad_att.shape[0]
    whole = pl.BlockSpec(memory_space=pltpu.VMEM)
    return pl.pallas_call(
        attend_back_kernel,
        in_specs=[whole] * 4,
        out_specs=whole,
        out_shape=jax.ShapeDtypeStruct((requests, key_width), jnp.bfloat16),
        compiler_params=pltpu.CompilerParams(vmem_limit_bytes=20 * MIB),
        cost_estimate=pl.CostEstimate(
            flops=4 * requests * events * key_width, bytes_accessed=1 << 23, transcendentals=0
        ),
        name="attend_back",
    )(grad_att, direct, slope, history)


def sum_rows(cands, at, slots_ref, grad_rows_ref):
    places = lax.broadcasted_iota(jnp.int32, (cands, slots_ref.shape[1]), 0) + at
    return dot((places == slots_ref[...]).astype(jnp.bfloat16), grad_rows_ref[...])


def cand_grad_kernel(slots_ref, grad_rows_ref, cand_grad_ref):
    cands = cand_grad_ref.shape[0]
    chunk = math.gcd(cands, 512)
    for at in range(0, cands, chunk):
        cand_grad_ref[at : at + chunk, :] = sum_rows(chunk, at, slots_ref, grad_rows_ref)


def own_cand_grad(cands, slots, grad_rows):
    requests, key_width = grad_rows.shape
    whole = pl.BlockSpec(memory_space=pltpu.VMEM)
    return pl.pallas_call(
        cand_grad_kernel,
        in_specs=[whole] * 2,
        out_specs=whole,
        out_shape=jax.ShapeDtypeStruct((cands, key_width), jnp.float32),
        compiler_params=pltpu.CompilerParams(vmem_limit_bytes=20 * MIB),
        cost_estimate=pl.CostEstimate(
            flops=2 * cands * key_width * requests, bytes_accessed=1 << 22, transcendentals=0
        ),
        name="own_cand_grad",
    )(slots, grad_rows)


def terms_kernel(
    origins, wide_ref, cand_grad_ref, slots_ref, grad_rows_ref, pooled_ref, out_ref, terms_ref
):
    cands = pooled_ref.shape[0]
    chunk = math.gcd(cands, 512)
    for at in range(0, cands, chunk):
        cand_grad = cand_grad_ref[at : at + chunk, :] + sum_rows(
            chunk, at, slots_ref, grad_rows_ref
        )
        term = dot_columns(pooled_ref[at : at + chunk, :], cand_grad.astype(jnp.bfloat16))
        if at == 0:
            terms_ref[...] = term
        else:
            terms_ref[...] += term
    rows = terms_ref.shape[0] // len(origins)
    wide = wide_ref[0]
    batch = max(1, 32 // rows)
    for slot in range(0, len(origins), batch):
        found = [
            terms_ref[pl.ds(pl.multiple_of((wide ^ origins[slot + i]) * rows, rows), rows), :]
            for i in range(batch)
        ]
        found = found[0] if batch == 1 else jnp.concatenate(found, axis=0)
        out_ref[slot * rows : (slot + batch) * rows, :] = found.astype(jnp.bfloat16)


def chip_terms(origins, wide, cand_grad, far_slots, far_grad_rows, pooled):
    cands, width = pooled.shape
    requests, key_width = far_grad_rows.shape
    whole = pl.BlockSpec(memory_space=pltpu.VMEM)
    return pl.pallas_call(
        functools.partial(terms_kernel, origins),
        in_specs=[pl.BlockSpec(memory_space=pltpu.SMEM)] + [whole] * 4,
        out_specs=whole,
        out_shape=jax.ShapeDtypeStruct((width, key_width), jnp.bfloat16),
        scratch_shapes=[pltpu.VMEM((width, key_width), jnp.float32)],
        compiler_params=pltpu.CompilerParams(vmem_limit_bytes=20 * MIB),
        cost_estimate=pl.CostEstimate(
            flops=2 * cands * key_width * (width + requests),
            bytes_accessed=1 << 22,
            transcendentals=0,
        ),
        name="chip_terms",
    )(wide, cand_grad, far_slots, far_grad_rows, pooled)


def bit_groups(size):
    groups = []
    bit = 0
    while (1 << bit) < size:
        values = min(4, size >> bit)
        groups.append((bit, values))
        bit += values.bit_length() - 1
    return groups


def exchange(values, axis_name, size, distance):
    return lax.ppermute(values, axis_name, [(i, i ^ distance) for i in range(size)])


def send_stage(rows, wides, bit, values):
    return [exchange(rows, "wide", wides, step << bit) for step in range(1, values)]


def after(values, *others):
    return lax.optimization_barrier((tuple(values),) + others)[0]


def slot_of(distance, wides):
    slot = 0
    for bit, values in bit_groups(wides):
        slot = slot * values + ((distance >> bit) & (values - 1))
    return slot


def sum_blocks(blocks, wides, logits):
    total = blocks
    for bit, values in bit_groups(wides):
        if bit > 0:
            total, logits = lax.optimization_barrier((total, logits))
        parts = total.astype(jnp.bfloat16).reshape((values, -1) + blocks.shape[1:])
        found = [
            exchange(parts[step], "wide", wides, step << bit).astype(jnp.float32)
            for step in range(1, values)
        ]
        total = sum(found, parts[0].astype(jnp.float32))
    return total, logits


def body(
    frames,
    qkv_weight,
    out_weight,
    proj_weight,
    mlp_weight,
    logit_weight,
    history,
    hist_len,
    hist_mask,
    req_owner,
    req_local,
    labels,
):
    wides = lax.axis_size("wide")
    core, wide = lax.axis_index("section"), lax.axis_index("wide")
    cand_count = frames.shape[0]
    requests = req_local.shape[0]
    users, events, _ = history.shape
    keep, send, embedded = encode_block(
        core.reshape(1), frames, qkv_weight, out_weight, proj_weight
    )
    positions = jnp.arange(events, dtype=jnp.int32)[None, :]
    usable = (
        (positions < hist_len[:, None]) & ((hist_mask == 1) | (positions == 0))
    ).astype(jnp.float32)
    inv_count = lax.rsqrt(jnp.sum(usable, axis=1))
    usable = usable.reshape(users, 1, events)
    owner_core = req_owner[:, 0] // wides
    owner_slot = slot_of((req_owner[:, 0] % wides) ^ wide, wides)
    slots = ((owner_core ^ core) * wides + owner_slot) * cand_count + req_local
    pooled_slots = (owner_slot * 2 + owner_core) * cand_count + req_local
    stages = list(reversed(bit_groups(wides)))
    near, pooled = embedded, None
    for place, stage in enumerate(stages):
        found = send_stage(near, wides, *stage)
        if place == 0:
            got = exchange(send, "section", 2, 1)
            far_slots = exchange(pooled_slots, "section", 2, 1)
            found, keep, got, far_slots = lax.optimization_barrier((found, keep, got, far_slots))
            pooled = jnp.where(
                core == 0,
                jnp.concatenate([keep, got], axis=0),
                jnp.concatenate([got, keep], axis=0),
            )
        else:
            found_pooled = send_stage(pooled, wides, *stages[place - 1])
            found, found_pooled = lax.optimization_barrier((found, found_pooled))
            pooled = jnp.concatenate([pooled] + found_pooled, axis=0)
        near = jnp.concatenate([near] + found, axis=0)
    far = exchange(near, "section", 2, 1)
    found_pooled = send_stage(pooled, wides, *stages[-1])
    queries, attended, slope = attend(
        inv_count, slots.reshape(requests, 1), near, far, history, usable
    )
    logits, grad_att, direct = score(
        inv_count,
        queries,
        attended,
        labels.reshape(requests, 1),
        mlp_weight,
        logit_weight.reshape(1, -1),
    )
    found_pooled, grad_att = lax.optimization_barrier((found_pooled, grad_att))
    grad_rows = attend_back(grad_att, direct, slope, history)
    far_grad_rows = exchange(grad_rows, "section", 2, 1)
    pooled = jnp.concatenate(after([pooled] + found_pooled, grad_rows), axis=0)
    cand_grad = own_cand_grad(pooled.shape[0], pooled_slots.reshape(1, requests), grad_rows)
    origins = [0] * wides
    for distance in range(wides):
        origins[slot_of(distance, wides)] = distance
    terms = chip_terms(
        origins,
        wide.reshape(1),
        cand_grad,
        far_slots.reshape(1, requests),
        far_grad_rows,
        pooled,
    )
    grad_proj, logits = sum_blocks(terms, wides, logits.reshape(requests))
    return (logits, grad_proj)


def solution(mesh):
    in_specs = (
        P(("section", "wide"), None, None),
        P(),
        P(),
        P(),
        P(),
        P(),
        P(("section", "wide"), None, None),
        P(("section", "wide")),
        P(("section", "wide"), None),
        P(("section", "wide"), None),
        P(("section", "wide")),
        P(("section", "wide")),
    )
    out_specs = (P(("section", "wide")), P(("section", "wide"), None))
    return jax.shard_map(body, mesh=mesh, in_specs=in_specs, out_specs=out_specs, check_vma=False)
```

```python
import functools
import math

import jax
import jax.numpy as jnp
from jax import lax
from jax.experimental import pallas as pl
from jax.experimental.pallas import tpu as pltpu
from jax.sharding import PartitionSpec as P

HEADS = 16
FRAMES = 3


EPSILON = 1e-06
MIB = 1024 * 1024


def layer_norm(values):
    center = values - jnp.mean(values, axis=-1, keepdims=True)
    spread = jnp.mean(jnp.square(center), axis=-1, keepdims=True)
    return center * lax.rsqrt(spread + EPSILON)


def dot(left, right):
    return jnp.dot(left, right, preferred_element_type=jnp.float32)


def dot_rows(left, right):
    return lax.dot_general(left, right, (((1,), (1,)), ((), ())), preferred_element_type=jnp.float32)


def dot_columns(left, right):
    return lax.dot_general(left, right, (((0,), (0,)), ((), ())), preferred_element_type=jnp.float32)


def split_rows(values):
    high = values.astype(jnp.bfloat16)
    low = (values - high.astype(jnp.float32)).astype(jnp.bfloat16)
    return jnp.concatenate([high, low], axis=0)


def dot_split(values, right):
    both = dot(split_rows(values), right)
    rows = values.shape[0]
    return both[:rows] + both[rows:]


def encode_kernel(
    tokens,
    core_ref,
    frames_hbm,
    qkv_hbm,
    out_hbm,
    proj_hbm,
    keep_ref,
    send_ref,
    embedded_ref,
    frames_ref,
    qkv_ref,
    out_ref,
    proj_ref,
    sems,
    normed_ref,
    packed_ref,
    scores_ref,
    mixed_rows_ref,
    sums_ref,
):
    total = embedded_ref.shape[0]
    rows, width = packed_ref.shape[0], packed_ref.shape[1] // 2
    cands = rows // tokens
    groups = total // cands
    head_dim = width // HEADS
    patches = tokens // FRAMES
    lanes = 2 * head_dim
    blocks = rows // lanes
    pairs = HEADS // 2
    quad = 4
    span = quad * head_dim

    def group_rows(group):
        return pl.ds(group * rows, rows)

    def columns(part):
        return pl.ds(part * width, width)

    pieces = [(frames_hbm.at[group_rows(0)], frames_ref.at[group_rows(0)])]
    pieces += [(qkv_hbm.at[:, columns(part)], qkv_ref.at[:, columns(part)]) for part in range(2)]
    pieces += [
        (frames_hbm.at[group_rows(group)], frames_ref.at[group_rows(group)])
        for group in range(1, groups)
    ]
    pieces += [(qkv_hbm.at[:, columns(2)], qkv_ref.at[:, columns(2)])]
    pieces += [(out_hbm, out_ref), (proj_hbm, proj_ref)]
    copies = [
        pltpu.make_async_copy(source, target, sems.at[place])
        for place, (source, target) in enumerate(pieces)
    ]
    for copy in copies:
        copy.start()

    def norm_cand(cand):
        at = slice(cand * tokens, (cand + 1) * tokens)
        inputs = frames_ref[at, :].astype(jnp.float32)
        normed_ref[at, :] = layer_norm(inputs).astype(jnp.bfloat16)
        sums_ref[cand] = jnp.sum(inputs, axis=0, keepdims=True)

    exponent = math.log2(math.e) / math.sqrt(head_dim)
    half = lanes // 2
    frame_at = (lax.broadcasted_iota(jnp.int32, (patches, 2 * lanes), 1) % half) // patches
    even_lanes = lax.broadcasted_iota(jnp.int32, (half, 2 * lanes), 1) % lanes < half
    first_half = lax.broadcasted_iota(jnp.int32, (head_dim, lanes), 1) < half
    low_lanes = lax.broadcasted_iota(jnp.int32, (HEADS // quad, lanes), 1) < half
    nothing = jnp.zeros((head_dim, lanes), jnp.bfloat16)
    ones_row = lax.broadcasted_iota(jnp.int32, (2 * lanes, 2 * lanes), 0) // patches
    ones_column = lax.broadcasted_iota(jnp.int32, (2 * lanes, 2 * lanes), 1) // patches
    frame_ones = (ones_row == ones_column).astype(jnp.bfloat16)
    own = lax.broadcasted_iota(jnp.int32, (cands, rows), 1) // tokens == lax.broadcasted_iota(
        jnp.int32, (cands, rows), 0
    )

    def own_scores(block, head):
        start = head * head_dim
        low, high = (
            packed_ref[block * lanes + side * half : block * lanes + (side + 1) * half, start : start + span]
            for side in range(2)
        )
        keys = packed_ref[
            block * lanes : (block + 1) * lanes, width + start : width + start + span
        ].T
        for turn in range(2):
            query = jnp.where(even_lanes, low, high) if turn == 0 else jnp.where(even_lanes, high, low)
            rows_of = []
            for place in range(quad):
                own_keys = keys[place * head_dim : (place + 1) * head_dim]
                if (place + turn) % 2 == 0:
                    own_keys = jnp.where(first_half, own_keys, nothing)
                else:
                    own_keys = jnp.where(first_half, nothing, own_keys)
                both = [own_keys, nothing] if place < 2 else [nothing, own_keys]
                rows_of.append(jnp.concatenate(both, axis=1))
            scores = dot(query, jnp.concatenate(rows_of, axis=0))
            found = scores[:patches]
            for frame in range(1, half // patches):
                found = jnp.where(
                    frame_at == frame, scores[frame * patches : (frame + 1) * patches], found
                )
            scores_ref[block, turn * (HEADS // quad) + head // quad] = found

    copies[0].wait()
    for cand in range(cands):
        norm_cand(cand)
    copies[1].wait()
    copies[2].wait()
    for group in range(groups):
        at = slice(group * rows, (group + 1) * rows)
        for part in range(2):
            part_columns = slice(part * width, (part + 1) * width)
            packed_ref[:, part_columns] = dot(normed_ref[at, :], qkv_ref[:, part_columns]).astype(
                jnp.bfloat16
            )
        if group + 1 < groups:
            copies[3 + group].wait()
        for head in range(0, HEADS, quad):
            for block in range(blocks):
                own_scores(block, head)
            if group + 1 < groups:
                for cand in range(head * cands // HEADS, (head + quad) * cands // HEADS):
                    norm_cand((group + 1) * cands + cand)
        exp_scores = jnp.exp2(
            scores_ref[...].reshape(blocks * pairs * patches, 2 * lanes) * exponent
        )
        totals = dot(exp_scores.astype(jnp.bfloat16), frame_ones)
        probs = (exp_scores / totals).reshape(blocks * pairs, patches, 2 * lanes)
        sums = jnp.sum(probs, axis=1)
        quads = HEADS // quad
        key_sums = []
        for pair in range(quad // 2):
            sides = []
            for side in range(2):
                found = []
                for block in range(blocks):
                    first = sums[block * pairs : block * pairs + quads, pair * lanes : (pair + 1) * lanes]
                    second = sums[
                        block * pairs + quads : (block + 1) * pairs, pair * lanes : (pair + 1) * lanes
                    ]
                    if side == 1:
                        first, second = second, first
                    found.append(jnp.where(low_lanes, first, second))
                sides.append(jnp.concatenate(found, axis=1))
            key_sums.append(sides)
        spread = jnp.concatenate(
            [
                jnp.where(
                    own, key_sums[head % quad // 2][head % 2][head // quad : head // quad + 1], 0.0
                )
                for head in range(HEADS)
            ],
            axis=0,
        ).astype(jnp.bfloat16)
        mixed_rows = dot(spread, normed_ref[at, :])
        for head in range(HEADS):
            mixed_rows_ref[head, group * cands : (group + 1) * cands, :] = mixed_rows[
                head * cands : (head + 1) * cands
            ]

    for copy in copies[2 + groups :]:
        copy.wait()
    mixed = []
    for head in range(0, HEADS, quad):
        left = mixed_rows_ref[head : head + quad].reshape(quad * total, width)
        start = 2 * width + head * head_dim
        both = dot_split(left, qkv_ref[:, start : start + span])
        head_at = lax.broadcasted_iota(jnp.int32, (total, span), 1) // head_dim
        piece = jnp.zeros((total, span), jnp.float32)
        for place in range(quad):
            piece = jnp.where(head_at == place, both[place * total : (place + 1) * total], piece)
        mixed.append(piece)
    mixed_mean = jnp.concatenate(mixed, axis=1) * (1.0 / tokens)
    hidden = sums_ref[...].reshape(total, width) * (1.0 / tokens)
    hidden += dot_split(mixed_mean, out_ref[...])
    pooled = layer_norm(hidden).astype(jnp.bfloat16)
    first, second = pooled[:, : width // 2], pooled[:, width // 2 :]
    keep_ref[...] = jnp.where(core_ref[0] == 0, first, second)
    send_ref[...] = jnp.where(core_ref[0] == 0, second, first)
    embedded_ref[...] = dot(pooled, proj_ref[...]).astype(jnp.bfloat16)


def in_hbm(*arrays):
    return [pltpu.with_memory_space_constraint(array, pltpu.HBM) for array in arrays]


def encode_block(core, frames, qkv_weight, out_weight, proj_weight):
    cand_count, tokens, width = frames.shape
    key_width = proj_weight.shape[1]
    groups = 2
    rows = cand_count * tokens // groups
    lanes = 2 * width // HEADS
    patches = tokens // FRAMES
    flat = frames.reshape(cand_count * tokens, width)
    whole = pl.BlockSpec(memory_space=pltpu.VMEM)
    return pl.pallas_call(
        functools.partial(encode_kernel, tokens),
        in_specs=[pl.BlockSpec(memory_space=pltpu.SMEM)]
        + [pl.BlockSpec(memory_space=pltpu.HBM)] * 4,
        out_specs=[whole] * 3,
        out_shape=[
            jax.ShapeDtypeStruct((cand_count, width // 2), jnp.bfloat16),
            jax.ShapeDtypeStruct((cand_count, width // 2), jnp.bfloat16),
            jax.ShapeDtypeStruct((cand_count, key_width), jnp.bfloat16),
        ],
        scratch_shapes=[
            pltpu.VMEM(flat.shape, jnp.bfloat16),
            pltpu.VMEM(qkv_weight.shape, jnp.bfloat16),
            pltpu.VMEM(out_weight.shape, jnp.bfloat16),
            pltpu.VMEM(proj_weight.shape, jnp.bfloat16),
            pltpu.SemaphoreType.DMA((groups + 5,)),
            pltpu.VMEM(flat.shape, jnp.bfloat16),
            pltpu.VMEM((rows, 2 * width), jnp.bfloat16),
            pltpu.VMEM((rows // lanes, HEADS // 2, patches, 2 * lanes), jnp.float32),
            pltpu.VMEM((HEADS, cand_count, width), jnp.float32),
            pltpu.VMEM((cand_count, 1, width), jnp.float32),
        ],
        compiler_params=pltpu.CompilerParams(vmem_limit_bytes=44 * MIB),
        cost_estimate=pl.CostEstimate(
            flops=5 * cand_count * tokens * width * width, bytes_accessed=1 << 24, transcendentals=0
        ),
        name="encode",
    )(core, *in_hbm(flat, qkv_weight, out_weight, proj_weight))


def attend_kernel(
    inv_ref,
    slots_ref,
    near_ref,
    far_ref,
    usable_ref,
    history_hbm,
    mlp_hbm,
    queries_ref,
    attended_ref,
    slope_ref,
    mlp_ref,
    history_ref,
    sems,
):
    users, events, _ = history_ref.shape
    chunk = math.gcd(events, 1024)
    copies = [
        pltpu.make_async_copy(history_hbm.at[user], history_ref.at[user], sems.at[user])
        for user in range(users)
    ]
    copies.append(pltpu.make_async_copy(mlp_hbm, mlp_ref, sems.at[users]))
    for copy in copies:
        copy.start()
    slots = slots_ref[...]
    half, key_width = near_ref.shape
    places = lax.broadcasted_iota(jnp.int32, (slots.shape[0], half), 1)
    queries = dot((slots == places).astype(jnp.bfloat16), near_ref[...])
    queries += dot((slots == places + half).astype(jnp.bfloat16), far_ref[...])
    queries_ref[...] = queries.astype(jnp.bfloat16)
    per_user = slots.shape[0] // users
    for user in range(users):
        copies[user].wait()
        rows = slice(user * per_user, (user + 1) * per_user)
        attended = jnp.zeros((per_user, key_width), jnp.float32)
        for at in range(0, events, chunk):
            keys = history_ref[user, at : at + chunk, :]
            usable = usable_ref[user, :, at : at + chunk]
            scores = dot_rows(queries_ref[rows, :], keys)
            half_gate = 0.5 * jnp.tanh(scores * (0.5 / math.sqrt(key_width)))
            weights = (0.5 + half_gate) * usable
            slope_ref[rows, at : at + chunk] = (weights * (0.5 - half_gate)).astype(jnp.bfloat16)
            attended += dot(weights.astype(jnp.bfloat16), keys)
        attended_ref[rows, :] = attended * inv_ref[user]
    copies[users].wait()


def attend(inv_count, slots, near, far, history, usable, mlp_weight):
    users, events, key_width = history.shape
    requests = slots.shape[0]
    whole = pl.BlockSpec(memory_space=pltpu.VMEM)
    return pl.pallas_call(
        attend_kernel,
        in_specs=[pl.BlockSpec(memory_space=pltpu.SMEM)]
        + [whole] * 4
        + [pl.BlockSpec(memory_space=pltpu.HBM)] * 2,
        out_specs=[whole] * 4,
        out_shape=[
            jax.ShapeDtypeStruct((requests, key_width), jnp.bfloat16),
            jax.ShapeDtypeStruct((requests, key_width), jnp.float32),
            jax.ShapeDtypeStruct((requests, events), jnp.bfloat16),
            pltpu.VMEM(mlp_weight.shape, mlp_weight.dtype),
        ],
        scratch_shapes=[
            pltpu.VMEM(history.shape, history.dtype),
            pltpu.SemaphoreType.DMA((users + 1,)),
        ],
        compiler_params=pltpu.CompilerParams(vmem_limit_bytes=32 * MIB),
        cost_estimate=pl.CostEstimate(
            flops=4 * requests * events * key_width, bytes_accessed=1 << 24, transcendentals=0
        ),
        name="attend",
    )(inv_count, slots, near, far, usable, *in_hbm(history, mlp_weight))


def score_kernel(
    inv_ref,
    queries_ref,
    attended_ref,
    labels_ref,
    mlp_ref,
    logit_weight_ref,
    logits_ref,
    grad_att_ref,
    direct_ref,
    grad_pre_ref,
):
    users = inv_ref.shape[0]
    per_user = queries_ref.shape[0] // users
    step_users = math.gcd(users, 2)
    step_rows = step_users * per_user
    key_width = queries_ref.shape[1]
    weight = logit_weight_ref[...].astype(jnp.float32)
    for first in range(0, users, step_users):
        at = slice(first * per_user, first * per_user + step_rows)
        query_b = queries_ref[at, :]
        query_f = query_b.astype(jnp.float32)
        attended = attended_ref[at, :]
        joined = jnp.concatenate(
            [query_b, attended.astype(jnp.bfloat16), (query_f * attended).astype(jnp.bfloat16)],
            axis=1,
        )
        pre_act = dot(joined, mlp_ref[...])
        act_sig = 0.5 * jnp.tanh(0.5 * pre_act) + 0.5
        hidden_units = (pre_act * act_sig).astype(jnp.bfloat16)
        logits = jnp.sum(hidden_units.astype(jnp.float32) * weight, axis=1, keepdims=True)
        logits_ref[at, :] = logits
        dlogit = (0.5 * jnp.tanh(0.5 * logits) + 0.5) - labels_ref[at, :].astype(jnp.float32)
        slope = act_sig * (1.0 + pre_act * (1.0 - act_sig))
        grad_pre = (dlogit * weight * slope).astype(jnp.bfloat16)
        grad_pre_ref[at, :] = grad_pre
    djoined = dot_rows(grad_pre_ref[...], mlp_ref[...])
    part_att = djoined[:, key_width : 2 * key_width]
    part_prod = djoined[:, 2 * key_width :]
    for user in range(users):
        at = slice(user * per_user, (user + 1) * per_user)
        grad_att = part_att[at] + part_prod[at] * queries_ref[at, :].astype(jnp.float32)
        grad_att_ref[at, :] = (grad_att * inv_ref[user]).astype(jnp.bfloat16)
    direct_ref[...] = djoined[:, :key_width] + part_prod * attended_ref[...]


def score(inv_count, queries, attended, labels, mlp_weight, logit_weight):
    requests, key_width = queries.shape
    whole = pl.BlockSpec(memory_space=pltpu.VMEM)
    return pl.pallas_call(
        score_kernel,
        in_specs=[pl.BlockSpec(memory_space=pltpu.SMEM)] + [whole] * 5,
        out_specs=[whole] * 3,
        out_shape=[
            jax.ShapeDtypeStruct((requests, 1), jnp.float32),
            jax.ShapeDtypeStruct((requests, key_width), jnp.bfloat16),
            jax.ShapeDtypeStruct((requests, key_width), jnp.float32),
        ],
        scratch_shapes=[pltpu.VMEM((requests, mlp_weight.shape[1]), jnp.bfloat16)],
        compiler_params=pltpu.CompilerParams(vmem_limit_bytes=32 * MIB),
        cost_estimate=pl.CostEstimate(
            flops=4 * requests * mlp_weight.shape[0] * mlp_weight.shape[1],
            bytes_accessed=1 << 23,
            transcendentals=0,
        ),
        name="score",
    )(inv_count, queries, attended, labels, mlp_weight, logit_weight)


def attend_back_kernel(grad_att_ref, direct_ref, slope_ref, history_ref, grad_rows_ref):
    users, events, key_width = history_ref.shape
    per_user = grad_att_ref.shape[0] // users
    chunk = math.gcd(events, 1024)
    for user in range(users):
        rows = slice(user * per_user, (user + 1) * per_user)
        back = jnp.zeros((per_user, key_width), jnp.float32)
        for at in range(0, events, chunk):
            keys = history_ref[user, at : at + chunk, :]
            slope = slope_ref[rows, at : at + chunk].astype(jnp.float32)
            grad_sig = (dot_rows(grad_att_ref[rows, :], keys) * slope).astype(jnp.bfloat16)
            back += dot(grad_sig, keys)
        grad_rows = direct_ref[rows, :] + back * (1.0 / math.sqrt(key_width))
        grad_rows_ref[rows, :] = grad_rows.astype(jnp.bfloat16)


def attend_back(grad_att, direct, slope, history):
    _, events, key_width = history.shape
    requests = grad_att.shape[0]
    whole = pl.BlockSpec(memory_space=pltpu.VMEM)
    return pl.pallas_call(
        attend_back_kernel,
        in_specs=[whole] * 4,
        out_specs=whole,
        out_shape=jax.ShapeDtypeStruct((requests, key_width), jnp.bfloat16),
        compiler_params=pltpu.CompilerParams(vmem_limit_bytes=20 * MIB),
        cost_estimate=pl.CostEstimate(
            flops=4 * requests * events * key_width, bytes_accessed=1 << 23, transcendentals=0
        ),
        name="attend_back",
    )(grad_att, direct, slope, history)


def sum_rows(cands, at, slots_ref, grad_rows_ref):
    places = lax.broadcasted_iota(jnp.int32, (cands, slots_ref.shape[1]), 0) + at
    return dot((places == slots_ref[...]).astype(jnp.bfloat16), grad_rows_ref[...])


def cand_grad_kernel(slots_ref, grad_rows_ref, cand_grad_ref):
    cands = cand_grad_ref.shape[0]
    chunk = math.gcd(cands, 512)
    for at in range(0, cands, chunk):
        cand_grad_ref[at : at + chunk, :] = sum_rows(chunk, at, slots_ref, grad_rows_ref)


def own_cand_grad(cands, slots, grad_rows):
    requests, key_width = grad_rows.shape
    whole = pl.BlockSpec(memory_space=pltpu.VMEM)
    return pl.pallas_call(
        cand_grad_kernel,
        in_specs=[whole] * 2,
        out_specs=whole,
        out_shape=jax.ShapeDtypeStruct((cands, key_width), jnp.float32),
        compiler_params=pltpu.CompilerParams(vmem_limit_bytes=20 * MIB),
        cost_estimate=pl.CostEstimate(
            flops=2 * cands * key_width * requests, bytes_accessed=1 << 22, transcendentals=0
        ),
        name="own_cand_grad",
    )(slots, grad_rows)


def terms_kernel(
    origins, wide_ref, cand_grad_ref, slots_ref, grad_rows_ref, pooled_ref, out_ref, terms_ref
):
    cands = pooled_ref.shape[0]
    chunk = math.gcd(cands, 512)
    for at in range(0, cands, chunk):
        cand_grad = cand_grad_ref[at : at + chunk, :] + sum_rows(
            chunk, at, slots_ref, grad_rows_ref
        )
        term = dot_columns(pooled_ref[at : at + chunk, :], cand_grad.astype(jnp.bfloat16))
        if at == 0:
            terms_ref[...] = term
        else:
            terms_ref[...] += term
    rows = terms_ref.shape[0] // len(origins)
    wide = wide_ref[0]
    batch = max(1, 32 // rows)
    for slot in range(0, len(origins), batch):
        found = [
            terms_ref[pl.ds(pl.multiple_of((wide ^ origins[slot + i]) * rows, rows), rows), :]
            for i in range(batch)
        ]
        found = found[0] if batch == 1 else jnp.concatenate(found, axis=0)
        out_ref[slot * rows : (slot + batch) * rows, :] = found.astype(jnp.bfloat16)


def chip_terms(origins, wide, cand_grad, far_slots, far_grad_rows, pooled):
    cands, width = pooled.shape
    requests, key_width = far_grad_rows.shape
    whole = pl.BlockSpec(memory_space=pltpu.VMEM)
    return pl.pallas_call(
        functools.partial(terms_kernel, origins),
        in_specs=[pl.BlockSpec(memory_space=pltpu.SMEM)] + [whole] * 4,
        out_specs=whole,
        out_shape=jax.ShapeDtypeStruct((width, key_width), jnp.bfloat16),
        scratch_shapes=[pltpu.VMEM((width, key_width), jnp.float32)],
        compiler_params=pltpu.CompilerParams(vmem_limit_bytes=20 * MIB),
        cost_estimate=pl.CostEstimate(
            flops=2 * cands * key_width * (width + requests),
            bytes_accessed=1 << 22,
            transcendentals=0,
        ),
        name="chip_terms",
    )(wide, cand_grad, far_slots, far_grad_rows, pooled)


def bit_groups(size):
    groups = []
    bit = 0
    while (1 << bit) < size:
        values = min(4, size >> bit)
        groups.append((bit, values))
        bit += values.bit_length() - 1
    return groups


def exchange(values, axis_name, size, distance):
    return lax.ppermute(values, axis_name, [(i, i ^ distance) for i in range(size)])


def send_stage(rows, wides, bit, values):
    return [exchange(rows, "wide", wides, step << bit) for step in range(1, values)]


def after(values, *others):
    return lax.optimization_barrier((tuple(values),) + others)[0]


def slot_of(distance, wides):
    slot = 0
    for bit, values in bit_groups(wides):
        slot = slot * values + ((distance >> bit) & (values - 1))
    return slot


def sum_blocks(blocks, wides, logits):
    total = blocks
    for bit, values in bit_groups(wides):
        if bit > 0:
            total, logits = lax.optimization_barrier((total, logits))
        parts = total.astype(jnp.bfloat16).reshape((values, -1) + blocks.shape[1:])
        found = [
            exchange(parts[step], "wide", wides, step << bit).astype(jnp.float32)
            for step in range(1, values)
        ]
        total = sum(found, parts[0].astype(jnp.float32))
    return total, logits


def body(
    frames,
    qkv_weight,
    out_weight,
    proj_weight,
    mlp_weight,
    logit_weight,
    history,
    hist_len,
    hist_mask,
    req_owner,
    req_local,
    labels,
):
    wides = lax.axis_size("wide")
    core, wide = lax.axis_index("section"), lax.axis_index("wide")
    cand_count = frames.shape[0]
    requests = req_local.shape[0]
    users, events, _ = history.shape
    keep, send, embedded = encode_block(
        core.reshape(1), frames, qkv_weight, out_weight, proj_weight
    )
    positions = jnp.arange(events, dtype=jnp.int32)[None, :]
    usable = (
        (positions < hist_len[:, None]) & ((hist_mask == 1) | (positions == 0))
    ).astype(jnp.float32)
    inv_count = lax.rsqrt(jnp.sum(usable, axis=1))
    usable = usable.reshape(users, 1, events)
    owner_core = req_owner[:, 0] // wides
    owner_slot = slot_of((req_owner[:, 0] % wides) ^ wide, wides)
    slots = ((owner_core ^ core) * wides + owner_slot) * cand_count + req_local
    pooled_slots = (owner_slot * 2 + owner_core) * cand_count + req_local
    stages = list(reversed(bit_groups(wides)))
    near, pooled = embedded, None
    for place, stage in enumerate(stages):
        found = send_stage(near, wides, *stage)
        if place == 0:
            got = exchange(send, "section", 2, 1)
            far_slots = exchange(pooled_slots, "section", 2, 1)
            found, keep, got, far_slots = lax.optimization_barrier((found, keep, got, far_slots))
            pooled = jnp.where(
                core == 0,
                jnp.concatenate([keep, got], axis=0),
                jnp.concatenate([got, keep], axis=0),
            )
        else:
            found_pooled = send_stage(pooled, wides, *stages[place - 1])
            found, found_pooled = lax.optimization_barrier((found, found_pooled))
            pooled = jnp.concatenate([pooled] + found_pooled, axis=0)
        near = jnp.concatenate([near] + found, axis=0)
    far = exchange(near, "section", 2, 1)
    found_pooled = send_stage(pooled, wides, *stages[-1])
    queries, attended, slope, mlp_weight = attend(
        inv_count, slots.reshape(requests, 1), near, far, history, usable, mlp_weight
    )
    logits, grad_att, direct = score(
        inv_count,
        queries,
        attended,
        labels.reshape(requests, 1),
        mlp_weight,
        logit_weight.reshape(1, -1),
    )
    found_pooled, grad_att = lax.optimization_barrier((found_pooled, grad_att))
    grad_rows = attend_back(grad_att, direct, slope, history)
    far_grad_rows = exchange(grad_rows, "section", 2, 1)
    pooled = jnp.concatenate(after([pooled] + found_pooled, grad_rows), axis=0)
    cand_grad = own_cand_grad(pooled.shape[0], pooled_slots.reshape(1, requests), grad_rows)
    origins = [0] * wides
    for distance in range(wides):
        origins[slot_of(distance, wides)] = distance
    terms = chip_terms(
        origins,
        wide.reshape(1),
        cand_grad,
        far_slots.reshape(1, requests),
        far_grad_rows,
        pooled,
    )
    grad_proj, logits = sum_blocks(terms, wides, logits.reshape(requests))
    return (logits, grad_proj)


def solution(mesh):
    in_specs = (
        P(("section", "wide"), None, None),
        P(),
        P(),
        P(),
        P(),
        P(),
        P(("section", "wide"), None, None),
        P(("section", "wide")),
        P(("section", "wide"), None),
        P(("section", "wide"), None),
        P(("section", "wide")),
        P(("section", "wide")),
    )
    out_specs = (P(("section", "wide")), P(("section", "wide"), None))
    return jax.shard_map(body, mesh=mesh, in_specs=in_specs, out_specs=out_specs, check_vma=False)
```

```python
import functools
import math

import jax
import jax.numpy as jnp
from jax import lax
from jax.experimental import pallas as pl
from jax.experimental.pallas import tpu as pltpu
from jax.sharding import PartitionSpec as P

HEADS = 16
FRAMES = 3


EPSILON = 1e-06
MIB = 1024 * 1024


def layer_norm(values):
    center = values - jnp.mean(values, axis=-1, keepdims=True)
    spread = jnp.mean(jnp.square(center), axis=-1, keepdims=True)
    return center * lax.rsqrt(spread + EPSILON)


def dot(left, right):
    return jnp.dot(left, right, preferred_element_type=jnp.float32)


def dot_rows(left, right):
    return lax.dot_general(left, right, (((1,), (1,)), ((), ())), preferred_element_type=jnp.float32)


def dot_columns(left, right):
    return lax.dot_general(left, right, (((0,), (0,)), ((), ())), preferred_element_type=jnp.float32)


def split_rows(values):
    high = values.astype(jnp.bfloat16)
    low = (values - high.astype(jnp.float32)).astype(jnp.bfloat16)
    return jnp.concatenate([high, low], axis=0)


def dot_split(values, right):
    both = dot(split_rows(values), right)
    rows = values.shape[0]
    return both[:rows] + both[rows:]


def encode_kernel(
    tokens,
    core_ref,
    frames_hbm,
    qkv_hbm,
    out_hbm,
    proj_hbm,
    keep_ref,
    send_ref,
    embedded_ref,
    frames_ref,
    qkv_ref,
    out_ref,
    proj_ref,
    sems,
    normed_ref,
    packed_ref,
    scores_ref,
    mixed_rows_ref,
    sums_ref,
):
    total = embedded_ref.shape[0]
    rows, width = packed_ref.shape[0], packed_ref.shape[1] // 2
    cands = rows // tokens
    groups = total // cands
    head_dim = width // HEADS
    patches = tokens // FRAMES
    lanes = 2 * head_dim
    blocks = rows // lanes
    pairs = HEADS // 2
    quad = 4
    span = quad * head_dim

    def group_rows(group):
        return pl.ds(group * rows, rows)

    def columns(part):
        return pl.ds(part * width, width)

    pieces = [(frames_hbm.at[group_rows(0)], frames_ref.at[group_rows(0)])]
    pieces += [(qkv_hbm.at[:, columns(part)], qkv_ref.at[:, columns(part)]) for part in range(2)]
    pieces += [
        (frames_hbm.at[group_rows(group)], frames_ref.at[group_rows(group)])
        for group in range(1, groups)
    ]
    pieces += [(qkv_hbm.at[:, columns(2)], qkv_ref.at[:, columns(2)])]
    pieces += [(out_hbm, out_ref), (proj_hbm, proj_ref)]
    copies = [
        pltpu.make_async_copy(source, target, sems.at[place])
        for place, (source, target) in enumerate(pieces)
    ]
    copies[0].start()
    copies[1].start()

    def norm_cand(cand):
        at = slice(cand * tokens, (cand + 1) * tokens)
        inputs = frames_ref[at, :].astype(jnp.float32)
        normed_ref[at, :] = layer_norm(inputs).astype(jnp.bfloat16)
        sums_ref[cand] = jnp.sum(inputs, axis=0, keepdims=True)

    exponent = math.log2(math.e) / math.sqrt(head_dim)
    frame_at = (lax.broadcasted_iota(jnp.int32, (patches, quad * lanes), 1) % lanes) // patches
    nothing = jnp.zeros((head_dim, lanes), jnp.bfloat16)
    ones_row = lax.broadcasted_iota(jnp.int32, (2 * lanes, 2 * lanes), 0) // patches
    ones_column = lax.broadcasted_iota(jnp.int32, (2 * lanes, 2 * lanes), 1) // patches
    frame_ones = (ones_row == ones_column).astype(jnp.bfloat16)
    own = lax.broadcasted_iota(jnp.int32, (cands, rows), 1) // tokens == lax.broadcasted_iota(
        jnp.int32, (cands, rows), 0
    )

    def own_scores(block, head):
        block_rows = slice(block * lanes, (block + 1) * lanes)
        start = head * head_dim
        query = packed_ref[block_rows, start : start + span]
        keys = packed_ref[block_rows, width + start : width + start + span].T
        keys = jnp.concatenate(
            [
                jnp.concatenate(
                    [nothing] * place
                    + [keys[place * head_dim : (place + 1) * head_dim]]
                    + [nothing] * (quad - 1 - place),
                    axis=1,
                )
                for place in range(quad)
            ],
            axis=0,
        )
        scores = dot(query, keys)
        found = scores[:patches]
        for frame in range(1, lanes // patches):
            found = jnp.where(
                frame_at == frame, scores[frame * patches : (frame + 1) * patches], found
            )
        for side in range(quad // 2):
            scores_ref[block, head // 2 + side] = found[
                :, side * 2 * lanes : (side + 1) * 2 * lanes
            ]

    copies[0].wait()
    copies[2].start()
    for cand in range(cands):
        norm_cand(cand)
    copies[1].wait()
    for copy in copies[3 : 2 + groups]:
        copy.start()
    for group in range(groups):
        at = slice(group * rows, (group + 1) * rows)
        for part in range(2):
            if group == 0 and part == 1:
                copies[2].wait()
                for copy in copies[2 + groups :]:
                    copy.start()
            part_columns = slice(part * width, (part + 1) * width)
            packed_ref[:, part_columns] = dot(normed_ref[at, :], qkv_ref[:, part_columns]).astype(
                jnp.bfloat16
            )
        if group + 1 < groups:
            copies[3 + group].wait()
        for head in range(0, HEADS, quad):
            for block in range(blocks):
                own_scores(block, head)
            if group + 1 < groups:
                for cand in range(head * cands // HEADS, (head + quad) * cands // HEADS):
                    norm_cand((group + 1) * cands + cand)
        exp_scores = jnp.exp2(
            scores_ref[...].reshape(blocks * pairs * patches, 2 * lanes) * exponent
        )
        totals = dot(exp_scores.astype(jnp.bfloat16), frame_ones)
        probs = (exp_scores / totals).reshape(blocks * pairs, patches, 2 * lanes)
        sums = jnp.sum(probs, axis=1)
        key_sums = [
            jnp.concatenate(
                [
                    sums[block * pairs : (block + 1) * pairs, side * lanes : (side + 1) * lanes]
                    for block in range(blocks)
                ],
                axis=1,
            )
            for side in range(2)
        ]
        spread = jnp.concatenate(
            [
                jnp.where(own, key_sums[head % 2][head // 2 : head // 2 + 1], 0.0)
                for head in range(HEADS)
            ],
            axis=0,
        ).astype(jnp.bfloat16)
        mixed_rows = dot(spread, normed_ref[at, :])
        for head in range(HEADS):
            mixed_rows_ref[head, group * cands : (group + 1) * cands, :] = mixed_rows[
                head * cands : (head + 1) * cands
            ]

    for copy in copies[2 + groups :]:
        copy.wait()
    mixed = []
    for head in range(0, HEADS, quad):
        left = mixed_rows_ref[head : head + quad].reshape(quad * total, width)
        start = 2 * width + head * head_dim
        both = dot_split(left, qkv_ref[:, start : start + span])
        head_at = lax.broadcasted_iota(jnp.int32, (total, span), 1) // head_dim
        piece = jnp.zeros((total, span), jnp.float32)
        for place in range(quad):
            piece = jnp.where(head_at == place, both[place * total : (place + 1) * total], piece)
        mixed.append(piece)
    mixed_mean = jnp.concatenate(mixed, axis=1) * (1.0 / tokens)
    hidden = sums_ref[...].reshape(total, width) * (1.0 / tokens)
    hidden += dot_split(mixed_mean, out_ref[...])
    pooled = layer_norm(hidden).astype(jnp.bfloat16)
    first, second = pooled[:, : width // 2], pooled[:, width // 2 :]
    keep_ref[...] = jnp.where(core_ref[0] == 0, first, second)
    send_ref[...] = jnp.where(core_ref[0] == 0, second, first)
    embedded_ref[...] = dot(pooled, proj_ref[...]).astype(jnp.bfloat16)


def in_hbm(*arrays):
    return [pltpu.with_memory_space_constraint(array, pltpu.HBM) for array in arrays]


def encode_block(core, frames, qkv_weight, out_weight, proj_weight):
    cand_count, tokens, width = frames.shape
    key_width = proj_weight.shape[1]
    groups = 2
    rows = cand_count * tokens // groups
    lanes = 2 * width // HEADS
    patches = tokens // FRAMES
    flat = frames.reshape(cand_count * tokens, width)
    whole = pl.BlockSpec(memory_space=pltpu.VMEM)
    return pl.pallas_call(
        functools.partial(encode_kernel, tokens),
        in_specs=[pl.BlockSpec(memory_space=pltpu.SMEM)]
        + [pl.BlockSpec(memory_space=pltpu.HBM)] * 4,
        out_specs=[whole] * 3,
        out_shape=[
            jax.ShapeDtypeStruct((cand_count, width // 2), jnp.bfloat16),
            jax.ShapeDtypeStruct((cand_count, width // 2), jnp.bfloat16),
            jax.ShapeDtypeStruct((cand_count, key_width), jnp.bfloat16),
        ],
        scratch_shapes=[
            pltpu.VMEM(flat.shape, jnp.bfloat16),
            pltpu.VMEM(qkv_weight.shape, jnp.bfloat16),
            pltpu.VMEM(out_weight.shape, jnp.bfloat16),
            pltpu.VMEM(proj_weight.shape, jnp.bfloat16),
            pltpu.SemaphoreType.DMA((groups + 5,)),
            pltpu.VMEM(flat.shape, jnp.bfloat16),
            pltpu.VMEM((rows, 2 * width), jnp.bfloat16),
            pltpu.VMEM((rows // lanes, HEADS // 2, patches, 2 * lanes), jnp.float32),
            pltpu.VMEM((HEADS, cand_count, width), jnp.float32),
            pltpu.VMEM((cand_count, 1, width), jnp.float32),
        ],
        compiler_params=pltpu.CompilerParams(vmem_limit_bytes=44 * MIB),
        cost_estimate=pl.CostEstimate(
            flops=5 * cand_count * tokens * width * width, bytes_accessed=1 << 24, transcendentals=0
        ),
        name="encode",
    )(core, *in_hbm(flat, qkv_weight, out_weight, proj_weight))


def attend_kernel(
    inv_ref,
    slots_ref,
    near_ref,
    far_ref,
    usable_ref,
    history_hbm,
    mlp_hbm,
    queries_ref,
    attended_ref,
    slope_ref,
    mlp_ref,
    history_ref,
    sems,
):
    users, events, _ = history_ref.shape
    chunk = math.gcd(events, 1024)
    copies = [
        pltpu.make_async_copy(history_hbm.at[user], history_ref.at[user], sems.at[user])
        for user in range(users)
    ]
    copies.append(pltpu.make_async_copy(mlp_hbm, mlp_ref, sems.at[users]))
    for copy in copies[:2]:
        copy.start()
    slots = slots_ref[...]
    half, key_width = near_ref.shape
    places = lax.broadcasted_iota(jnp.int32, (slots.shape[0], half), 1)
    queries = dot((slots == places).astype(jnp.bfloat16), near_ref[...])
    queries += dot((slots == places + half).astype(jnp.bfloat16), far_ref[...])
    queries_ref[...] = queries.astype(jnp.bfloat16)
    per_user = slots.shape[0] // users
    for user in range(users):
        copies[user].wait()
        if user + 2 < len(copies):
            copies[user + 2].start()
        rows = slice(user * per_user, (user + 1) * per_user)
        attended = jnp.zeros((per_user, key_width), jnp.float32)
        for at in range(0, events, chunk):
            keys = history_ref[user, at : at + chunk, :]
            usable = usable_ref[user, :, at : at + chunk]
            scores = dot_rows(queries_ref[rows, :], keys)
            half_gate = 0.5 * jnp.tanh(scores * (0.5 / math.sqrt(key_width)))
            weights = (0.5 + half_gate) * usable
            slope_ref[rows, at : at + chunk] = (weights * (0.5 - half_gate)).astype(jnp.bfloat16)
            attended += dot(weights.astype(jnp.bfloat16), keys)
        attended_ref[rows, :] = attended * inv_ref[user]
    copies[users].wait()


def attend(inv_count, slots, near, far, history, usable, mlp_weight):
    users, events, key_width = history.shape
    requests = slots.shape[0]
    whole = pl.BlockSpec(memory_space=pltpu.VMEM)
    return pl.pallas_call(
        attend_kernel,
        in_specs=[pl.BlockSpec(memory_space=pltpu.SMEM)]
        + [whole] * 4
        + [pl.BlockSpec(memory_space=pltpu.HBM)] * 2,
        out_specs=[whole] * 4,
        out_shape=[
            jax.ShapeDtypeStruct((requests, key_width), jnp.bfloat16),
            jax.ShapeDtypeStruct((requests, key_width), jnp.float32),
            jax.ShapeDtypeStruct((requests, events), jnp.bfloat16),
            pltpu.VMEM(mlp_weight.shape, mlp_weight.dtype),
        ],
        scratch_shapes=[
            pltpu.VMEM(history.shape, history.dtype),
            pltpu.SemaphoreType.DMA((users + 1,)),
        ],
        compiler_params=pltpu.CompilerParams(vmem_limit_bytes=32 * MIB),
        cost_estimate=pl.CostEstimate(
            flops=4 * requests * events * key_width, bytes_accessed=1 << 24, transcendentals=0
        ),
        name="attend",
    )(inv_count, slots, near, far, usable, *in_hbm(history, mlp_weight))


def score_kernel(
    inv_ref,
    queries_ref,
    attended_ref,
    labels_ref,
    mlp_ref,
    logit_weight_ref,
    logits_ref,
    grad_att_ref,
    direct_ref,
    grad_pre_ref,
):
    users = inv_ref.shape[0]
    per_user = queries_ref.shape[0] // users
    step_users = math.gcd(users, 2)
    step_rows = step_users * per_user
    key_width = queries_ref.shape[1]
    weight = logit_weight_ref[...].astype(jnp.float32)
    for first in range(0, users, step_users):
        at = slice(first * per_user, first * per_user + step_rows)
        query_b = queries_ref[at, :]
        query_f = query_b.astype(jnp.float32)
        attended = attended_ref[at, :]
        joined = jnp.concatenate(
            [query_b, attended.astype(jnp.bfloat16), (query_f * attended).astype(jnp.bfloat16)],
            axis=1,
        )
        pre_act = dot(joined, mlp_ref[...])
        act_sig = 0.5 * jnp.tanh(0.5 * pre_act) + 0.5
        hidden_units = (pre_act * act_sig).astype(jnp.bfloat16)
        logits = jnp.sum(hidden_units.astype(jnp.float32) * weight, axis=1, keepdims=True)
        logits_ref[at, :] = logits
        dlogit = (0.5 * jnp.tanh(0.5 * logits) + 0.5) - labels_ref[at, :].astype(jnp.float32)
        slope = act_sig * (1.0 + pre_act * (1.0 - act_sig))
        grad_pre = (dlogit * weight * slope).astype(jnp.bfloat16)
        grad_pre_ref[at, :] = grad_pre
    djoined = dot_rows(grad_pre_ref[...], mlp_ref[...])
    part_att = djoined[:, key_width : 2 * key_width]
    part_prod = djoined[:, 2 * key_width :]
    for user in range(users):
        at = slice(user * per_user, (user + 1) * per_user)
        grad_att = part_att[at] + part_prod[at] * queries_ref[at, :].astype(jnp.float32)
        grad_att_ref[at, :] = (grad_att * inv_ref[user]).astype(jnp.bfloat16)
    direct_ref[...] = djoined[:, :key_width] + part_prod * attended_ref[...]


def score(inv_count, queries, attended, labels, mlp_weight, logit_weight):
    requests, key_width = queries.shape
    whole = pl.BlockSpec(memory_space=pltpu.VMEM)
    return pl.pallas_call(
        score_kernel,
        in_specs=[pl.BlockSpec(memory_space=pltpu.SMEM)] + [whole] * 5,
        out_specs=[whole] * 3,
        out_shape=[
            jax.ShapeDtypeStruct((requests, 1), jnp.float32),
            jax.ShapeDtypeStruct((requests, key_width), jnp.bfloat16),
            jax.ShapeDtypeStruct((requests, key_width), jnp.float32),
        ],
        scratch_shapes=[pltpu.VMEM((requests, mlp_weight.shape[1]), jnp.bfloat16)],
        compiler_params=pltpu.CompilerParams(vmem_limit_bytes=32 * MIB),
        cost_estimate=pl.CostEstimate(
            flops=4 * requests * mlp_weight.shape[0] * mlp_weight.shape[1],
            bytes_accessed=1 << 23,
            transcendentals=0,
        ),
        name="score",
    )(inv_count, queries, attended, labels, mlp_weight, logit_weight)


def attend_back_kernel(grad_att_ref, direct_ref, slope_ref, history_ref, grad_rows_ref):
    users, events, key_width = history_ref.shape
    per_user = grad_att_ref.shape[0] // users
    chunk = math.gcd(events, 1024)
    for user in range(users):
        rows = slice(user * per_user, (user + 1) * per_user)
        back = jnp.zeros((per_user, key_width), jnp.float32)
        for at in range(0, events, chunk):
            keys = history_ref[user, at : at + chunk, :]
            slope = slope_ref[rows, at : at + chunk].astype(jnp.float32)
            grad_sig = (dot_rows(grad_att_ref[rows, :], keys) * slope).astype(jnp.bfloat16)
            back += dot(grad_sig, keys)
        grad_rows = direct_ref[rows, :] + back * (1.0 / math.sqrt(key_width))
        grad_rows_ref[rows, :] = grad_rows.astype(jnp.bfloat16)


def attend_back(grad_att, direct, slope, history):
    _, events, key_width = history.shape
    requests = grad_att.shape[0]
    whole = pl.BlockSpec(memory_space=pltpu.VMEM)
    return pl.pallas_call(
        attend_back_kernel,
        in_specs=[whole] * 4,
        out_specs=whole,
        out_shape=jax.ShapeDtypeStruct((requests, key_width), jnp.bfloat16),
        compiler_params=pltpu.CompilerParams(vmem_limit_bytes=20 * MIB),
        cost_estimate=pl.CostEstimate(
            flops=4 * requests * events * key_width, bytes_accessed=1 << 23, transcendentals=0
        ),
        name="attend_back",
    )(grad_att, direct, slope, history)


def sum_rows(cands, at, slots_ref, grad_rows_ref):
    places = lax.broadcasted_iota(jnp.int32, (cands, slots_ref.shape[1]), 0) + at
    return dot((places == slots_ref[...]).astype(jnp.bfloat16), grad_rows_ref[...])


def cand_grad_kernel(slots_ref, grad_rows_ref, cand_grad_ref):
    cands = cand_grad_ref.shape[0]
    chunk = math.gcd(cands, 512)
    for at in range(0, cands, chunk):
        cand_grad_ref[at : at + chunk, :] = sum_rows(chunk, at, slots_ref, grad_rows_ref)


def own_cand_grad(cands, slots, grad_rows):
    requests, key_width = grad_rows.shape
    whole = pl.BlockSpec(memory_space=pltpu.VMEM)
    return pl.pallas_call(
        cand_grad_kernel,
        in_specs=[whole] * 2,
        out_specs=whole,
        out_shape=jax.ShapeDtypeStruct((cands, key_width), jnp.float32),
        compiler_params=pltpu.CompilerParams(vmem_limit_bytes=20 * MIB),
        cost_estimate=pl.CostEstimate(
            flops=2 * cands * key_width * requests, bytes_accessed=1 << 22, transcendentals=0
        ),
        name="own_cand_grad",
    )(slots, grad_rows)


def terms_kernel(
    origins, wide_ref, cand_grad_ref, slots_ref, grad_rows_ref, pooled_ref, out_ref, terms_ref
):
    cands = pooled_ref.shape[0]
    chunk = math.gcd(cands, 512)
    for at in range(0, cands, chunk):
        cand_grad = cand_grad_ref[at : at + chunk, :] + sum_rows(
            chunk, at, slots_ref, grad_rows_ref
        )
        term = dot_columns(pooled_ref[at : at + chunk, :], cand_grad.astype(jnp.bfloat16))
        if at == 0:
            terms_ref[...] = term
        else:
            terms_ref[...] += term
    rows = terms_ref.shape[0] // len(origins)
    wide = wide_ref[0]
    batch = max(1, 32 // rows)
    for slot in range(0, len(origins), batch):
        found = [
            terms_ref[pl.ds(pl.multiple_of((wide ^ origins[slot + i]) * rows, rows), rows), :]
            for i in range(batch)
        ]
        found = found[0] if batch == 1 else jnp.concatenate(found, axis=0)
        out_ref[slot * rows : (slot + batch) * rows, :] = found.astype(jnp.bfloat16)


def chip_terms(origins, wide, cand_grad, far_slots, far_grad_rows, pooled):
    cands, width = pooled.shape
    requests, key_width = far_grad_rows.shape
    whole = pl.BlockSpec(memory_space=pltpu.VMEM)
    return pl.pallas_call(
        functools.partial(terms_kernel, origins),
        in_specs=[pl.BlockSpec(memory_space=pltpu.SMEM)] + [whole] * 4,
        out_specs=whole,
        out_shape=jax.ShapeDtypeStruct((width, key_width), jnp.bfloat16),
        scratch_shapes=[pltpu.VMEM((width, key_width), jnp.float32)],
        compiler_params=pltpu.CompilerParams(vmem_limit_bytes=20 * MIB),
        cost_estimate=pl.CostEstimate(
            flops=2 * cands * key_width * (width + requests),
            bytes_accessed=1 << 22,
            transcendentals=0,
        ),
        name="chip_terms",
    )(wide, cand_grad, far_slots, far_grad_rows, pooled)


def bit_groups(size):
    groups = []
    bit = 0
    while (1 << bit) < size:
        values = min(4, size >> bit)
        groups.append((bit, values))
        bit += values.bit_length() - 1
    return groups


def exchange(values, axis_name, size, distance):
    return lax.ppermute(values, axis_name, [(i, i ^ distance) for i in range(size)])


def send_stage(rows, wides, bit, values):
    return [exchange(rows, "wide", wides, step << bit) for step in range(1, values)]


def after(values, *others):
    return lax.optimization_barrier((tuple(values),) + others)[0]


def slot_of(distance, wides):
    slot = 0
    for bit, values in bit_groups(wides):
        slot = slot * values + ((distance >> bit) & (values - 1))
    return slot


def sum_blocks(blocks, wides, logits):
    total = blocks
    for bit, values in bit_groups(wides):
        if bit > 0:
            total, logits = lax.optimization_barrier((total, logits))
        parts = total.astype(jnp.bfloat16).reshape((values, -1) + blocks.shape[1:])
        found = [
            exchange(parts[step], "wide", wides, step << bit).astype(jnp.float32)
            for step in range(1, values)
        ]
        total = sum(found, parts[0].astype(jnp.float32))
    return total, logits


def body(
    frames,
    qkv_weight,
    out_weight,
    proj_weight,
    mlp_weight,
    logit_weight,
    history,
    hist_len,
    hist_mask,
    req_owner,
    req_local,
    labels,
):
    wides = lax.axis_size("wide")
    core, wide = lax.axis_index("section"), lax.axis_index("wide")
    cand_count = frames.shape[0]
    requests = req_local.shape[0]
    users, events, _ = history.shape
    keep, send, embedded = encode_block(
        core.reshape(1), frames, qkv_weight, out_weight, proj_weight
    )
    positions = jnp.arange(events, dtype=jnp.int32)[None, :]
    usable = (
        (positions < hist_len[:, None]) & ((hist_mask == 1) | (positions == 0))
    ).astype(jnp.float32)
    inv_count = lax.rsqrt(jnp.sum(usable, axis=1))
    usable = usable.reshape(users, 1, events)
    owner_core = req_owner[:, 0] // wides
    owner_slot = slot_of((req_owner[:, 0] % wides) ^ wide, wides)
    slots = ((owner_core ^ core) * wides + owner_slot) * cand_count + req_local
    pooled_slots = (owner_slot * 2 + owner_core) * cand_count + req_local
    stages = list(reversed(bit_groups(wides)))
    near, pooled = embedded, None
    for place, stage in enumerate(stages):
        found = send_stage(near, wides, *stage)
        if place == 0:
            got = exchange(send, "section", 2, 1)
            far_slots = exchange(pooled_slots, "section", 2, 1)
            found, keep, got, far_slots = lax.optimization_barrier((found, keep, got, far_slots))
            pooled = jnp.where(
                core == 0,
                jnp.concatenate([keep, got], axis=0),
                jnp.concatenate([got, keep], axis=0),
            )
        else:
            found_pooled = send_stage(pooled, wides, *stages[place - 1])
            found, found_pooled = lax.optimization_barrier((found, found_pooled))
            pooled = jnp.concatenate([pooled] + found_pooled, axis=0)
        near = jnp.concatenate([near] + found, axis=0)
    far = exchange(near, "section", 2, 1)
    found_pooled = send_stage(pooled, wides, *stages[-1])
    queries, attended, slope, mlp_weight = attend(
        inv_count, slots.reshape(requests, 1), near, far, history, usable, mlp_weight
    )
    logits, grad_att, direct = score(
        inv_count,
        queries,
        attended,
        labels.reshape(requests, 1),
        mlp_weight,
        logit_weight.reshape(1, -1),
    )
    found_pooled, grad_att = lax.optimization_barrier((found_pooled, grad_att))
    grad_rows = attend_back(grad_att, direct, slope, history)
    far_grad_rows = exchange(grad_rows, "section", 2, 1)
    pooled = jnp.concatenate(after([pooled] + found_pooled, grad_rows), axis=0)
    cand_grad = own_cand_grad(pooled.shape[0], pooled_slots.reshape(1, requests), grad_rows)
    origins = [0] * wides
    for distance in range(wides):
        origins[slot_of(distance, wides)] = distance
    terms = chip_terms(
        origins,
        wide.reshape(1),
        cand_grad,
        far_slots.reshape(1, requests),
        far_grad_rows,
        pooled,
    )
    grad_proj, logits = sum_blocks(terms, wides, logits.reshape(requests))
    return (logits, grad_proj)


def solution(mesh):
    in_specs = (
        P(("section", "wide"), None, None),
        P(),
        P(),
        P(),
        P(),
        P(),
        P(("section", "wide"), None, None),
        P(("section", "wide")),
        P(("section", "wide"), None),
        P(("section", "wide"), None),
        P(("section", "wide")),
        P(("section", "wide")),
    )
    out_specs = (P(("section", "wide")), P(("section", "wide"), None))
    return jax.shard_map(body, mesh=mesh, in_specs=in_specs, out_specs=out_specs, check_vma=False)
```

```python
import functools
import math

import jax
import jax.numpy as jnp
from jax import lax
from jax.experimental import pallas as pl
from jax.experimental.pallas import tpu as pltpu
from jax.sharding import PartitionSpec as P

HEADS = 16
FRAMES = 3


EPSILON = 1e-06
MIB = 1024 * 1024


def layer_norm(values):
    center = values - jnp.mean(values, axis=-1, keepdims=True)
    spread = jnp.mean(jnp.square(center), axis=-1, keepdims=True)
    return center * lax.rsqrt(spread + EPSILON)


def dot(left, right):
    return jnp.dot(left, right, preferred_element_type=jnp.float32)


def dot_rows(left, right):
    return lax.dot_general(left, right, (((1,), (1,)), ((), ())), preferred_element_type=jnp.float32)


def dot_columns(left, right):
    return lax.dot_general(left, right, (((0,), (0,)), ((), ())), preferred_element_type=jnp.float32)


def split_rows(values):
    high = values.astype(jnp.bfloat16)
    low = (values - high.astype(jnp.float32)).astype(jnp.bfloat16)
    return jnp.concatenate([high, low], axis=0)


def dot_split(values, right):
    both = dot(split_rows(values), right)
    rows = values.shape[0]
    return both[:rows] + both[rows:]


def encode_kernel(
    tokens,
    core_ref,
    frames_hbm,
    qkv_hbm,
    out_hbm,
    proj_hbm,
    keep_ref,
    send_ref,
    embedded_ref,
    frames_ref,
    qkv_ref,
    out_ref,
    proj_ref,
    sems,
    normed_ref,
    packed_ref,
    scores_ref,
    mixed_rows_ref,
    sums_ref,
):
    total = embedded_ref.shape[0]
    rows, width = packed_ref.shape[0], packed_ref.shape[1] // 2
    cands = rows // tokens
    groups = total // cands
    head_dim = width // HEADS
    patches = tokens // FRAMES
    lanes = 2 * head_dim
    blocks = rows // lanes
    pairs = HEADS // 2
    quad = 4
    span = quad * head_dim

    def group_rows(group):
        return pl.ds(group * rows, rows)

    def columns(part):
        return pl.ds(part * width, width)

    pieces = [(frames_hbm.at[group_rows(0)], frames_ref.at[group_rows(0)])]
    pieces += [(qkv_hbm.at[:, columns(part)], qkv_ref.at[:, columns(part)]) for part in range(2)]
    pieces += [
        (frames_hbm.at[group_rows(group)], frames_ref.at[group_rows(group)])
        for group in range(1, groups)
    ]
    pieces += [(qkv_hbm.at[:, columns(2)], qkv_ref.at[:, columns(2)])]
    pieces += [(out_hbm, out_ref), (proj_hbm, proj_ref)]
    copies = [
        pltpu.make_async_copy(source, target, sems.at[place])
        for place, (source, target) in enumerate(pieces)
    ]
    copies[0].start()
    copies[1].start()

    def norm_cand(cand):
        at = slice(cand * tokens, (cand + 1) * tokens)
        inputs = frames_ref[at, :].astype(jnp.float32)
        normed_ref[at, :] = layer_norm(inputs).astype(jnp.bfloat16)
        sums_ref[cand] = jnp.sum(inputs, axis=0, keepdims=True)

    exponent = math.log2(math.e) / math.sqrt(head_dim)
    frame_at = (lax.broadcasted_iota(jnp.int32, (patches, quad * lanes), 1) % lanes) // patches
    nothing = jnp.zeros((head_dim, lanes), jnp.bfloat16)
    ones_row = lax.broadcasted_iota(jnp.int32, (2 * lanes, 2 * lanes), 0) // patches
    ones_column = lax.broadcasted_iota(jnp.int32, (2 * lanes, 2 * lanes), 1) // patches
    frame_ones = (ones_row == ones_column).astype(jnp.bfloat16)
    own = lax.broadcasted_iota(jnp.int32, (cands, rows), 1) // tokens == lax.broadcasted_iota(
        jnp.int32, (cands, rows), 0
    )

    def own_scores(block, head):
        block_rows = slice(block * lanes, (block + 1) * lanes)
        start = head * head_dim
        query = packed_ref[block_rows, start : start + span]
        keys = packed_ref[block_rows, width + start : width + start + span].T
        keys = jnp.concatenate(
            [
                jnp.concatenate(
                    [nothing] * place
                    + [keys[place * head_dim : (place + 1) * head_dim]]
                    + [nothing] * (quad - 1 - place),
                    axis=1,
                )
                for place in range(quad)
            ],
            axis=0,
        )
        scores = dot(query, keys)
        found = scores[:patches]
        for frame in range(1, lanes // patches):
            found = jnp.where(
                frame_at == frame, scores[frame * patches : (frame + 1) * patches], found
            )
        for side in range(quad // 2):
            scores_ref[block, head // 2 + side] = found[
                :, side * 2 * lanes : (side + 1) * 2 * lanes
            ]

    copies[0].wait()
    copies[2].start()
    for cand in range(cands):
        norm_cand(cand)
    copies[1].wait()
    for copy in copies[3 : 2 + groups]:
        copy.start()
    for group in range(groups):
        at = slice(group * rows, (group + 1) * rows)
        for part in range(2):
            if group == 0 and part == 1:
                copies[2].wait()
                for copy in copies[2 + groups :]:
                    copy.start()
            part_columns = slice(part * width, (part + 1) * width)
            packed_ref[:, part_columns] = dot(normed_ref[at, :], qkv_ref[:, part_columns]).astype(
                jnp.bfloat16
            )
        if group + 1 < groups:
            copies[3 + group].wait()
        for head in range(0, HEADS, quad):
            for block in range(blocks):
                own_scores(block, head)
            if group + 1 < groups:
                for cand in range(head * cands // HEADS, (head + quad) * cands // HEADS):
                    norm_cand((group + 1) * cands + cand)
        exp_scores = jnp.exp2(
            scores_ref[...].reshape(blocks * pairs * patches, 2 * lanes) * exponent
        )
        totals = dot(exp_scores.astype(jnp.bfloat16), frame_ones)
        probs = (exp_scores / totals).reshape(blocks * pairs, patches, 2 * lanes)
        sums = jnp.sum(probs, axis=1)
        key_sums = [
            jnp.concatenate(
                [
                    sums[block * pairs : (block + 1) * pairs, side * lanes : (side + 1) * lanes]
                    for block in range(blocks)
                ],
                axis=1,
            )
            for side in range(2)
        ]
        spread = jnp.concatenate(
            [
                jnp.where(own, key_sums[head % 2][head // 2 : head // 2 + 1], 0.0)
                for head in range(HEADS)
            ],
            axis=0,
        ).astype(jnp.bfloat16)
        mixed_rows = dot(spread, normed_ref[at, :])
        for head in range(HEADS):
            mixed_rows_ref[head, group * cands : (group + 1) * cands, :] = mixed_rows[
                head * cands : (head + 1) * cands
            ]

    for copy in copies[2 + groups :]:
        copy.wait()
    mixed = []
    for head in range(0, HEADS, quad):
        left = mixed_rows_ref[head : head + quad].reshape(quad * total, width)
        start = 2 * width + head * head_dim
        both = dot_split(left, qkv_ref[:, start : start + span])
        head_at = lax.broadcasted_iota(jnp.int32, (total, span), 1) // head_dim
        piece = jnp.zeros((total, span), jnp.float32)
        for place in range(quad):
            piece = jnp.where(head_at == place, both[place * total : (place + 1) * total], piece)
        mixed.append(piece)
    mixed_mean = jnp.concatenate(mixed, axis=1) * (1.0 / tokens)
    hidden = sums_ref[...].reshape(total, width) * (1.0 / tokens)
    hidden += dot_split(mixed_mean, out_ref[...])
    pooled = layer_norm(hidden).astype(jnp.bfloat16)
    first, second = pooled[:, : width // 2], pooled[:, width // 2 :]
    keep_ref[...] = jnp.where(core_ref[0] == 0, first, second)
    send_ref[...] = jnp.where(core_ref[0] == 0, second, first)
    embedded_ref[...] = dot(pooled, proj_ref[...]).astype(jnp.bfloat16)


def in_hbm(*arrays):
    return [pltpu.with_memory_space_constraint(array, pltpu.HBM) for array in arrays]


def encode_block(core, frames, qkv_weight, out_weight, proj_weight):
    cand_count, tokens, width = frames.shape
    key_width = proj_weight.shape[1]
    groups = 2
    rows = cand_count * tokens // groups
    lanes = 2 * width // HEADS
    patches = tokens // FRAMES
    flat = frames.reshape(cand_count * tokens, width)
    whole = pl.BlockSpec(memory_space=pltpu.VMEM)
    return pl.pallas_call(
        functools.partial(encode_kernel, tokens),
        in_specs=[pl.BlockSpec(memory_space=pltpu.SMEM)]
        + [pl.BlockSpec(memory_space=pltpu.HBM)] * 4,
        out_specs=[whole] * 3,
        out_shape=[
            jax.ShapeDtypeStruct((cand_count, width // 2), jnp.bfloat16),
            jax.ShapeDtypeStruct((cand_count, width // 2), jnp.bfloat16),
            jax.ShapeDtypeStruct((cand_count, key_width), jnp.bfloat16),
        ],
        scratch_shapes=[
            pltpu.VMEM(flat.shape, jnp.bfloat16),
            pltpu.VMEM(qkv_weight.shape, jnp.bfloat16),
            pltpu.VMEM(out_weight.shape, jnp.bfloat16),
            pltpu.VMEM(proj_weight.shape, jnp.bfloat16),
            pltpu.SemaphoreType.DMA((groups + 5,)),
            pltpu.VMEM(flat.shape, jnp.bfloat16),
            pltpu.VMEM((rows, 2 * width), jnp.bfloat16),
            pltpu.VMEM((rows // lanes, HEADS // 2, patches, 2 * lanes), jnp.float32),
            pltpu.VMEM((HEADS, cand_count, width), jnp.float32),
            pltpu.VMEM((cand_count, 1, width), jnp.float32),
        ],
        compiler_params=pltpu.CompilerParams(vmem_limit_bytes=44 * MIB),
        cost_estimate=pl.CostEstimate(
            flops=5 * cand_count * tokens * width * width, bytes_accessed=1 << 24, transcendentals=0
        ),
        name="encode",
    )(core, *in_hbm(flat, qkv_weight, out_weight, proj_weight))


def attend_kernel(
    inv_ref,
    slots_ref,
    near_ref,
    far_ref,
    usable_ref,
    history_hbm,
    mlp_hbm,
    queries_ref,
    attended_ref,
    slope_ref,
    mlp_ref,
    history_ref,
    sems,
):
    users, events, _ = history_ref.shape
    chunk = math.gcd(events, 1024)
    copies = [
        pltpu.make_async_copy(history_hbm.at[user], history_ref.at[user], sems.at[user])
        for user in range(users)
    ]
    copies.append(pltpu.make_async_copy(mlp_hbm, mlp_ref, sems.at[users]))
    for copy in copies[:2]:
        copy.start()
    slots = slots_ref[...]
    half, key_width = near_ref.shape
    places = lax.broadcasted_iota(jnp.int32, (slots.shape[0], half), 1)
    queries = dot((slots == places).astype(jnp.bfloat16), near_ref[...])
    queries += dot((slots == places + half).astype(jnp.bfloat16), far_ref[...])
    queries_ref[...] = queries.astype(jnp.bfloat16)
    per_user = slots.shape[0] // users
    for user in range(users):
        copies[user].wait()
        if user + 2 < len(copies):
            copies[user + 2].start()
        rows = slice(user * per_user, (user + 1) * per_user)
        attended = jnp.zeros((per_user, key_width), jnp.float32)
        for at in range(0, events, chunk):
            keys = history_ref[user, at : at + chunk, :]
            usable = usable_ref[user, :, at : at + chunk]
            scores = dot_rows(queries_ref[rows, :], keys)
            half_gate = 0.5 * jnp.tanh(scores * (0.5 / math.sqrt(key_width)))
            weights = (0.5 + half_gate) * usable
            slope_ref[rows, at : at + chunk] = (weights * (0.5 - half_gate)).astype(jnp.bfloat16)
            attended += dot(weights.astype(jnp.bfloat16), keys)
        attended_ref[rows, :] = attended * inv_ref[user]
    copies[users].wait()


def attend(inv_count, slots, near, far, history, usable, mlp_weight):
    users, events, key_width = history.shape
    requests = slots.shape[0]
    whole = pl.BlockSpec(memory_space=pltpu.VMEM)
    return pl.pallas_call(
        attend_kernel,
        in_specs=[pl.BlockSpec(memory_space=pltpu.SMEM)]
        + [whole] * 4
        + [pl.BlockSpec(memory_space=pltpu.HBM)] * 2,
        out_specs=[whole] * 4,
        out_shape=[
            jax.ShapeDtypeStruct((requests, key_width), jnp.bfloat16),
            jax.ShapeDtypeStruct((requests, key_width), jnp.float32),
            jax.ShapeDtypeStruct((requests, events), jnp.bfloat16),
            pltpu.VMEM(mlp_weight.shape, mlp_weight.dtype),
        ],
        scratch_shapes=[
            pltpu.VMEM(history.shape, history.dtype),
            pltpu.SemaphoreType.DMA((users + 1,)),
        ],
        compiler_params=pltpu.CompilerParams(vmem_limit_bytes=32 * MIB),
        cost_estimate=pl.CostEstimate(
            flops=4 * requests * events * key_width, bytes_accessed=1 << 24, transcendentals=0
        ),
        name="attend",
    )(inv_count, slots, near, far, usable, *in_hbm(history, mlp_weight))


def score_kernel(
    inv_ref,
    queries_ref,
    attended_ref,
    labels_ref,
    mlp_ref,
    logit_weight_ref,
    logits_ref,
    grad_att_ref,
    direct_ref,
    grad_pre_ref,
):
    users = inv_ref.shape[0]
    per_user = queries_ref.shape[0] // users
    step_users = math.gcd(users, 2)
    step_rows = step_users * per_user
    key_width = queries_ref.shape[1]
    weight = logit_weight_ref[...].astype(jnp.float32)
    for first in range(0, users, step_users):
        at = slice(first * per_user, first * per_user + step_rows)
        query_b = queries_ref[at, :]
        query_f = query_b.astype(jnp.float32)
        attended = attended_ref[at, :]
        joined = jnp.concatenate(
            [query_b, attended.astype(jnp.bfloat16), (query_f * attended).astype(jnp.bfloat16)],
            axis=1,
        )
        pre_act = dot(joined, mlp_ref[...])
        act_sig = 0.5 * jnp.tanh(0.5 * pre_act) + 0.5
        hidden_units = (pre_act * act_sig).astype(jnp.bfloat16)
        logits = jnp.sum(hidden_units.astype(jnp.float32) * weight, axis=1, keepdims=True)
        logits_ref[at, :] = logits
        dlogit = (0.5 * jnp.tanh(0.5 * logits) + 0.5) - labels_ref[at, :].astype(jnp.float32)
        slope = act_sig * (1.0 + pre_act * (1.0 - act_sig))
        grad_pre = (dlogit * weight * slope).astype(jnp.bfloat16)
        grad_pre_ref[at, :] = grad_pre
    djoined = dot_rows(grad_pre_ref[...], mlp_ref[...])
    part_att = djoined[:, key_width : 2 * key_width]
    part_prod = djoined[:, 2 * key_width :]
    for user in range(users):
        at = slice(user * per_user, (user + 1) * per_user)
        grad_att = part_att[at] + part_prod[at] * queries_ref[at, :].astype(jnp.float32)
        grad_att_ref[at, :] = (grad_att * inv_ref[user]).astype(jnp.bfloat16)
    direct_ref[...] = djoined[:, :key_width] + part_prod * attended_ref[...]


def score(inv_count, queries, attended, labels, mlp_weight, logit_weight):
    requests, key_width = queries.shape
    whole = pl.BlockSpec(memory_space=pltpu.VMEM)
    return pl.pallas_call(
        score_kernel,
        in_specs=[pl.BlockSpec(memory_space=pltpu.SMEM)] + [whole] * 5,
        out_specs=[whole] * 3,
        out_shape=[
            jax.ShapeDtypeStruct((requests, 1), jnp.float32),
            jax.ShapeDtypeStruct((requests, key_width), jnp.bfloat16),
            jax.ShapeDtypeStruct((requests, key_width), jnp.float32),
        ],
        scratch_shapes=[pltpu.VMEM((requests, mlp_weight.shape[1]), jnp.bfloat16)],
        compiler_params=pltpu.CompilerParams(vmem_limit_bytes=32 * MIB),
        cost_estimate=pl.CostEstimate(
            flops=4 * requests * mlp_weight.shape[0] * mlp_weight.shape[1],
            bytes_accessed=1 << 23,
            transcendentals=0,
        ),
        name="score",
    )(inv_count, queries, attended, labels, mlp_weight, logit_weight)


def attend_back_kernel(first, grad_att_ref, direct_ref, slope_ref, history_ref, grad_rows_ref):
    users, events, key_width = history_ref.shape
    per_user = grad_att_ref.shape[0] // users
    chunk = math.gcd(events, 1024)
    for user in range(grad_rows_ref.shape[0] // per_user):
        rows = slice((first + user) * per_user, (first + user + 1) * per_user)
        back = jnp.zeros((per_user, key_width), jnp.float32)
        for at in range(0, events, chunk):
            keys = history_ref[first + user, at : at + chunk, :]
            slope = slope_ref[rows, at : at + chunk].astype(jnp.float32)
            grad_sig = (dot_rows(grad_att_ref[rows, :], keys) * slope).astype(jnp.bfloat16)
            back += dot(grad_sig, keys)
        grad_rows = direct_ref[rows, :] + back * (1.0 / math.sqrt(key_width))
        grad_rows_ref[user * per_user : (user + 1) * per_user, :] = grad_rows.astype(jnp.bfloat16)


def attend_back(first, count, grad_att, direct, slope, history):
    users, events, key_width = history.shape
    per_user = grad_att.shape[0] // users
    whole = pl.BlockSpec(memory_space=pltpu.VMEM)
    return pl.pallas_call(
        functools.partial(attend_back_kernel, first),
        in_specs=[whole] * 4,
        out_specs=whole,
        out_shape=jax.ShapeDtypeStruct((count * per_user, key_width), jnp.bfloat16),
        compiler_params=pltpu.CompilerParams(vmem_limit_bytes=20 * MIB),
        cost_estimate=pl.CostEstimate(
            flops=4 * count * per_user * events * key_width,
            bytes_accessed=1 << 23,
            transcendentals=0,
        ),
        name="attend_back",
    )(grad_att, direct, slope, history)


def join_rows(parts, joined_ref):
    at = 0
    for part in parts:
        joined_ref[at : at + part.shape[0], :] = part[...]
        at += part.shape[0]


def sum_rows(cands, at, slots_ref, grad_rows_ref):
    places = lax.broadcasted_iota(jnp.int32, (cands, slots_ref.shape[1]), 0) + at
    return dot((places == slots_ref[...]).astype(jnp.bfloat16), grad_rows_ref[...])


def cand_grad_kernel(slots_ref, first_ref, second_ref, cand_grad_ref, grad_rows_ref):
    join_rows((first_ref, second_ref), grad_rows_ref)
    cands = cand_grad_ref.shape[0]
    chunk = math.gcd(cands, 512)
    for at in range(0, cands, chunk):
        cand_grad_ref[at : at + chunk, :] = sum_rows(chunk, at, slots_ref, grad_rows_ref)


def own_cand_grad(cands, slots, grad_parts):
    requests, key_width = slots.shape[1], grad_parts[0].shape[1]
    whole = pl.BlockSpec(memory_space=pltpu.VMEM)
    return pl.pallas_call(
        cand_grad_kernel,
        in_specs=[whole] * 3,
        out_specs=whole,
        out_shape=jax.ShapeDtypeStruct((cands, key_width), jnp.float32),
        scratch_shapes=[pltpu.VMEM((requests, key_width), jnp.bfloat16)],
        compiler_params=pltpu.CompilerParams(vmem_limit_bytes=20 * MIB),
        cost_estimate=pl.CostEstimate(
            flops=2 * cands * key_width * requests, bytes_accessed=1 << 22, transcendentals=0
        ),
        name="own_cand_grad",
    )(slots, *grad_parts)


def terms_kernel(
    origins,
    wide_ref,
    cand_grad_ref,
    slots_ref,
    first_ref,
    second_ref,
    pooled_ref,
    out_ref,
    grad_rows_ref,
    terms_ref,
):
    join_rows((first_ref, second_ref), grad_rows_ref)
    cands = pooled_ref.shape[0]
    chunk = math.gcd(cands, 512)
    for at in range(0, cands, chunk):
        cand_grad = cand_grad_ref[at : at + chunk, :] + sum_rows(
            chunk, at, slots_ref, grad_rows_ref
        )
        term = dot_columns(pooled_ref[at : at + chunk, :], cand_grad.astype(jnp.bfloat16))
        if at == 0:
            terms_ref[...] = term
        else:
            terms_ref[...] += term
    rows = terms_ref.shape[0] // len(origins)
    wide = wide_ref[0]
    batch = max(1, 32 // rows)
    for slot in range(0, len(origins), batch):
        found = [
            terms_ref[pl.ds(pl.multiple_of((wide ^ origins[slot + i]) * rows, rows), rows), :]
            for i in range(batch)
        ]
        found = found[0] if batch == 1 else jnp.concatenate(found, axis=0)
        out_ref[slot * rows : (slot + batch) * rows, :] = found.astype(jnp.bfloat16)


def chip_terms(origins, wide, cand_grad, far_slots, far_parts, pooled):
    cands, width = pooled.shape
    requests, key_width = far_slots.shape[1], cand_grad.shape[1]
    whole = pl.BlockSpec(memory_space=pltpu.VMEM)
    return pl.pallas_call(
        functools.partial(terms_kernel, origins),
        in_specs=[pl.BlockSpec(memory_space=pltpu.SMEM)] + [whole] * 5,
        out_specs=whole,
        out_shape=jax.ShapeDtypeStruct((width, key_width), jnp.bfloat16),
        scratch_shapes=[
            pltpu.VMEM((requests, key_width), jnp.bfloat16),
            pltpu.VMEM((width, key_width), jnp.float32),
        ],
        compiler_params=pltpu.CompilerParams(vmem_limit_bytes=20 * MIB),
        cost_estimate=pl.CostEstimate(
            flops=2 * cands * key_width * (width + requests),
            bytes_accessed=1 << 22,
            transcendentals=0,
        ),
        name="chip_terms",
    )(wide, cand_grad, far_slots, *far_parts, pooled)


def bit_groups(size):
    groups = []
    bit = 0
    while (1 << bit) < size:
        values = min(4, size >> bit)
        groups.append((bit, values))
        bit += values.bit_length() - 1
    return groups


def exchange(values, axis_name, size, distance):
    return lax.ppermute(values, axis_name, [(i, i ^ distance) for i in range(size)])


def send_stage(rows, wides, bit, values):
    return [exchange(rows, "wide", wides, step << bit) for step in range(1, values)]


def after(values, *others):
    return lax.optimization_barrier((tuple(values),) + others)[0]


def slot_of(distance, wides):
    slot = 0
    for bit, values in bit_groups(wides):
        slot = slot * values + ((distance >> bit) & (values - 1))
    return slot


def sum_blocks(blocks, wides, logits):
    total = blocks
    for bit, values in bit_groups(wides):
        if bit > 0:
            total, logits = lax.optimization_barrier((total, logits))
        parts = total.astype(jnp.bfloat16).reshape((values, -1) + blocks.shape[1:])
        found = [
            exchange(parts[step], "wide", wides, step << bit).astype(jnp.float32)
            for step in range(1, values)
        ]
        total = sum(found, parts[0].astype(jnp.float32))
    return total, logits


def body(
    frames,
    qkv_weight,
    out_weight,
    proj_weight,
    mlp_weight,
    logit_weight,
    history,
    hist_len,
    hist_mask,
    req_owner,
    req_local,
    labels,
):
    wides = lax.axis_size("wide")
    core, wide = lax.axis_index("section"), lax.axis_index("wide")
    cand_count = frames.shape[0]
    requests = req_local.shape[0]
    users, events, _ = history.shape
    keep, send, embedded = encode_block(
        core.reshape(1), frames, qkv_weight, out_weight, proj_weight
    )
    positions = jnp.arange(events, dtype=jnp.int32)[None, :]
    usable = (
        (positions < hist_len[:, None]) & ((hist_mask == 1) | (positions == 0))
    ).astype(jnp.float32)
    inv_count = lax.rsqrt(jnp.sum(usable, axis=1))
    usable = usable.reshape(users, 1, events)
    owner_core = req_owner[:, 0] // wides
    owner_slot = slot_of((req_owner[:, 0] % wides) ^ wide, wides)
    slots = ((owner_core ^ core) * wides + owner_slot) * cand_count + req_local
    pooled_slots = (owner_slot * 2 + owner_core) * cand_count + req_local
    stages = list(reversed(bit_groups(wides)))
    near, pooled = embedded, None
    for place, stage in enumerate(stages):
        found = send_stage(near, wides, *stage)
        if place == 0:
            got = exchange(send, "section", 2, 1)
            far_slots = exchange(pooled_slots, "section", 2, 1)
            found, keep, got, far_slots = lax.optimization_barrier((found, keep, got, far_slots))
            pooled = jnp.where(
                core == 0,
                jnp.concatenate([keep, got], axis=0),
                jnp.concatenate([got, keep], axis=0),
            )
        else:
            bit, values = stages[place - 1]
            early = send_stage(pooled, wides, bit, values - 1)
            found, early = lax.optimization_barrier((found, early))
            late = exchange(after([pooled], *found)[0], "wide", wides, (values - 1) << bit)
            if place + 1 < len(stages):
                pooled = jnp.concatenate([pooled] + early + [late], axis=0)
        near = jnp.concatenate([near] + found, axis=0)
    far = exchange(near, "section", 2, 1)
    queries, attended, slope, mlp_weight = attend(
        inv_count, slots.reshape(requests, 1), near, far, history, usable, mlp_weight
    )
    pooled = jnp.concatenate(after([pooled] + early + [late], attended), axis=0)
    found_pooled = send_stage(pooled, wides, *stages[-1])
    logits, grad_att, direct = score(
        inv_count,
        queries,
        attended,
        labels.reshape(requests, 1),
        mlp_weight,
        logit_weight.reshape(1, -1),
    )
    half = users // 2
    first_rows = attend_back(0, half, grad_att, direct, slope, history)
    found_pooled, grad_att, first_rows = lax.optimization_barrier(
        (found_pooled, grad_att, first_rows)
    )
    pooled = jnp.concatenate([pooled] + found_pooled, axis=0)
    grad_parts = [first_rows, attend_back(half, users - half, grad_att, direct, slope, history)]
    far_parts = [exchange(part, "section", 2, 1) for part in grad_parts]
    cand_grad = own_cand_grad(pooled.shape[0], pooled_slots.reshape(1, requests), grad_parts)
    origins = [0] * wides
    for distance in range(wides):
        origins[slot_of(distance, wides)] = distance
    terms = chip_terms(
        origins,
        wide.reshape(1),
        cand_grad,
        far_slots.reshape(1, requests),
        far_parts,
        pooled,
    )
    grad_proj, logits = sum_blocks(terms, wides, logits.reshape(requests))
    return (logits, grad_proj)


def solution(mesh):
    in_specs = (
        P(("section", "wide"), None, None),
        P(),
        P(),
        P(),
        P(),
        P(),
        P(("section", "wide"), None, None),
        P(("section", "wide")),
        P(("section", "wide"), None),
        P(("section", "wide"), None),
        P(("section", "wide")),
        P(("section", "wide")),
    )
    out_specs = (P(("section", "wide")), P(("section", "wide"), None))
    return jax.shard_map(body, mesh=mesh, in_specs=in_specs, out_specs=out_specs, check_vma=False)
```

```python
import functools
import math

import jax
import jax.numpy as jnp
from jax import lax
from jax.experimental import pallas as pl
from jax.experimental.pallas import tpu as pltpu
from jax.sharding import PartitionSpec as P

HEADS = 16
FRAMES = 3


EPSILON = 1e-06
MIB = 1024 * 1024


def layer_norm(values):
    center = values - jnp.mean(values, axis=-1, keepdims=True)
    spread = jnp.mean(jnp.square(center), axis=-1, keepdims=True)
    return center * lax.rsqrt(spread + EPSILON)


def dot(left, right):
    return jnp.dot(left, right, preferred_element_type=jnp.float32)


def dot_rows(left, right):
    return lax.dot_general(left, right, (((1,), (1,)), ((), ())), preferred_element_type=jnp.float32)


def dot_columns(left, right):
    return lax.dot_general(left, right, (((0,), (0,)), ((), ())), preferred_element_type=jnp.float32)


def split_rows(values):
    high = values.astype(jnp.bfloat16)
    low = (values - high.astype(jnp.float32)).astype(jnp.bfloat16)
    return jnp.concatenate([high, low], axis=0)


def dot_split(values, right):
    both = dot(split_rows(values), right)
    rows = values.shape[0]
    return both[:rows] + both[rows:]


def encode_kernel(
    tokens,
    core_ref,
    frames_hbm,
    qkv_hbm,
    out_hbm,
    proj_hbm,
    keep_ref,
    send_ref,
    embedded_ref,
    frames_ref,
    qkv_ref,
    out_ref,
    proj_ref,
    sems,
    normed_ref,
    packed_ref,
    scores_ref,
    mixed_rows_ref,
    sums_ref,
):
    total = embedded_ref.shape[0]
    rows, width = packed_ref.shape[0], packed_ref.shape[1] // 2
    cands = rows // tokens
    groups = total // cands
    head_dim = width // HEADS
    patches = tokens // FRAMES
    lanes = 2 * head_dim
    blocks = rows // lanes
    pairs = HEADS // 2
    quad = 4
    span = quad * head_dim

    def group_rows(group):
        return pl.ds(group * rows, rows)

    def columns(part):
        return pl.ds(part * width, width)

    pieces = [(frames_hbm.at[group_rows(0)], frames_ref.at[group_rows(0)])]
    pieces += [(qkv_hbm.at[:, columns(part)], qkv_ref.at[:, columns(part)]) for part in range(2)]
    pieces += [
        (frames_hbm.at[group_rows(group)], frames_ref.at[group_rows(group)])
        for group in range(1, groups)
    ]
    pieces += [(qkv_hbm.at[:, columns(2)], qkv_ref.at[:, columns(2)])]
    pieces += [(out_hbm, out_ref), (proj_hbm, proj_ref)]
    copies = [
        pltpu.make_async_copy(source, target, sems.at[place])
        for place, (source, target) in enumerate(pieces)
    ]
    copies[0].start()
    copies[1].start()

    def norm_cand(cand):
        at = slice(cand * tokens, (cand + 1) * tokens)
        inputs = frames_ref[at, :].astype(jnp.float32)
        normed_ref[at, :] = layer_norm(inputs).astype(jnp.bfloat16)
        sums_ref[cand] = jnp.sum(inputs, axis=0, keepdims=True)

    exponent = math.log2(math.e) / math.sqrt(head_dim)
    frame_at = (lax.broadcasted_iota(jnp.int32, (patches, quad * lanes), 1) % lanes) // patches
    nothing = jnp.zeros((head_dim, lanes), jnp.bfloat16)
    ones_row = lax.broadcasted_iota(jnp.int32, (2 * lanes, 2 * lanes), 0) // patches
    ones_column = lax.broadcasted_iota(jnp.int32, (2 * lanes, 2 * lanes), 1) // patches
    frame_ones = (ones_row == ones_column).astype(jnp.bfloat16)
    own = lax.broadcasted_iota(jnp.int32, (cands, rows), 1) // tokens == lax.broadcasted_iota(
        jnp.int32, (cands, rows), 0
    )

    def own_scores(block, head):
        block_rows = slice(block * lanes, (block + 1) * lanes)
        start = head * head_dim
        query = packed_ref[block_rows, start : start + span]
        keys = packed_ref[block_rows, width + start : width + start + span].T
        keys = jnp.concatenate(
            [
                jnp.concatenate(
                    [nothing] * place
                    + [keys[place * head_dim : (place + 1) * head_dim]]
                    + [nothing] * (quad - 1 - place),
                    axis=1,
                )
                for place in range(quad)
            ],
            axis=0,
        )
        scores = dot(query, keys)
        found = scores[:patches]
        for frame in range(1, lanes // patches):
            found = jnp.where(
                frame_at == frame, scores[frame * patches : (frame + 1) * patches], found
            )
        for side in range(quad // 2):
            scores_ref[block, head // 2 + side] = found[
                :, side * 2 * lanes : (side + 1) * 2 * lanes
            ]

    copies[0].wait()
    copies[2].start()
    for cand in range(cands):
        norm_cand(cand)
    copies[1].wait()
    for copy in copies[3 : 2 + groups]:
        copy.start()
    for group in range(groups):
        at = slice(group * rows, (group + 1) * rows)
        for part in range(2):
            if group == 0 and part == 1:
                copies[2].wait()
                for copy in copies[2 + groups :]:
                    copy.start()
            part_columns = slice(part * width, (part + 1) * width)
            packed_ref[:, part_columns] = dot(normed_ref[at, :], qkv_ref[:, part_columns]).astype(
                jnp.bfloat16
            )
        if group + 1 < groups:
            copies[3 + group].wait()
        for head in range(0, HEADS, quad):
            for block in range(blocks):
                own_scores(block, head)
            if group + 1 < groups:
                for cand in range(head * cands // HEADS, (head + quad) * cands // HEADS):
                    norm_cand((group + 1) * cands + cand)
        exp_scores = jnp.exp2(
            scores_ref[...].reshape(blocks * pairs * patches, 2 * lanes) * exponent
        )
        totals = dot(exp_scores.astype(jnp.bfloat16), frame_ones)
        probs = (exp_scores / totals).reshape(blocks * pairs, patches, 2 * lanes)
        sums = jnp.sum(probs, axis=1)
        key_sums = [
            jnp.concatenate(
                [
                    sums[block * pairs : (block + 1) * pairs, side * lanes : (side + 1) * lanes]
                    for block in range(blocks)
                ],
                axis=1,
            )
            for side in range(2)
        ]
        spread = jnp.concatenate(
            [
                jnp.where(own, key_sums[head % 2][head // 2 : head // 2 + 1], 0.0)
                for head in range(HEADS)
            ],
            axis=0,
        ).astype(jnp.bfloat16)
        mixed_rows = dot(spread, normed_ref[at, :])
        for head in range(HEADS):
            mixed_rows_ref[head, group * cands : (group + 1) * cands, :] = mixed_rows[
                head * cands : (head + 1) * cands
            ]

    for copy in copies[2 + groups :]:
        copy.wait()
    mixed = []
    for head in range(0, HEADS, quad):
        left = mixed_rows_ref[head : head + quad].reshape(quad * total, width)
        start = 2 * width + head * head_dim
        both = dot_split(left, qkv_ref[:, start : start + span])
        head_at = lax.broadcasted_iota(jnp.int32, (total, span), 1) // head_dim
        piece = jnp.zeros((total, span), jnp.float32)
        for place in range(quad):
            piece = jnp.where(head_at == place, both[place * total : (place + 1) * total], piece)
        mixed.append(piece)
    mixed_mean = jnp.concatenate(mixed, axis=1) * (1.0 / tokens)
    hidden = sums_ref[...].reshape(total, width) * (1.0 / tokens)
    hidden += dot_split(mixed_mean, out_ref[...])
    pooled = layer_norm(hidden).astype(jnp.bfloat16)
    first, second = pooled[:, : width // 2], pooled[:, width // 2 :]
    keep_ref[...] = jnp.where(core_ref[0] == 0, first, second)
    send_ref[...] = jnp.where(core_ref[0] == 0, second, first)
    embedded_ref[...] = dot(pooled, proj_ref[...]).astype(jnp.bfloat16)


def in_hbm(*arrays):
    return [pltpu.with_memory_space_constraint(array, pltpu.HBM) for array in arrays]


def encode_block(core, frames, qkv_weight, out_weight, proj_weight):
    cand_count, tokens, width = frames.shape
    key_width = proj_weight.shape[1]
    groups = 2
    rows = cand_count * tokens // groups
    lanes = 2 * width // HEADS
    patches = tokens // FRAMES
    flat = frames.reshape(cand_count * tokens, width)
    whole = pl.BlockSpec(memory_space=pltpu.VMEM)
    return pl.pallas_call(
        functools.partial(encode_kernel, tokens),
        in_specs=[pl.BlockSpec(memory_space=pltpu.SMEM)]
        + [pl.BlockSpec(memory_space=pltpu.HBM)] * 4,
        out_specs=[whole] * 3,
        out_shape=[
            jax.ShapeDtypeStruct((cand_count, width // 2), jnp.bfloat16),
            jax.ShapeDtypeStruct((cand_count, width // 2), jnp.bfloat16),
            jax.ShapeDtypeStruct((cand_count, key_width), jnp.bfloat16),
        ],
        scratch_shapes=[
            pltpu.VMEM(flat.shape, jnp.bfloat16),
            pltpu.VMEM(qkv_weight.shape, jnp.bfloat16),
            pltpu.VMEM(out_weight.shape, jnp.bfloat16),
            pltpu.VMEM(proj_weight.shape, jnp.bfloat16),
            pltpu.SemaphoreType.DMA((groups + 5,)),
            pltpu.VMEM(flat.shape, jnp.bfloat16),
            pltpu.VMEM((rows, 2 * width), jnp.bfloat16),
            pltpu.VMEM((rows // lanes, HEADS // 2, patches, 2 * lanes), jnp.float32),
            pltpu.VMEM((HEADS, cand_count, width), jnp.float32),
            pltpu.VMEM((cand_count, 1, width), jnp.float32),
        ],
        compiler_params=pltpu.CompilerParams(vmem_limit_bytes=44 * MIB),
        cost_estimate=pl.CostEstimate(
            flops=5 * cand_count * tokens * width * width, bytes_accessed=1 << 24, transcendentals=0
        ),
        name="encode",
    )(core, *in_hbm(flat, qkv_weight, out_weight, proj_weight))


def attend_kernel(
    inv_ref,
    slots_ref,
    near_ref,
    far_ref,
    usable_ref,
    history_hbm,
    mlp_hbm,
    queries_ref,
    attended_ref,
    slope_ref,
    mlp_ref,
    history_ref,
    sems,
):
    users, events, _ = history_ref.shape
    chunk = math.gcd(events, 1024)
    copies = [
        pltpu.make_async_copy(history_hbm.at[user], history_ref.at[user], sems.at[user])
        for user in range(users)
    ]
    copies.append(pltpu.make_async_copy(mlp_hbm, mlp_ref, sems.at[users]))
    for copy in copies[:2]:
        copy.start()
    slots = slots_ref[...]
    half, key_width = near_ref.shape
    places = lax.broadcasted_iota(jnp.int32, (slots.shape[0], half), 1)
    queries = dot((slots == places).astype(jnp.bfloat16), near_ref[...])
    queries += dot((slots == places + half).astype(jnp.bfloat16), far_ref[...])
    queries_ref[...] = queries.astype(jnp.bfloat16)
    per_user = slots.shape[0] // users
    for user in range(users):
        copies[user].wait()
        if user + 2 < len(copies):
            copies[user + 2].start()
        rows = slice(user * per_user, (user + 1) * per_user)
        attended = jnp.zeros((per_user, key_width), jnp.float32)
        for at in range(0, events, chunk):
            keys = history_ref[user, at : at + chunk, :]
            usable = usable_ref[user, :, at : at + chunk]
            scores = dot_rows(queries_ref[rows, :], keys)
            half_gate = 0.5 * jnp.tanh(scores * (0.5 / math.sqrt(key_width)))
            weights = (0.5 + half_gate) * usable
            slope_ref[rows, at : at + chunk] = (weights * (0.5 - half_gate)).astype(jnp.bfloat16)
            attended += dot(weights.astype(jnp.bfloat16), keys)
        attended_ref[rows, :] = attended * inv_ref[user]
    copies[users].wait()


def attend(inv_count, slots, near, far, history, usable, mlp_weight):
    users, events, key_width = history.shape
    requests = slots.shape[0]
    whole = pl.BlockSpec(memory_space=pltpu.VMEM)
    return pl.pallas_call(
        attend_kernel,
        in_specs=[pl.BlockSpec(memory_space=pltpu.SMEM)]
        + [whole] * 4
        + [pl.BlockSpec(memory_space=pltpu.HBM)] * 2,
        out_specs=[whole] * 4,
        out_shape=[
            jax.ShapeDtypeStruct((requests, key_width), jnp.bfloat16),
            jax.ShapeDtypeStruct((requests, key_width), jnp.float32),
            jax.ShapeDtypeStruct((requests, events), jnp.bfloat16),
            pltpu.VMEM(mlp_weight.shape, mlp_weight.dtype),
        ],
        scratch_shapes=[
            pltpu.VMEM(history.shape, history.dtype),
            pltpu.SemaphoreType.DMA((users + 1,)),
        ],
        compiler_params=pltpu.CompilerParams(vmem_limit_bytes=32 * MIB),
        cost_estimate=pl.CostEstimate(
            flops=4 * requests * events * key_width, bytes_accessed=1 << 24, transcendentals=0
        ),
        name="attend",
    )(inv_count, slots, near, far, usable, *in_hbm(history, mlp_weight))


def score_kernel(
    inv_ref,
    queries_ref,
    attended_ref,
    labels_ref,
    mlp_ref,
    logit_weight_ref,
    logits_ref,
    grad_att_ref,
    direct_ref,
    grad_pre_ref,
):
    users = inv_ref.shape[0]
    per_user = queries_ref.shape[0] // users
    step_users = math.gcd(users, 2)
    step_rows = step_users * per_user
    key_width = queries_ref.shape[1]
    weight = logit_weight_ref[...].astype(jnp.float32)
    for first in range(0, users, step_users):
        at = slice(first * per_user, first * per_user + step_rows)
        query_b = queries_ref[at, :]
        query_f = query_b.astype(jnp.float32)
        attended = attended_ref[at, :]
        joined = jnp.concatenate(
            [query_b, attended.astype(jnp.bfloat16), (query_f * attended).astype(jnp.bfloat16)],
            axis=1,
        )
        pre_act = dot(joined, mlp_ref[...])
        act_sig = 0.5 * jnp.tanh(0.5 * pre_act) + 0.5
        hidden_units = (pre_act * act_sig).astype(jnp.bfloat16)
        logits = jnp.sum(hidden_units.astype(jnp.float32) * weight, axis=1, keepdims=True)
        logits_ref[at, :] = logits
        dlogit = (0.5 * jnp.tanh(0.5 * logits) + 0.5) - labels_ref[at, :].astype(jnp.float32)
        slope = act_sig * (1.0 + pre_act * (1.0 - act_sig))
        grad_pre = (dlogit * weight * slope).astype(jnp.bfloat16)
        grad_pre_ref[at, :] = grad_pre
    djoined = dot_rows(grad_pre_ref[...], mlp_ref[...])
    part_att = djoined[:, key_width : 2 * key_width]
    part_prod = djoined[:, 2 * key_width :]
    for user in range(users):
        at = slice(user * per_user, (user + 1) * per_user)
        grad_att = part_att[at] + part_prod[at] * queries_ref[at, :].astype(jnp.float32)
        grad_att_ref[at, :] = (grad_att * inv_ref[user]).astype(jnp.bfloat16)
    direct_ref[...] = djoined[:, :key_width] + part_prod * attended_ref[...]


def score(inv_count, queries, attended, labels, mlp_weight, logit_weight):
    requests, key_width = queries.shape
    whole = pl.BlockSpec(memory_space=pltpu.VMEM)
    return pl.pallas_call(
        score_kernel,
        in_specs=[pl.BlockSpec(memory_space=pltpu.SMEM)] + [whole] * 5,
        out_specs=[whole] * 3,
        out_shape=[
            jax.ShapeDtypeStruct((requests, 1), jnp.float32),
            jax.ShapeDtypeStruct((requests, key_width), jnp.bfloat16),
            jax.ShapeDtypeStruct((requests, key_width), jnp.float32),
        ],
        scratch_shapes=[pltpu.VMEM((requests, mlp_weight.shape[1]), jnp.bfloat16)],
        compiler_params=pltpu.CompilerParams(vmem_limit_bytes=32 * MIB),
        cost_estimate=pl.CostEstimate(
            flops=4 * requests * mlp_weight.shape[0] * mlp_weight.shape[1],
            bytes_accessed=1 << 23,
            transcendentals=0,
        ),
        name="score",
    )(inv_count, queries, attended, labels, mlp_weight, logit_weight)


def attend_back_kernel(first, grad_att_ref, direct_ref, slope_ref, history_ref, grad_rows_ref):
    users, events, key_width = history_ref.shape
    per_user = grad_att_ref.shape[0] // users
    chunk = math.gcd(events, 1024)
    for user in range(grad_rows_ref.shape[0] // per_user):
        rows = slice((first + user) * per_user, (first + user + 1) * per_user)
        back = jnp.zeros((per_user, key_width), jnp.float32)
        for at in range(0, events, chunk):
            keys = history_ref[first + user, at : at + chunk, :]
            slope = slope_ref[rows, at : at + chunk].astype(jnp.float32)
            grad_sig = (dot_rows(grad_att_ref[rows, :], keys) * slope).astype(jnp.bfloat16)
            back += dot(grad_sig, keys)
        grad_rows = direct_ref[rows, :] + back * (1.0 / math.sqrt(key_width))
        grad_rows_ref[user * per_user : (user + 1) * per_user, :] = grad_rows.astype(jnp.bfloat16)


def attend_back(first, count, grad_att, direct, slope, history):
    users, events, key_width = history.shape
    per_user = grad_att.shape[0] // users
    whole = pl.BlockSpec(memory_space=pltpu.VMEM)
    return pl.pallas_call(
        functools.partial(attend_back_kernel, first),
        in_specs=[whole] * 4,
        out_specs=whole,
        out_shape=jax.ShapeDtypeStruct((count * per_user, key_width), jnp.bfloat16),
        compiler_params=pltpu.CompilerParams(vmem_limit_bytes=20 * MIB),
        cost_estimate=pl.CostEstimate(
            flops=4 * count * per_user * events * key_width,
            bytes_accessed=1 << 23,
            transcendentals=0,
        ),
        name="attend_back",
    )(grad_att, direct, slope, history)


def join_rows(parts, joined_ref):
    at = 0
    for part in parts:
        joined_ref[at : at + part.shape[0], :] = part[...]
        at += part.shape[0]


def sum_rows(cands, at, slots_ref, grad_rows_ref):
    places = lax.broadcasted_iota(jnp.int32, (cands, slots_ref.shape[1]), 0) + at
    return dot((places == slots_ref[...]).astype(jnp.bfloat16), grad_rows_ref[...])


def cand_grad_kernel(slots_ref, first_ref, second_ref, cand_grad_ref, grad_rows_ref):
    join_rows((first_ref, second_ref), grad_rows_ref)
    cands = cand_grad_ref.shape[0]
    chunk = math.gcd(cands, 512)
    for at in range(0, cands, chunk):
        cand_grad_ref[at : at + chunk, :] = sum_rows(chunk, at, slots_ref, grad_rows_ref)


def own_cand_grad(cands, slots, grad_parts):
    requests, key_width = slots.shape[1], grad_parts[0].shape[1]
    whole = pl.BlockSpec(memory_space=pltpu.VMEM)
    return pl.pallas_call(
        cand_grad_kernel,
        in_specs=[whole] * 3,
        out_specs=whole,
        out_shape=jax.ShapeDtypeStruct((cands, key_width), jnp.float32),
        scratch_shapes=[pltpu.VMEM((requests, key_width), jnp.bfloat16)],
        compiler_params=pltpu.CompilerParams(vmem_limit_bytes=20 * MIB),
        cost_estimate=pl.CostEstimate(
            flops=2 * cands * key_width * requests, bytes_accessed=1 << 22, transcendentals=0
        ),
        name="own_cand_grad",
    )(slots, *grad_parts)


def terms_kernel(
    origins,
    wide_ref,
    cand_grad_ref,
    slots_ref,
    first_ref,
    second_ref,
    pooled_ref,
    out_ref,
    grad_rows_ref,
    terms_ref,
):
    join_rows((first_ref, second_ref), grad_rows_ref)
    cands = pooled_ref.shape[0]
    chunk = math.gcd(cands, 512)
    for at in range(0, cands, chunk):
        cand_grad = cand_grad_ref[at : at + chunk, :] + sum_rows(
            chunk, at, slots_ref, grad_rows_ref
        )
        term = dot_columns(pooled_ref[at : at + chunk, :], cand_grad.astype(jnp.bfloat16))
        if at == 0:
            terms_ref[...] = term
        else:
            terms_ref[...] += term
    rows = terms_ref.shape[0] // len(origins)
    wide = wide_ref[0]
    batch = max(1, 32 // rows)
    for slot in range(0, len(origins), batch):
        found = [
            terms_ref[pl.ds(pl.multiple_of((wide ^ origins[slot + i]) * rows, rows), rows), :]
            for i in range(batch)
        ]
        found = found[0] if batch == 1 else jnp.concatenate(found, axis=0)
        out_ref[slot * rows : (slot + batch) * rows, :] = found.astype(jnp.bfloat16)


def chip_terms(origins, wide, cand_grad, far_slots, far_parts, pooled):
    cands, width = pooled.shape
    requests, key_width = far_slots.shape[1], cand_grad.shape[1]
    whole = pl.BlockSpec(memory_space=pltpu.VMEM)
    return pl.pallas_call(
        functools.partial(terms_kernel, origins),
        in_specs=[pl.BlockSpec(memory_space=pltpu.SMEM)] + [whole] * 5,
        out_specs=whole,
        out_shape=jax.ShapeDtypeStruct((width, key_width), jnp.bfloat16),
        scratch_shapes=[
            pltpu.VMEM((requests, key_width), jnp.bfloat16),
            pltpu.VMEM((width, key_width), jnp.float32),
        ],
        compiler_params=pltpu.CompilerParams(vmem_limit_bytes=20 * MIB),
        cost_estimate=pl.CostEstimate(
            flops=2 * cands * key_width * (width + requests),
            bytes_accessed=1 << 22,
            transcendentals=0,
        ),
        name="chip_terms",
    )(wide, cand_grad, far_slots, *far_parts, pooled)


def bit_groups(size):
    groups = []
    bit = 0
    while (1 << bit) < size:
        values = min(4, size >> bit)
        groups.append((bit, values))
        bit += values.bit_length() - 1
    return groups


def exchange(values, axis_name, size, distance):
    return lax.ppermute(values, axis_name, [(i, i ^ distance) for i in range(size)])


def send_stage(rows, wides, bit, values):
    found = [exchange(rows, "wide", wides, step << bit) for step in reversed(range(1, values))]
    return found[::-1]


def after(values, *others):
    return lax.optimization_barrier((tuple(values),) + others)[0]


def slot_of(distance, wides):
    slot = 0
    for bit, values in bit_groups(wides):
        slot = slot * values + ((distance >> bit) & (values - 1))
    return slot


def sum_blocks(blocks, wides, logits):
    total = blocks
    for bit, values in bit_groups(wides):
        if bit > 0:
            total, logits = lax.optimization_barrier((total, logits))
        parts = total.astype(jnp.bfloat16).reshape((values, -1) + blocks.shape[1:])
        found = [
            exchange(parts[step], "wide", wides, step << bit).astype(jnp.float32)
            for step in reversed(range(1, values))
        ]
        total = sum(found, parts[0].astype(jnp.float32))
    return total, logits


def body(
    frames,
    qkv_weight,
    out_weight,
    proj_weight,
    mlp_weight,
    logit_weight,
    history,
    hist_len,
    hist_mask,
    req_owner,
    req_local,
    labels,
):
    wides = lax.axis_size("wide")
    core, wide = lax.axis_index("section"), lax.axis_index("wide")
    cand_count = frames.shape[0]
    requests = req_local.shape[0]
    users, events, _ = history.shape
    keep, send, embedded = encode_block(
        core.reshape(1), frames, qkv_weight, out_weight, proj_weight
    )
    positions = jnp.arange(events, dtype=jnp.int32)[None, :]
    usable = (
        (positions < hist_len[:, None]) & ((hist_mask == 1) | (positions == 0))
    ).astype(jnp.float32)
    inv_count = lax.rsqrt(jnp.sum(usable, axis=1))
    usable = usable.reshape(users, 1, events)
    owner_core = req_owner[:, 0] // wides
    owner_slot = slot_of((req_owner[:, 0] % wides) ^ wide, wides)
    slots = ((owner_core ^ core) * wides + owner_slot) * cand_count + req_local
    pooled_slots = (owner_slot * 2 + owner_core) * cand_count + req_local
    stages = list(reversed(bit_groups(wides)))
    near, pooled = embedded, None
    for place, stage in enumerate(stages):
        found = send_stage(near, wides, *stage)
        if place == 0:
            got = exchange(send, "section", 2, 1)
            far_slots = exchange(pooled_slots, "section", 2, 1)
            found, keep, got, far_slots = lax.optimization_barrier((found, keep, got, far_slots))
            pooled = jnp.where(
                core == 0,
                jnp.concatenate([keep, got], axis=0),
                jnp.concatenate([got, keep], axis=0),
            )
        else:
            bit, values = stages[place - 1]
            early = send_stage(pooled, wides, bit, values - 1)
            found, early = lax.optimization_barrier((found, early))
            late = exchange(after([pooled], *found)[0], "wide", wides, (values - 1) << bit)
            if place + 1 < len(stages):
                pooled = jnp.concatenate([pooled] + early + [late], axis=0)
        near = jnp.concatenate([near] + found, axis=0)
    far = exchange(near, "section", 2, 1)
    queries, attended, slope, mlp_weight = attend(
        inv_count, slots.reshape(requests, 1), near, far, history, usable, mlp_weight
    )
    pooled = jnp.concatenate(after([pooled] + early + [late], attended), axis=0)
    found_pooled = send_stage(pooled, wides, *stages[-1])
    logits, grad_att, direct = score(
        inv_count,
        queries,
        attended,
        labels.reshape(requests, 1),
        mlp_weight,
        logit_weight.reshape(1, -1),
    )
    half = max(1, users - 1)
    first_rows = attend_back(0, half, grad_att, direct, slope, history)
    found_pooled, grad_att, first_rows = lax.optimization_barrier(
        (found_pooled, grad_att, first_rows)
    )
    pooled = jnp.concatenate([pooled] + found_pooled, axis=0)
    grad_parts = [first_rows, attend_back(half, users - half, grad_att, direct, slope, history)]
    far_parts = [exchange(part, "section", 2, 1) for part in grad_parts]
    cand_grad = own_cand_grad(pooled.shape[0], pooled_slots.reshape(1, requests), grad_parts)
    origins = [0] * wides
    for distance in range(wides):
        origins[slot_of(distance, wides)] = distance
    terms = chip_terms(
        origins,
        wide.reshape(1),
        cand_grad,
        far_slots.reshape(1, requests),
        far_parts,
        pooled,
    )
    grad_proj, logits = sum_blocks(terms, wides, logits.reshape(requests))
    return (logits, grad_proj)


def solution(mesh):
    in_specs = (
        P(("section", "wide"), None, None),
        P(),
        P(),
        P(),
        P(),
        P(),
        P(("section", "wide"), None, None),
        P(("section", "wide")),
        P(("section", "wide"), None),
        P(("section", "wide"), None),
        P(("section", "wide")),
        P(("section", "wide")),
    )
    out_specs = (P(("section", "wide")), P(("section", "wide"), None))
    return jax.shard_map(body, mesh=mesh, in_specs=in_specs, out_specs=out_specs, check_vma=False)
```

```python
import functools
import math

import jax
import jax.numpy as jnp
from jax import lax
from jax.experimental import pallas as pl
from jax.experimental.pallas import tpu as pltpu
from jax.sharding import PartitionSpec as P

HEADS = 16
FRAMES = 3


EPSILON = 1e-06
MIB = 1024 * 1024


def layer_norm(values):
    center = values - jnp.mean(values, axis=-1, keepdims=True)
    spread = jnp.mean(jnp.square(center), axis=-1, keepdims=True)
    return center * lax.rsqrt(spread + EPSILON)


def dot(left, right):
    return jnp.dot(left, right, preferred_element_type=jnp.float32)


def dot_rows(left, right):
    return lax.dot_general(left, right, (((1,), (1,)), ((), ())), preferred_element_type=jnp.float32)


def dot_columns(left, right):
    return lax.dot_general(left, right, (((0,), (0,)), ((), ())), preferred_element_type=jnp.float32)


def split_rows(values):
    high = values.astype(jnp.bfloat16)
    low = (values - high.astype(jnp.float32)).astype(jnp.bfloat16)
    return jnp.concatenate([high, low], axis=0)


def dot_split(values, right):
    both = dot(split_rows(values), right)
    rows = values.shape[0]
    return both[:rows] + both[rows:]


def encode_kernel(
    tokens,
    core_ref,
    frames_hbm,
    qkv_hbm,
    out_hbm,
    proj_hbm,
    keep_ref,
    send_ref,
    embedded_ref,
    frames_ref,
    qkv_ref,
    out_ref,
    proj_ref,
    sems,
    normed_ref,
    packed_ref,
    scores_ref,
    mixed_rows_ref,
    sums_ref,
):
    total = embedded_ref.shape[0]
    rows, width = packed_ref.shape[0], packed_ref.shape[1] // 2
    cands = rows // tokens
    groups = total // cands
    head_dim = width // HEADS
    patches = tokens // FRAMES
    lanes = 2 * head_dim
    blocks = rows // lanes
    pairs = HEADS // 2
    quad = 4
    span = quad * head_dim

    def group_rows(group):
        return pl.ds(group * rows, rows)

    def columns(part):
        return pl.ds(part * width, width)

    pieces = [(frames_hbm.at[group_rows(0)], frames_ref.at[group_rows(0)])]
    pieces += [(qkv_hbm.at[:, columns(part)], qkv_ref.at[:, columns(part)]) for part in range(2)]
    pieces += [
        (frames_hbm.at[group_rows(group)], frames_ref.at[group_rows(group)])
        for group in range(1, groups)
    ]
    pieces += [(qkv_hbm.at[:, columns(2)], qkv_ref.at[:, columns(2)])]
    pieces += [(out_hbm, out_ref), (proj_hbm, proj_ref)]
    copies = [
        pltpu.make_async_copy(source, target, sems.at[place])
        for place, (source, target) in enumerate(pieces)
    ]
    copies[0].start()
    copies[1].start()

    def norm_cand(cand):
        at = slice(cand * tokens, (cand + 1) * tokens)
        inputs = frames_ref[at, :].astype(jnp.float32)
        normed_ref[at, :] = layer_norm(inputs).astype(jnp.bfloat16)
        sums_ref[cand] = jnp.sum(inputs, axis=0, keepdims=True)

    exponent = math.log2(math.e) / math.sqrt(head_dim)
    frame_at = (lax.broadcasted_iota(jnp.int32, (patches, quad * lanes), 1) % lanes) // patches
    nothing = jnp.zeros((head_dim, lanes), jnp.bfloat16)
    ones_row = lax.broadcasted_iota(jnp.int32, (2 * lanes, 2 * lanes), 0) // patches
    ones_column = lax.broadcasted_iota(jnp.int32, (2 * lanes, 2 * lanes), 1) // patches
    frame_ones = (ones_row == ones_column).astype(jnp.bfloat16)
    own = lax.broadcasted_iota(jnp.int32, (cands, rows), 1) // tokens == lax.broadcasted_iota(
        jnp.int32, (cands, rows), 0
    )

    def own_scores(block, head):
        block_rows = slice(block * lanes, (block + 1) * lanes)
        start = head * head_dim
        query = packed_ref[block_rows, start : start + span]
        keys = packed_ref[block_rows, width + start : width + start + span].T
        keys = jnp.concatenate(
            [
                jnp.concatenate(
                    [nothing] * place
                    + [keys[place * head_dim : (place + 1) * head_dim]]
                    + [nothing] * (quad - 1 - place),
                    axis=1,
                )
                for place in range(quad)
            ],
            axis=0,
        )
        scores = dot(query, keys)
        found = scores[:patches]
        for frame in range(1, lanes // patches):
            found = jnp.where(
                frame_at == frame, scores[frame * patches : (frame + 1) * patches], found
            )
        for side in range(quad // 2):
            scores_ref[block, head // 2 + side] = found[
                :, side * 2 * lanes : (side + 1) * 2 * lanes
            ]

    copies[0].wait()
    copies[2].start()
    for cand in range(cands):
        norm_cand(cand)
    copies[1].wait()
    for copy in copies[3 : 2 + groups]:
        copy.start()
    for group in range(groups):
        at = slice(group * rows, (group + 1) * rows)
        for part in range(2):
            if group == 0 and part == 1:
                copies[2].wait()
                for copy in copies[2 + groups :]:
                    copy.start()
            part_columns = slice(part * width, (part + 1) * width)
            packed_ref[:, part_columns] = dot(normed_ref[at, :], qkv_ref[:, part_columns]).astype(
                jnp.bfloat16
            )
            if group + 1 < groups:
                if part == 0:
                    copies[3 + group].wait()
                for cand in range(part * cands // 2, (part + 1) * cands // 2):
                    norm_cand((group + 1) * cands + cand)
        for head in range(0, HEADS, quad):
            for block in range(blocks):
                own_scores(block, head)
        exp_scores = jnp.exp2(
            scores_ref[...].reshape(blocks * pairs * patches, 2 * lanes) * exponent
        )
        totals = dot(exp_scores.astype(jnp.bfloat16), frame_ones)
        probs = (exp_scores / totals).reshape(blocks * pairs, patches, 2 * lanes)
        sums = jnp.sum(probs, axis=1)
        key_sums = [
            jnp.concatenate(
                [
                    sums[block * pairs : (block + 1) * pairs, side * lanes : (side + 1) * lanes]
                    for block in range(blocks)
                ],
                axis=1,
            )
            for side in range(2)
        ]
        spread = jnp.concatenate(
            [
                jnp.where(own, key_sums[head % 2][head // 2 : head // 2 + 1], 0.0)
                for head in range(HEADS)
            ],
            axis=0,
        ).astype(jnp.bfloat16)
        mixed_rows = dot(spread, normed_ref[at, :])
        for head in range(HEADS):
            mixed_rows_ref[head, group * cands : (group + 1) * cands, :] = mixed_rows[
                head * cands : (head + 1) * cands
            ]

    for copy in copies[2 + groups :]:
        copy.wait()
    mixed = []
    for head in range(0, HEADS, quad):
        left = mixed_rows_ref[head : head + quad].reshape(quad * total, width)
        start = 2 * width + head * head_dim
        both = dot_split(left, qkv_ref[:, start : start + span])
        head_at = lax.broadcasted_iota(jnp.int32, (total, span), 1) // head_dim
        piece = jnp.zeros((total, span), jnp.float32)
        for place in range(quad):
            piece = jnp.where(head_at == place, both[place * total : (place + 1) * total], piece)
        mixed.append(piece)
    mixed_mean = jnp.concatenate(mixed, axis=1) * (1.0 / tokens)
    hidden = sums_ref[...].reshape(total, width) * (1.0 / tokens)
    hidden += dot_split(mixed_mean, out_ref[...])
    pooled = layer_norm(hidden).astype(jnp.bfloat16)
    first, second = pooled[:, : width // 2], pooled[:, width // 2 :]
    keep_ref[...] = jnp.where(core_ref[0] == 0, first, second)
    send_ref[...] = jnp.where(core_ref[0] == 0, second, first)
    embedded_ref[...] = dot(pooled, proj_ref[...]).astype(jnp.bfloat16)


def in_hbm(*arrays):
    return [pltpu.with_memory_space_constraint(array, pltpu.HBM) for array in arrays]


def encode_block(core, frames, qkv_weight, out_weight, proj_weight):
    cand_count, tokens, width = frames.shape
    key_width = proj_weight.shape[1]
    groups = 2
    rows = cand_count * tokens // groups
    lanes = 2 * width // HEADS
    patches = tokens // FRAMES
    flat = frames.reshape(cand_count * tokens, width)
    whole = pl.BlockSpec(memory_space=pltpu.VMEM)
    return pl.pallas_call(
        functools.partial(encode_kernel, tokens),
        in_specs=[pl.BlockSpec(memory_space=pltpu.SMEM)]
        + [pl.BlockSpec(memory_space=pltpu.HBM)] * 4,
        out_specs=[whole] * 3,
        out_shape=[
            jax.ShapeDtypeStruct((cand_count, width // 2), jnp.bfloat16),
            jax.ShapeDtypeStruct((cand_count, width // 2), jnp.bfloat16),
            jax.ShapeDtypeStruct((cand_count, key_width), jnp.bfloat16),
        ],
        scratch_shapes=[
            pltpu.VMEM(flat.shape, jnp.bfloat16),
            pltpu.VMEM(qkv_weight.shape, jnp.bfloat16),
            pltpu.VMEM(out_weight.shape, jnp.bfloat16),
            pltpu.VMEM(proj_weight.shape, jnp.bfloat16),
            pltpu.SemaphoreType.DMA((groups + 5,)),
            pltpu.VMEM(flat.shape, jnp.bfloat16),
            pltpu.VMEM((rows, 2 * width), jnp.bfloat16),
            pltpu.VMEM((rows // lanes, HEADS // 2, patches, 2 * lanes), jnp.float32),
            pltpu.VMEM((HEADS, cand_count, width), jnp.float32),
            pltpu.VMEM((cand_count, 1, width), jnp.float32),
        ],
        compiler_params=pltpu.CompilerParams(vmem_limit_bytes=44 * MIB),
        cost_estimate=pl.CostEstimate(
            flops=5 * cand_count * tokens * width * width, bytes_accessed=1 << 24, transcendentals=0
        ),
        name="encode",
    )(core, *in_hbm(flat, qkv_weight, out_weight, proj_weight))


def attend_kernel(
    inv_ref,
    slots_ref,
    near_ref,
    far_ref,
    usable_ref,
    history_hbm,
    mlp_hbm,
    queries_ref,
    attended_ref,
    slope_ref,
    mlp_ref,
    history_ref,
    sems,
):
    users, events, _ = history_ref.shape
    chunk = math.gcd(events, 1024)
    copies = [
        pltpu.make_async_copy(history_hbm.at[user], history_ref.at[user], sems.at[user])
        for user in range(users)
    ]
    copies.append(pltpu.make_async_copy(mlp_hbm, mlp_ref, sems.at[users]))
    for copy in copies[:2]:
        copy.start()
    slots = slots_ref[...]
    half, key_width = near_ref.shape
    places = lax.broadcasted_iota(jnp.int32, (slots.shape[0], half), 1)
    queries = dot((slots == places).astype(jnp.bfloat16), near_ref[...])
    queries += dot((slots == places + half).astype(jnp.bfloat16), far_ref[...])
    queries_ref[...] = queries.astype(jnp.bfloat16)
    per_user = slots.shape[0] // users
    for user in range(users):
        copies[user].wait()
        if user + 2 < len(copies):
            copies[user + 2].start()
        rows = slice(user * per_user, (user + 1) * per_user)
        attended = jnp.zeros((per_user, key_width), jnp.float32)
        for at in range(0, events, chunk):
            keys = history_ref[user, at : at + chunk, :]
            usable = usable_ref[user, :, at : at + chunk]
            scores = dot_rows(queries_ref[rows, :], keys)
            half_gate = 0.5 * jnp.tanh(scores * (0.5 / math.sqrt(key_width)))
            weights = (0.5 + half_gate) * usable
            slope_ref[rows, at : at + chunk] = (weights * (0.5 - half_gate)).astype(jnp.bfloat16)
            attended += dot(weights.astype(jnp.bfloat16), keys)
        attended_ref[rows, :] = attended * inv_ref[user]
    copies[users].wait()


def attend(inv_count, slots, near, far, history, usable, mlp_weight):
    users, events, key_width = history.shape
    requests = slots.shape[0]
    whole = pl.BlockSpec(memory_space=pltpu.VMEM)
    return pl.pallas_call(
        attend_kernel,
        in_specs=[pl.BlockSpec(memory_space=pltpu.SMEM)]
        + [whole] * 4
        + [pl.BlockSpec(memory_space=pltpu.HBM)] * 2,
        out_specs=[whole] * 4,
        out_shape=[
            jax.ShapeDtypeStruct((requests, key_width), jnp.bfloat16),
            jax.ShapeDtypeStruct((requests, key_width), jnp.float32),
            jax.ShapeDtypeStruct((requests, events), jnp.bfloat16),
            pltpu.VMEM(mlp_weight.shape, mlp_weight.dtype),
        ],
        scratch_shapes=[
            pltpu.VMEM(history.shape, history.dtype),
            pltpu.SemaphoreType.DMA((users + 1,)),
        ],
        compiler_params=pltpu.CompilerParams(vmem_limit_bytes=32 * MIB),
        cost_estimate=pl.CostEstimate(
            flops=4 * requests * events * key_width, bytes_accessed=1 << 24, transcendentals=0
        ),
        name="attend",
    )(inv_count, slots, near, far, usable, *in_hbm(history, mlp_weight))


def score_kernel(
    inv_ref,
    queries_ref,
    attended_ref,
    labels_ref,
    mlp_ref,
    logit_weight_ref,
    logits_ref,
    grad_att_ref,
    direct_ref,
    grad_pre_ref,
):
    users = inv_ref.shape[0]
    per_user = queries_ref.shape[0] // users
    step_users = math.gcd(users, 2)
    step_rows = step_users * per_user
    key_width = queries_ref.shape[1]
    weight = logit_weight_ref[...].astype(jnp.float32)
    for first in range(0, users, step_users):
        at = slice(first * per_user, first * per_user + step_rows)
        query_b = queries_ref[at, :]
        query_f = query_b.astype(jnp.float32)
        attended = attended_ref[at, :]
        joined = jnp.concatenate(
            [query_b, attended.astype(jnp.bfloat16), (query_f * attended).astype(jnp.bfloat16)],
            axis=1,
        )
        pre_act = dot(joined, mlp_ref[...])
        act_sig = 0.5 * jnp.tanh(0.5 * pre_act) + 0.5
        hidden_units = (pre_act * act_sig).astype(jnp.bfloat16)
        logits = jnp.sum(hidden_units.astype(jnp.float32) * weight, axis=1, keepdims=True)
        logits_ref[at, :] = logits
        dlogit = (0.5 * jnp.tanh(0.5 * logits) + 0.5) - labels_ref[at, :].astype(jnp.float32)
        slope = act_sig * (1.0 + pre_act * (1.0 - act_sig))
        grad_pre = (dlogit * weight * slope).astype(jnp.bfloat16)
        grad_pre_ref[at, :] = grad_pre
    djoined = dot_rows(grad_pre_ref[...], mlp_ref[...])
    part_att = djoined[:, key_width : 2 * key_width]
    part_prod = djoined[:, 2 * key_width :]
    for user in range(users):
        at = slice(user * per_user, (user + 1) * per_user)
        grad_att = part_att[at] + part_prod[at] * queries_ref[at, :].astype(jnp.float32)
        grad_att_ref[at, :] = (grad_att * inv_ref[user]).astype(jnp.bfloat16)
    direct_ref[...] = djoined[:, :key_width] + part_prod * attended_ref[...]


def score(inv_count, queries, attended, labels, mlp_weight, logit_weight):
    requests, key_width = queries.shape
    whole = pl.BlockSpec(memory_space=pltpu.VMEM)
    return pl.pallas_call(
        score_kernel,
        in_specs=[pl.BlockSpec(memory_space=pltpu.SMEM)] + [whole] * 5,
        out_specs=[whole] * 3,
        out_shape=[
            jax.ShapeDtypeStruct((requests, 1), jnp.float32),
            jax.ShapeDtypeStruct((requests, key_width), jnp.bfloat16),
            jax.ShapeDtypeStruct((requests, key_width), jnp.float32),
        ],
        scratch_shapes=[pltpu.VMEM((requests, mlp_weight.shape[1]), jnp.bfloat16)],
        compiler_params=pltpu.CompilerParams(vmem_limit_bytes=32 * MIB),
        cost_estimate=pl.CostEstimate(
            flops=4 * requests * mlp_weight.shape[0] * mlp_weight.shape[1],
            bytes_accessed=1 << 23,
            transcendentals=0,
        ),
        name="score",
    )(inv_count, queries, attended, labels, mlp_weight, logit_weight)


def attend_back_kernel(first, grad_att_ref, direct_ref, slope_ref, history_ref, grad_rows_ref):
    users, events, key_width = history_ref.shape
    per_user = grad_att_ref.shape[0] // users
    chunk = math.gcd(events, 1024)
    for user in range(grad_rows_ref.shape[0] // per_user):
        rows = slice((first + user) * per_user, (first + user + 1) * per_user)
        back = jnp.zeros((per_user, key_width), jnp.float32)
        for at in range(0, events, chunk):
            keys = history_ref[first + user, at : at + chunk, :]
            slope = slope_ref[rows, at : at + chunk].astype(jnp.float32)
            grad_sig = (dot_rows(grad_att_ref[rows, :], keys) * slope).astype(jnp.bfloat16)
            back += dot(grad_sig, keys)
        grad_rows = direct_ref[rows, :] + back * (1.0 / math.sqrt(key_width))
        grad_rows_ref[user * per_user : (user + 1) * per_user, :] = grad_rows.astype(jnp.bfloat16)


def attend_back(first, count, grad_att, direct, slope, history):
    users, events, key_width = history.shape
    per_user = grad_att.shape[0] // users
    whole = pl.BlockSpec(memory_space=pltpu.VMEM)
    return pl.pallas_call(
        functools.partial(attend_back_kernel, first),
        in_specs=[whole] * 4,
        out_specs=whole,
        out_shape=jax.ShapeDtypeStruct((count * per_user, key_width), jnp.bfloat16),
        compiler_params=pltpu.CompilerParams(vmem_limit_bytes=20 * MIB),
        cost_estimate=pl.CostEstimate(
            flops=4 * count * per_user * events * key_width,
            bytes_accessed=1 << 23,
            transcendentals=0,
        ),
        name="attend_back",
    )(grad_att, direct, slope, history)


def join_rows(parts, joined_ref):
    at = 0
    for part in parts:
        joined_ref[at : at + part.shape[0], :] = part[...]
        at += part.shape[0]


def sum_rows(cands, at, slots_ref, grad_rows_ref):
    places = lax.broadcasted_iota(jnp.int32, (cands, slots_ref.shape[1]), 0) + at
    return dot((places == slots_ref[...]).astype(jnp.bfloat16), grad_rows_ref[...])


def cand_grad_kernel(slots_ref, first_ref, second_ref, cand_grad_ref, grad_rows_ref):
    join_rows((first_ref, second_ref), grad_rows_ref)
    cands = cand_grad_ref.shape[0]
    chunk = math.gcd(cands, 512)
    for at in range(0, cands, chunk):
        cand_grad_ref[at : at + chunk, :] = sum_rows(chunk, at, slots_ref, grad_rows_ref)


def own_cand_grad(cands, slots, grad_parts):
    requests, key_width = slots.shape[1], grad_parts[0].shape[1]
    whole = pl.BlockSpec(memory_space=pltpu.VMEM)
    return pl.pallas_call(
        cand_grad_kernel,
        in_specs=[whole] * 3,
        out_specs=whole,
        out_shape=jax.ShapeDtypeStruct((cands, key_width), jnp.float32),
        scratch_shapes=[pltpu.VMEM((requests, key_width), jnp.bfloat16)],
        compiler_params=pltpu.CompilerParams(vmem_limit_bytes=20 * MIB),
        cost_estimate=pl.CostEstimate(
            flops=2 * cands * key_width * requests, bytes_accessed=1 << 22, transcendentals=0
        ),
        name="own_cand_grad",
    )(slots, *grad_parts)


def terms_kernel(
    origins,
    wide_ref,
    cand_grad_ref,
    slots_ref,
    first_ref,
    second_ref,
    pooled_ref,
    out_ref,
    grad_rows_ref,
    terms_ref,
):
    join_rows((first_ref, second_ref), grad_rows_ref)
    cands = pooled_ref.shape[0]
    chunk = math.gcd(cands, 512)
    for at in range(0, cands, chunk):
        cand_grad = cand_grad_ref[at : at + chunk, :] + sum_rows(
            chunk, at, slots_ref, grad_rows_ref
        )
        term = dot_columns(pooled_ref[at : at + chunk, :], cand_grad.astype(jnp.bfloat16))
        if at == 0:
            terms_ref[...] = term
        else:
            terms_ref[...] += term
    rows = terms_ref.shape[0] // len(origins)
    wide = wide_ref[0]
    batch = max(1, 32 // rows)
    for slot in range(0, len(origins), batch):
        found = [
            terms_ref[pl.ds(pl.multiple_of((wide ^ origins[slot + i]) * rows, rows), rows), :]
            for i in range(batch)
        ]
        found = found[0] if batch == 1 else jnp.concatenate(found, axis=0)
        out_ref[slot * rows : (slot + batch) * rows, :] = found.astype(jnp.bfloat16)


def chip_terms(origins, wide, cand_grad, far_slots, far_parts, pooled):
    cands, width = pooled.shape
    requests, key_width = far_slots.shape[1], cand_grad.shape[1]
    whole = pl.BlockSpec(memory_space=pltpu.VMEM)
    return pl.pallas_call(
        functools.partial(terms_kernel, origins),
        in_specs=[pl.BlockSpec(memory_space=pltpu.SMEM)] + [whole] * 5,
        out_specs=whole,
        out_shape=jax.ShapeDtypeStruct((width, key_width), jnp.bfloat16),
        scratch_shapes=[
            pltpu.VMEM((requests, key_width), jnp.bfloat16),
            pltpu.VMEM((width, key_width), jnp.float32),
        ],
        compiler_params=pltpu.CompilerParams(vmem_limit_bytes=20 * MIB),
        cost_estimate=pl.CostEstimate(
            flops=2 * cands * key_width * (width + requests),
            bytes_accessed=1 << 22,
            transcendentals=0,
        ),
        name="chip_terms",
    )(wide, cand_grad, far_slots, *far_parts, pooled)


def bit_groups(size):
    groups = []
    bit = 0
    while (1 << bit) < size:
        values = min(4, size >> bit)
        groups.append((bit, values))
        bit += values.bit_length() - 1
    return groups


def exchange(values, axis_name, size, distance):
    return lax.ppermute(values, axis_name, [(i, i ^ distance) for i in range(size)])


def send_stage(rows, wides, bit, values):
    found = [exchange(rows, "wide", wides, step << bit) for step in reversed(range(1, values))]
    return found[::-1]


def after(values, *others):
    return lax.optimization_barrier((tuple(values),) + others)[0]


def slot_of(distance, wides):
    slot = 0
    for bit, values in bit_groups(wides):
        slot = slot * values + ((distance >> bit) & (values - 1))
    return slot


def sum_blocks(blocks, wides, logits):
    total = blocks
    for bit, values in bit_groups(wides):
        if bit > 0:
            total, logits = lax.optimization_barrier((total, logits))
        parts = total.astype(jnp.bfloat16).reshape((values, -1) + blocks.shape[1:])
        found = [
            exchange(parts[step], "wide", wides, step << bit).astype(jnp.float32)
            for step in reversed(range(1, values))
        ]
        total = sum(found, parts[0].astype(jnp.float32))
    return total, logits


def body(
    frames,
    qkv_weight,
    out_weight,
    proj_weight,
    mlp_weight,
    logit_weight,
    history,
    hist_len,
    hist_mask,
    req_owner,
    req_local,
    labels,
):
    wides = lax.axis_size("wide")
    core, wide = lax.axis_index("section"), lax.axis_index("wide")
    cand_count = frames.shape[0]
    requests = req_local.shape[0]
    users, events, _ = history.shape
    keep, send, embedded = encode_block(
        core.reshape(1), frames, qkv_weight, out_weight, proj_weight
    )
    positions = jnp.arange(events, dtype=jnp.int32)[None, :]
    usable = (
        (positions < hist_len[:, None]) & ((hist_mask == 1) | (positions == 0))
    ).astype(jnp.float32)
    inv_count = lax.rsqrt(jnp.sum(usable, axis=1))
    usable = usable.reshape(users, 1, events)
    owner_core = req_owner[:, 0] // wides
    owner_slot = slot_of((req_owner[:, 0] % wides) ^ wide, wides)
    slots = ((owner_core ^ core) * wides + owner_slot) * cand_count + req_local
    pooled_slots = (owner_slot * 2 + owner_core) * cand_count + req_local
    stages = list(reversed(bit_groups(wides)))
    near, pooled = embedded, None
    for place, stage in enumerate(stages):
        found = send_stage(near, wides, *stage)
        if place == 0:
            got = exchange(send, "section", 2, 1)
            far_slots = exchange(pooled_slots, "section", 2, 1)
            found, keep, got, far_slots = lax.optimization_barrier((found[::-1], keep, got, far_slots))
            found = found[::-1]
            pooled = jnp.where(
                core == 0,
                jnp.concatenate([keep, got], axis=0),
                jnp.concatenate([got, keep], axis=0),
            )
        else:
            bit, values = stages[place - 1]
            paired = exchange(pooled, "wide", wides, 1 << bit)
            found, paired = lax.optimization_barrier((found[::-1], paired))
            found = found[::-1]
            pooled_parts = [jnp.concatenate([pooled, paired], axis=0)]
            if values > 2:
                pooled_parts.append(exchange(pooled_parts[0], "wide", wides, 2 << bit))
            if place + 1 < len(stages):
                pooled = jnp.concatenate(pooled_parts, axis=0)
        near = jnp.concatenate([near] + found, axis=0)
    far = exchange(near, "section", 2, 1)
    queries, attended, slope, mlp_weight = attend(
        inv_count, slots.reshape(requests, 1), near, far, history, usable, mlp_weight
    )
    pooled = jnp.concatenate(after(pooled_parts, attended), axis=0)
    found_pooled = send_stage(pooled, wides, *stages[-1])
    logits, grad_att, direct = score(
        inv_count,
        queries,
        attended,
        labels.reshape(requests, 1),
        mlp_weight,
        logit_weight.reshape(1, -1),
    )
    half = max(1, users - 1)
    first_rows = attend_back(0, half, grad_att, direct, slope, history)
    found_pooled, grad_att, first_rows = lax.optimization_barrier(
        (found_pooled[::-1], grad_att, first_rows)
    )
    pooled = jnp.concatenate([pooled] + found_pooled[::-1], axis=0)
    grad_parts = [first_rows, attend_back(half, users - half, grad_att, direct, slope, history)]
    far_parts = [exchange(part, "section", 2, 1) for part in grad_parts]
    cand_grad = own_cand_grad(pooled.shape[0], pooled_slots.reshape(1, requests), grad_parts)
    origins = [0] * wides
    for distance in range(wides):
        origins[slot_of(distance, wides)] = distance
    terms = chip_terms(
        origins,
        wide.reshape(1),
        cand_grad,
        far_slots.reshape(1, requests),
        far_parts,
        pooled,
    )
    grad_proj, logits = sum_blocks(terms, wides, logits.reshape(requests))
    return (logits, grad_proj)


def solution(mesh):
    in_specs = (
        P(("section", "wide"), None, None),
        P(),
        P(),
        P(),
        P(),
        P(),
        P(("section", "wide"), None, None),
        P(("section", "wide")),
        P(("section", "wide"), None),
        P(("section", "wide"), None),
        P(("section", "wide")),
        P(("section", "wide")),
    )
    out_specs = (P(("section", "wide")), P(("section", "wide"), None))
    return jax.shard_map(body, mesh=mesh, in_specs=in_specs, out_specs=out_specs, check_vma=False)
```

```python
import functools
import math

import jax
import jax.numpy as jnp
from jax import lax
from jax.experimental import pallas as pl
from jax.experimental.pallas import tpu as pltpu
from jax.sharding import PartitionSpec as P

HEADS = 16
FRAMES = 3


EPSILON = 1e-06
MIB = 1024 * 1024


def layer_norm(values):
    center = values - jnp.mean(values, axis=-1, keepdims=True)
    spread = jnp.mean(jnp.square(center), axis=-1, keepdims=True)
    return center * lax.rsqrt(spread + EPSILON)


def dot(left, right):
    return jnp.dot(left, right, preferred_element_type=jnp.float32)


def dot_rows(left, right):
    return lax.dot_general(left, right, (((1,), (1,)), ((), ())), preferred_element_type=jnp.float32)


def dot_columns(left, right):
    return lax.dot_general(left, right, (((0,), (0,)), ((), ())), preferred_element_type=jnp.float32)


def split_rows(values):
    high = values.astype(jnp.bfloat16)
    low = (values - high.astype(jnp.float32)).astype(jnp.bfloat16)
    return jnp.concatenate([high, low], axis=0)


def dot_split(values, right):
    both = dot(split_rows(values), right)
    rows = values.shape[0]
    return both[:rows] + both[rows:]


def encode_kernel(
    tokens,
    core_ref,
    frames_hbm,
    qkv_hbm,
    out_hbm,
    proj_hbm,
    keep_ref,
    send_ref,
    embedded_ref,
    frames_ref,
    qkv_ref,
    out_ref,
    proj_ref,
    sems,
    normed_ref,
    packed_ref,
    scores_ref,
    mixed_rows_ref,
    sums_ref,
):
    total = embedded_ref.shape[0]
    rows, width = packed_ref.shape[0], packed_ref.shape[1] // 2
    cands = rows // tokens
    groups = total // cands
    head_dim = width // HEADS
    patches = tokens // FRAMES
    lanes = 2 * head_dim
    blocks = rows // lanes
    pairs = HEADS // 2
    quad = 4
    span = quad * head_dim

    def group_rows(group):
        return pl.ds(group * rows, rows)

    def columns(part):
        return pl.ds(part * width, width)

    pieces = [(frames_hbm.at[group_rows(0)], frames_ref.at[group_rows(0)])]
    pieces += [(qkv_hbm.at[:, columns(part)], qkv_ref.at[:, columns(part)]) for part in range(2)]
    pieces += [
        (frames_hbm.at[group_rows(group)], frames_ref.at[group_rows(group)])
        for group in range(1, groups)
    ]
    pieces += [(qkv_hbm.at[:, columns(2)], qkv_ref.at[:, columns(2)])]
    pieces += [(out_hbm, out_ref), (proj_hbm, proj_ref)]
    copies = [
        pltpu.make_async_copy(source, target, sems.at[place])
        for place, (source, target) in enumerate(pieces)
    ]
    copies[0].start()
    copies[1].start()

    def norm_cand(cand):
        at = slice(cand * tokens, (cand + 1) * tokens)
        inputs = frames_ref[at, :].astype(jnp.float32)
        normed_ref[at, :] = layer_norm(inputs).astype(jnp.bfloat16)
        sums_ref[cand] = jnp.sum(inputs, axis=0, keepdims=True)

    exponent = math.log2(math.e) / math.sqrt(head_dim)
    frame_at = (lax.broadcasted_iota(jnp.int32, (patches, quad * lanes), 1) % lanes) // patches
    nothing = jnp.zeros((head_dim, lanes), jnp.bfloat16)
    ones_row = lax.broadcasted_iota(jnp.int32, (2 * lanes, 2 * lanes), 0) // patches
    ones_column = lax.broadcasted_iota(jnp.int32, (2 * lanes, 2 * lanes), 1) // patches
    frame_ones = (ones_row == ones_column).astype(jnp.bfloat16)
    own = lax.broadcasted_iota(jnp.int32, (cands, rows), 1) // tokens == lax.broadcasted_iota(
        jnp.int32, (cands, rows), 0
    )

    def own_scores(block, head):
        block_rows = slice(block * lanes, (block + 1) * lanes)
        start = head * head_dim
        query = packed_ref[block_rows, start : start + span]
        keys = packed_ref[block_rows, width + start : width + start + span].T
        keys = jnp.concatenate(
            [
                jnp.concatenate(
                    [nothing] * place
                    + [keys[place * head_dim : (place + 1) * head_dim]]
                    + [nothing] * (quad - 1 - place),
                    axis=1,
                )
                for place in range(quad)
            ],
            axis=0,
        )
        scores = dot(query, keys)
        found = scores[:patches]
        for frame in range(1, lanes // patches):
            found = jnp.where(
                frame_at == frame, scores[frame * patches : (frame + 1) * patches], found
            )
        for side in range(quad // 2):
            scores_ref[block, head // 2 + side] = found[
                :, side * 2 * lanes : (side + 1) * 2 * lanes
            ]

    copies[0].wait()
    copies[2].start()
    for cand in range(cands):
        norm_cand(cand)
    copies[1].wait()
    for copy in copies[3 : 2 + groups]:
        copy.start()
    for group in range(groups):
        at = slice(group * rows, (group + 1) * rows)
        for part in range(2):
            if group == 0 and part == 1:
                copies[2].wait()
                for copy in copies[2 + groups :]:
                    copy.start()
            part_columns = slice(part * width, (part + 1) * width)
            packed_ref[:, part_columns] = dot(normed_ref[at, :], qkv_ref[:, part_columns]).astype(
                jnp.bfloat16
            )
            if group + 1 < groups:
                if part == 0:
                    copies[3 + group].wait()
                for cand in range(part * cands // 2, (part + 1) * cands // 2):
                    norm_cand((group + 1) * cands + cand)
        for head in range(0, HEADS, quad):
            for block in range(blocks):
                own_scores(block, head)
        exp_scores = jnp.exp2(
            scores_ref[...].reshape(blocks * pairs * patches, 2 * lanes) * exponent
        )
        totals = dot(exp_scores.astype(jnp.bfloat16), frame_ones)
        probs = (exp_scores / totals).reshape(blocks * pairs, patches, 2 * lanes)
        sums = jnp.sum(probs, axis=1)
        key_sums = [
            jnp.concatenate(
                [
                    sums[block * pairs : (block + 1) * pairs, side * lanes : (side + 1) * lanes]
                    for block in range(blocks)
                ],
                axis=1,
            )
            for side in range(2)
        ]
        spread = jnp.concatenate(
            [
                jnp.where(own, key_sums[head % 2][head // 2 : head // 2 + 1], 0.0)
                for head in range(HEADS)
            ],
            axis=0,
        ).astype(jnp.bfloat16)
        mixed_rows = dot(spread, normed_ref[at, :])
        for head in range(HEADS):
            mixed_rows_ref[head, group * cands : (group + 1) * cands, :] = mixed_rows[
                head * cands : (head + 1) * cands
            ]

    for copy in copies[2 + groups :]:
        copy.wait()
    mixed = []
    for head in range(0, HEADS, quad):
        left = mixed_rows_ref[head : head + quad].reshape(quad * total, width)
        start = 2 * width + head * head_dim
        both = dot(left.astype(jnp.bfloat16), qkv_ref[:, start : start + span])
        head_at = lax.broadcasted_iota(jnp.int32, (total, span), 1) // head_dim
        piece = jnp.zeros((total, span), jnp.float32)
        for place in range(quad):
            piece = jnp.where(head_at == place, both[place * total : (place + 1) * total], piece)
        mixed.append(piece)
    mixed_mean = jnp.concatenate(mixed, axis=1) * (1.0 / tokens)
    hidden = sums_ref[...].reshape(total, width) * (1.0 / tokens)
    hidden += dot_split(mixed_mean, out_ref[...])
    pooled = layer_norm(hidden).astype(jnp.bfloat16)
    first, second = pooled[:, : width // 2], pooled[:, width // 2 :]
    keep_ref[...] = jnp.where(core_ref[0] == 0, first, second)
    send_ref[...] = jnp.where(core_ref[0] == 0, second, first)
    embedded_ref[...] = dot(pooled, proj_ref[...]).astype(jnp.bfloat16)


def in_hbm(*arrays):
    return [pltpu.with_memory_space_constraint(array, pltpu.HBM) for array in arrays]


def encode_block(core, frames, qkv_weight, out_weight, proj_weight):
    cand_count, tokens, width = frames.shape
    key_width = proj_weight.shape[1]
    groups = 2
    rows = cand_count * tokens // groups
    lanes = 2 * width // HEADS
    patches = tokens // FRAMES
    flat = frames.reshape(cand_count * tokens, width)
    whole = pl.BlockSpec(memory_space=pltpu.VMEM)
    return pl.pallas_call(
        functools.partial(encode_kernel, tokens),
        in_specs=[pl.BlockSpec(memory_space=pltpu.SMEM)]
        + [pl.BlockSpec(memory_space=pltpu.HBM)] * 4,
        out_specs=[whole] * 3,
        out_shape=[
            jax.ShapeDtypeStruct((cand_count, width // 2), jnp.bfloat16),
            jax.ShapeDtypeStruct((cand_count, width // 2), jnp.bfloat16),
            jax.ShapeDtypeStruct((cand_count, key_width), jnp.bfloat16),
        ],
        scratch_shapes=[
            pltpu.VMEM(flat.shape, jnp.bfloat16),
            pltpu.VMEM(qkv_weight.shape, jnp.bfloat16),
            pltpu.VMEM(out_weight.shape, jnp.bfloat16),
            pltpu.VMEM(proj_weight.shape, jnp.bfloat16),
            pltpu.SemaphoreType.DMA((groups + 5,)),
            pltpu.VMEM(flat.shape, jnp.bfloat16),
            pltpu.VMEM((rows, 2 * width), jnp.bfloat16),
            pltpu.VMEM((rows // lanes, HEADS // 2, patches, 2 * lanes), jnp.float32),
            pltpu.VMEM((HEADS, cand_count, width), jnp.float32),
            pltpu.VMEM((cand_count, 1, width), jnp.float32),
        ],
        compiler_params=pltpu.CompilerParams(vmem_limit_bytes=44 * MIB),
        cost_estimate=pl.CostEstimate(
            flops=5 * cand_count * tokens * width * width, bytes_accessed=1 << 24, transcendentals=0
        ),
        name="encode",
    )(core, *in_hbm(flat, qkv_weight, out_weight, proj_weight))


def attend_kernel(
    inv_ref,
    slots_ref,
    near_ref,
    far_ref,
    usable_ref,
    history_hbm,
    mlp_hbm,
    queries_ref,
    attended_ref,
    slope_ref,
    mlp_ref,
    history_ref,
    sems,
):
    users, events, _ = history_ref.shape
    chunk = math.gcd(events, 2048)
    copies = [
        pltpu.make_async_copy(history_hbm.at[user], history_ref.at[user], sems.at[user])
        for user in range(users)
    ]
    copies.append(pltpu.make_async_copy(mlp_hbm, mlp_ref, sems.at[users]))
    for copy in copies[:2]:
        copy.start()
    slots = slots_ref[...]
    half, key_width = near_ref.shape
    places = lax.broadcasted_iota(jnp.int32, (slots.shape[0], half), 1)
    queries = dot((slots == places).astype(jnp.bfloat16), near_ref[...])
    queries += dot((slots == places + half).astype(jnp.bfloat16), far_ref[...])
    queries_ref[...] = queries.astype(jnp.bfloat16)
    per_user = slots.shape[0] // users
    for user in range(users):
        copies[user].wait()
        if user + 2 < len(copies):
            copies[user + 2].start()
        rows = slice(user * per_user, (user + 1) * per_user)
        attended = jnp.zeros((per_user, key_width), jnp.float32)
        for at in range(0, events, chunk):
            keys = history_ref[user, at : at + chunk, :]
            usable = usable_ref[user, :, at : at + chunk]
            scores = dot_rows(queries_ref[rows, :], keys)
            half_gate = 0.5 * jnp.tanh(scores * (0.5 / math.sqrt(key_width)))
            weights = (0.5 + half_gate) * usable
            slope_ref[rows, at : at + chunk] = (weights * (0.5 - half_gate)).astype(jnp.bfloat16)
            attended += dot(weights.astype(jnp.bfloat16), keys)
        attended_ref[rows, :] = attended * inv_ref[user]
    copies[users].wait()


def attend(inv_count, slots, near, far, history, usable, mlp_weight):
    users, events, key_width = history.shape
    requests = slots.shape[0]
    whole = pl.BlockSpec(memory_space=pltpu.VMEM)
    return pl.pallas_call(
        attend_kernel,
        in_specs=[pl.BlockSpec(memory_space=pltpu.SMEM)]
        + [whole] * 4
        + [pl.BlockSpec(memory_space=pltpu.HBM)] * 2,
        out_specs=[whole] * 4,
        out_shape=[
            jax.ShapeDtypeStruct((requests, key_width), jnp.bfloat16),
            jax.ShapeDtypeStruct((requests, key_width), jnp.float32),
            jax.ShapeDtypeStruct((requests, events), jnp.bfloat16),
            pltpu.VMEM(mlp_weight.shape, mlp_weight.dtype),
        ],
        scratch_shapes=[
            pltpu.VMEM(history.shape, history.dtype),
            pltpu.SemaphoreType.DMA((users + 1,)),
        ],
        compiler_params=pltpu.CompilerParams(vmem_limit_bytes=32 * MIB),
        cost_estimate=pl.CostEstimate(
            flops=4 * requests * events * key_width, bytes_accessed=1 << 24, transcendentals=0
        ),
        name="attend",
    )(inv_count, slots, near, far, usable, *in_hbm(history, mlp_weight))


def score_kernel(
    inv_ref,
    queries_ref,
    attended_ref,
    labels_ref,
    mlp_ref,
    logit_weight_ref,
    logits_ref,
    grad_att_ref,
    direct_ref,
    grad_pre_ref,
):
    users = inv_ref.shape[0]
    per_user = queries_ref.shape[0] // users
    step_users = math.gcd(users, 2)
    step_rows = step_users * per_user
    key_width = queries_ref.shape[1]
    weight = logit_weight_ref[...].astype(jnp.float32)
    for first in range(0, users, step_users):
        at = slice(first * per_user, first * per_user + step_rows)
        query_b = queries_ref[at, :]
        query_f = query_b.astype(jnp.float32)
        attended = attended_ref[at, :]
        joined = jnp.concatenate(
            [query_b, attended.astype(jnp.bfloat16), (query_f * attended).astype(jnp.bfloat16)],
            axis=1,
        )
        pre_act = dot(joined, mlp_ref[...])
        act_sig = 0.5 * jnp.tanh(0.5 * pre_act) + 0.5
        hidden_units = (pre_act * act_sig).astype(jnp.bfloat16)
        logits = jnp.sum(hidden_units.astype(jnp.float32) * weight, axis=1, keepdims=True)
        logits_ref[at, :] = logits
        dlogit = (0.5 * jnp.tanh(0.5 * logits) + 0.5) - labels_ref[at, :].astype(jnp.float32)
        slope = act_sig * (1.0 + pre_act * (1.0 - act_sig))
        grad_pre = (dlogit * weight * slope).astype(jnp.bfloat16)
        grad_pre_ref[at, :] = grad_pre
    djoined = dot_rows(grad_pre_ref[...], mlp_ref[...])
    part_att = djoined[:, key_width : 2 * key_width]
    part_prod = djoined[:, 2 * key_width :]
    for user in range(users):
        at = slice(user * per_user, (user + 1) * per_user)
        grad_att = part_att[at] + part_prod[at] * queries_ref[at, :].astype(jnp.float32)
        grad_att_ref[at, :] = (grad_att * inv_ref[user]).astype(jnp.bfloat16)
    direct_ref[...] = djoined[:, :key_width] + part_prod * attended_ref[...]


def score(inv_count, queries, attended, labels, mlp_weight, logit_weight):
    requests, key_width = queries.shape
    whole = pl.BlockSpec(memory_space=pltpu.VMEM)
    return pl.pallas_call(
        score_kernel,
        in_specs=[pl.BlockSpec(memory_space=pltpu.SMEM)] + [whole] * 5,
        out_specs=[whole] * 3,
        out_shape=[
            jax.ShapeDtypeStruct((requests, 1), jnp.float32),
            jax.ShapeDtypeStruct((requests, key_width), jnp.bfloat16),
            jax.ShapeDtypeStruct((requests, key_width), jnp.float32),
        ],
        scratch_shapes=[pltpu.VMEM((requests, mlp_weight.shape[1]), jnp.bfloat16)],
        compiler_params=pltpu.CompilerParams(vmem_limit_bytes=32 * MIB),
        cost_estimate=pl.CostEstimate(
            flops=4 * requests * mlp_weight.shape[0] * mlp_weight.shape[1],
            bytes_accessed=1 << 23,
            transcendentals=0,
        ),
        name="score",
    )(inv_count, queries, attended, labels, mlp_weight, logit_weight)


def attend_back_kernel(first, grad_att_ref, direct_ref, slope_ref, history_ref, grad_rows_ref):
    users, events, key_width = history_ref.shape
    per_user = grad_att_ref.shape[0] // users
    chunk = math.gcd(events, 2048)
    for user in range(grad_rows_ref.shape[0] // per_user):
        rows = slice((first + user) * per_user, (first + user + 1) * per_user)
        back = jnp.zeros((per_user, key_width), jnp.float32)
        for at in range(0, events, chunk):
            keys = history_ref[first + user, at : at + chunk, :]
            slope = slope_ref[rows, at : at + chunk].astype(jnp.float32)
            grad_sig = (dot_rows(grad_att_ref[rows, :], keys) * slope).astype(jnp.bfloat16)
            back += dot(grad_sig, keys)
        grad_rows = direct_ref[rows, :] + back * (1.0 / math.sqrt(key_width))
        grad_rows_ref[user * per_user : (user + 1) * per_user, :] = grad_rows.astype(jnp.bfloat16)


def attend_back(first, count, grad_att, direct, slope, history):
    users, events, key_width = history.shape
    per_user = grad_att.shape[0] // users
    whole = pl.BlockSpec(memory_space=pltpu.VMEM)
    return pl.pallas_call(
        functools.partial(attend_back_kernel, first),
        in_specs=[whole] * 4,
        out_specs=whole,
        out_shape=jax.ShapeDtypeStruct((count * per_user, key_width), jnp.bfloat16),
        compiler_params=pltpu.CompilerParams(vmem_limit_bytes=20 * MIB),
        cost_estimate=pl.CostEstimate(
            flops=4 * count * per_user * events * key_width,
            bytes_accessed=1 << 23,
            transcendentals=0,
        ),
        name="attend_back",
    )(grad_att, direct, slope, history)


def join_rows(parts, joined_ref):
    at = 0
    for part in parts:
        joined_ref[at : at + part.shape[0], :] = part[...]
        at += part.shape[0]


def sum_rows(cands, at, slots_ref, grad_rows_ref):
    places = lax.broadcasted_iota(jnp.int32, (cands, slots_ref.shape[1]), 0) + at
    return dot((places == slots_ref[...]).astype(jnp.bfloat16), grad_rows_ref[...])


def cand_grad_kernel(slots_ref, grad_rows_ref, cand_grad_ref):
    cands = cand_grad_ref.shape[0]
    chunk = math.gcd(cands, 512)
    for at in range(0, cands, chunk):
        cand_grad_ref[at : at + chunk, :] = sum_rows(chunk, at, slots_ref, grad_rows_ref)


def sum_by_cand(cands, slots, grad_rows):
    requests, key_width = grad_rows.shape
    whole = pl.BlockSpec(memory_space=pltpu.VMEM)
    return pl.pallas_call(
        cand_grad_kernel,
        in_specs=[whole] * 2,
        out_specs=whole,
        out_shape=jax.ShapeDtypeStruct((cands, key_width), jnp.float32),
        compiler_params=pltpu.CompilerParams(vmem_limit_bytes=20 * MIB),
        cost_estimate=pl.CostEstimate(
            flops=2 * cands * key_width * requests, bytes_accessed=1 << 22, transcendentals=0
        ),
        name="sum_by_cand",
    )(slots, grad_rows)


def terms_kernel(
    origins,
    wide_ref,
    cand_grad_ref,
    slots_ref,
    pooled_ref,
    *refs,
):
    *parts, out_ref, grad_rows_ref, terms_ref = refs
    join_rows(parts, grad_rows_ref)
    cands = pooled_ref.shape[0]
    chunk = math.gcd(cands, 512)
    for at in range(0, cands, chunk):
        cand_grad = cand_grad_ref[at : at + chunk, :] + sum_rows(
            chunk, at, slots_ref, grad_rows_ref
        )
        term = dot_columns(pooled_ref[at : at + chunk, :], cand_grad.astype(jnp.bfloat16))
        if at == 0:
            terms_ref[...] = term
        else:
            terms_ref[...] += term
    rows = terms_ref.shape[0] // len(origins)
    wide = wide_ref[0]
    batch = max(1, 32 // rows)
    for slot in range(0, len(origins), batch):
        found = [
            terms_ref[pl.ds(pl.multiple_of((wide ^ origins[slot + i]) * rows, rows), rows), :]
            for i in range(batch)
        ]
        found = found[0] if batch == 1 else jnp.concatenate(found, axis=0)
        out_ref[slot * rows : (slot + batch) * rows, :] = found.astype(jnp.bfloat16)


def chip_terms(origins, wide, cand_grad, slots, grad_parts, pooled):
    cands, width = pooled.shape
    requests, key_width = slots.shape[1], cand_grad.shape[1]
    whole = pl.BlockSpec(memory_space=pltpu.VMEM)
    return pl.pallas_call(
        functools.partial(terms_kernel, origins),
        in_specs=[pl.BlockSpec(memory_space=pltpu.SMEM)] + [whole] * (3 + len(grad_parts)),
        out_specs=whole,
        out_shape=jax.ShapeDtypeStruct((width, key_width), jnp.bfloat16),
        scratch_shapes=[
            pltpu.VMEM((requests, key_width), jnp.bfloat16),
            pltpu.VMEM((width, key_width), jnp.float32),
        ],
        compiler_params=pltpu.CompilerParams(vmem_limit_bytes=20 * MIB),
        cost_estimate=pl.CostEstimate(
            flops=2 * cands * key_width * (width + requests),
            bytes_accessed=1 << 22,
            transcendentals=0,
        ),
        name="chip_terms",
    )(wide, cand_grad, slots, pooled, *grad_parts)


def bit_groups(size):
    groups = []
    bit = 0
    while (1 << bit) < size:
        values = min(4, size >> bit)
        groups.append((bit, values))
        bit += values.bit_length() - 1
    return groups


def exchange(values, axis_name, size, distance):
    return lax.ppermute(values, axis_name, [(i, i ^ distance) for i in range(size)])


def send_stage(rows, wides, bit, values):
    found = [exchange(rows, "wide", wides, step << bit) for step in reversed(range(1, values))]
    return found[::-1]


def after(values, *others):
    return lax.optimization_barrier((tuple(values),) + others)[0]


def slot_of(distance, wides):
    slot = 0
    for bit, values in bit_groups(wides):
        slot = slot * values + ((distance >> bit) & (values - 1))
    return slot


def sum_blocks(blocks, wides, logits):
    total = blocks
    for bit, values in bit_groups(wides):
        if bit > 0:
            total, logits = lax.optimization_barrier((total, logits))
        parts = total.astype(jnp.bfloat16).reshape((values, -1) + blocks.shape[1:])
        found = [
            exchange(parts[step], "wide", wides, step << bit).astype(jnp.float32)
            for step in reversed(range(1, values))
        ]
        total = sum(found, parts[0].astype(jnp.float32))
    return total, logits


def body(
    frames,
    qkv_weight,
    out_weight,
    proj_weight,
    mlp_weight,
    logit_weight,
    history,
    hist_len,
    hist_mask,
    req_owner,
    req_local,
    labels,
):
    wides = lax.axis_size("wide")
    core, wide = lax.axis_index("section"), lax.axis_index("wide")
    cand_count = frames.shape[0]
    requests = req_local.shape[0]
    users, events, _ = history.shape
    keep, send, embedded = encode_block(
        core.reshape(1), frames, qkv_weight, out_weight, proj_weight
    )
    positions = jnp.arange(events, dtype=jnp.int32)[None, :]
    usable = (
        (positions < hist_len[:, None]) & ((hist_mask == 1) | (positions == 0))
    ).astype(jnp.float32)
    inv_count = lax.rsqrt(jnp.sum(usable, axis=1))
    usable = usable.reshape(users, 1, events)
    owner_core = req_owner[:, 0] // wides
    owner_slot = slot_of((req_owner[:, 0] % wides) ^ wide, wides)
    slots = ((owner_core ^ core) * wides + owner_slot) * cand_count + req_local
    pooled_slots = (owner_slot * 2 + owner_core) * cand_count + req_local
    stages = list(reversed(bit_groups(wides)))
    near, pooled = embedded, None
    for place, stage in enumerate(stages):
        found = send_stage(near, wides, *stage)
        if place == 0:
            got = exchange(send, "section", 2, 1)
            far_slots = exchange(pooled_slots, "section", 2, 1)
            found, keep, got, far_slots = lax.optimization_barrier((found[::-1], keep, got, far_slots))
            found = found[::-1]
            pooled = jnp.where(
                core == 0,
                jnp.concatenate([keep, got], axis=0),
                jnp.concatenate([got, keep], axis=0),
            )
        else:
            bit, values = stages[place - 1]
            paired = exchange(pooled, "wide", wides, 1 << bit)
            found, paired = lax.optimization_barrier((found[::-1], paired))
            found = found[::-1]
            pooled_parts = [jnp.concatenate([pooled, paired], axis=0)]
            if values > 2:
                pooled_parts.append(exchange(pooled_parts[0], "wide", wides, 2 << bit))
            if place + 1 < len(stages):
                pooled = jnp.concatenate(pooled_parts, axis=0)
        near = jnp.concatenate([near] + found, axis=0)
    far = exchange(near, "section", 2, 1)
    queries, attended, slope, mlp_weight = attend(
        inv_count, slots.reshape(requests, 1), near, far, history, usable, mlp_weight
    )
    pooled = jnp.concatenate(after(pooled_parts, attended), axis=0)
    found_pooled = send_stage(pooled, wides, *stages[-1])
    logits, grad_att, direct = score(
        inv_count,
        queries,
        attended,
        labels.reshape(requests, 1),
        mlp_weight,
        logit_weight.reshape(1, -1),
    )
    half = max(1, users - 1)
    first_rows = attend_back(0, half, grad_att, direct, slope, history)
    first_count = first_rows.shape[0]
    cands = cand_count * wides * 2
    cand_grad = sum_by_cand(cands, pooled_slots[:first_count].reshape(1, first_count), first_rows)
    found_pooled, grad_att, first_rows, cand_grad = lax.optimization_barrier(
        (found_pooled[::-1], grad_att, first_rows, cand_grad)
    )
    pooled = jnp.concatenate([pooled] + found_pooled[::-1], axis=0)
    second_rows = attend_back(half, users - half, grad_att, direct, slope, history)
    far_parts = [exchange(part, "section", 2, 1) for part in (first_rows, second_rows)]
    rest_slots = jnp.concatenate([pooled_slots[first_count:], far_slots])
    origins = [0] * wides
    for distance in range(wides):
        origins[slot_of(distance, wides)] = distance
    terms = chip_terms(
        origins,
        wide.reshape(1),
        cand_grad,
        rest_slots.reshape(1, -1),
        [second_rows] + far_parts,
        pooled,
    )
    grad_proj, logits = sum_blocks(terms, wides, logits.reshape(requests))
    return (logits, grad_proj)


def solution(mesh):
    in_specs = (
        P(("section", "wide"), None, None),
        P(),
        P(),
        P(),
        P(),
        P(),
        P(("section", "wide"), None, None),
        P(("section", "wide")),
        P(("section", "wide"), None),
        P(("section", "wide"), None),
        P(("section", "wide")),
        P(("section", "wide")),
    )
    out_specs = (P(("section", "wide")), P(("section", "wide"), None))
    return jax.shard_map(body, mesh=mesh, in_specs=in_specs, out_specs=out_specs, check_vma=False)
```

```python
import functools
import math

import jax
import jax.numpy as jnp
from jax import lax
from jax.experimental import pallas as pl
from jax.experimental.pallas import tpu as pltpu
from jax.sharding import PartitionSpec as P

HEADS = 16
FRAMES = 3


EPSILON = 1e-06
MIB = 1024 * 1024


def layer_norm(values):
    center = values - jnp.mean(values, axis=-1, keepdims=True)
    spread = jnp.mean(jnp.square(center), axis=-1, keepdims=True)
    return center * lax.rsqrt(spread + EPSILON)


def dot(left, right):
    return jnp.dot(left, right, preferred_element_type=jnp.float32)


def dot_rows(left, right):
    return lax.dot_general(left, right, (((1,), (1,)), ((), ())), preferred_element_type=jnp.float32)


def dot_columns(left, right):
    return lax.dot_general(left, right, (((0,), (0,)), ((), ())), preferred_element_type=jnp.float32)


def split_rows(values):
    high = values.astype(jnp.bfloat16)
    low = (values - high.astype(jnp.float32)).astype(jnp.bfloat16)
    return jnp.concatenate([high, low], axis=0)


def dot_split(values, right):
    both = dot(split_rows(values), right)
    rows = values.shape[0]
    return both[:rows] + both[rows:]


def encode_kernel(
    tokens,
    core_ref,
    frames_hbm,
    qkv_hbm,
    out_hbm,
    proj_hbm,
    keep_ref,
    send_ref,
    embedded_ref,
    frames_ref,
    qkv_ref,
    out_ref,
    proj_ref,
    sems,
    normed_ref,
    packed_ref,
    scores_ref,
    mixed_rows_ref,
    sums_ref,
):
    total = embedded_ref.shape[0]
    rows, width = packed_ref.shape[0], packed_ref.shape[1] // 2
    cands = rows // tokens
    groups = total // cands
    head_dim = width // HEADS
    patches = tokens // FRAMES
    lanes = 2 * head_dim
    blocks = rows // lanes
    pairs = HEADS // 2
    quad = 4
    span = quad * head_dim

    def group_rows(group):
        return pl.ds(group * rows, rows)

    def columns(part):
        return pl.ds(part * width, width)

    first_rows = cands // 2 * tokens
    pieces = [
        (frames_hbm.at[pl.ds(at, count)], frames_ref.at[pl.ds(at, count)])
        for at, count in ((0, first_rows), (first_rows, rows - first_rows))
    ]
    pieces += [(qkv_hbm.at[:, columns(part)], qkv_ref.at[:, columns(part)]) for part in range(2)]
    pieces += [
        (frames_hbm.at[group_rows(group)], frames_ref.at[group_rows(group)])
        for group in range(1, groups)
    ]
    pieces += [(qkv_hbm.at[:, columns(2)], qkv_ref.at[:, columns(2)])]
    pieces += [(out_hbm, out_ref), (proj_hbm, proj_ref)]
    copies = [
        pltpu.make_async_copy(source, target, sems.at[place])
        for place, (source, target) in enumerate(pieces)
    ]
    copies[0].start()
    copies[1].start()

    def norm_cand(cand):
        at = slice(cand * tokens, (cand + 1) * tokens)
        inputs = frames_ref[at, :].astype(jnp.float32)
        normed_ref[at, :] = layer_norm(inputs).astype(jnp.bfloat16)
        sums_ref[cand] = jnp.sum(inputs, axis=0, keepdims=True)

    exponent = math.log2(math.e) / math.sqrt(head_dim)
    frame_at = (lax.broadcasted_iota(jnp.int32, (patches, quad * lanes), 1) % lanes) // patches
    nothing = jnp.zeros((head_dim, lanes), jnp.bfloat16)
    ones_row = lax.broadcasted_iota(jnp.int32, (2 * lanes, 2 * lanes), 0) // patches
    ones_column = lax.broadcasted_iota(jnp.int32, (2 * lanes, 2 * lanes), 1) // patches
    frame_ones = (ones_row == ones_column).astype(jnp.bfloat16)
    own = lax.broadcasted_iota(jnp.int32, (cands, rows), 1) // tokens == lax.broadcasted_iota(
        jnp.int32, (cands, rows), 0
    )

    def own_scores(block, head):
        block_rows = slice(block * lanes, (block + 1) * lanes)
        start = head * head_dim
        query = packed_ref[block_rows, start : start + span]
        keys = packed_ref[block_rows, width + start : width + start + span].T
        keys = jnp.concatenate(
            [
                jnp.concatenate(
                    [nothing] * place
                    + [keys[place * head_dim : (place + 1) * head_dim]]
                    + [nothing] * (quad - 1 - place),
                    axis=1,
                )
                for place in range(quad)
            ],
            axis=0,
        )
        scores = dot(query, keys)
        found = scores[:patches]
        for frame in range(1, lanes // patches):
            found = jnp.where(
                frame_at == frame, scores[frame * patches : (frame + 1) * patches], found
            )
        for side in range(quad // 2):
            scores_ref[block, head // 2 + side] = found[
                :, side * 2 * lanes : (side + 1) * 2 * lanes
            ]

    for side in range(2):
        copies[side].wait()
        copies[2 + side].start()
        for cand in range(side * (cands // 2), cands if side else cands // 2):
            norm_cand(cand)
    copies[2].wait()
    for copy in copies[4 : 3 + groups]:
        copy.start()
    for group in range(groups):
        at = slice(group * rows, (group + 1) * rows)
        for part in range(2):
            if group == 0 and part == 1:
                copies[3].wait()
                for copy in copies[3 + groups :]:
                    copy.start()
            part_columns = slice(part * width, (part + 1) * width)
            packed_ref[:, part_columns] = dot(normed_ref[at, :], qkv_ref[:, part_columns]).astype(
                jnp.bfloat16
            )
            if group + 1 < groups:
                if part == 0:
                    copies[4 + group].wait()
                for cand in range(part * cands // 2, (part + 1) * cands // 2):
                    norm_cand((group + 1) * cands + cand)
        for head in range(0, HEADS, quad):
            for block in range(blocks):
                own_scores(block, head)
        exp_scores = jnp.exp2(
            scores_ref[...].reshape(blocks * pairs * patches, 2 * lanes) * exponent
        )
        totals = dot(exp_scores.astype(jnp.bfloat16), frame_ones)
        probs = (exp_scores / totals).reshape(blocks * pairs, patches, 2 * lanes)
        sums = jnp.sum(probs, axis=1)
        key_sums = [
            jnp.concatenate(
                [
                    sums[block * pairs : (block + 1) * pairs, side * lanes : (side + 1) * lanes]
                    for block in range(blocks)
                ],
                axis=1,
            )
            for side in range(2)
        ]
        spread = jnp.concatenate(
            [
                jnp.where(own, key_sums[head % 2][head // 2 : head // 2 + 1], 0.0)
                for head in range(HEADS)
            ],
            axis=0,
        ).astype(jnp.bfloat16)
        mixed_rows = dot(spread, normed_ref[at, :])
        for head in range(HEADS):
            mixed_rows_ref[head, group * cands : (group + 1) * cands, :] = mixed_rows[
                head * cands : (head + 1) * cands
            ]

    for copy in copies[3 + groups :]:
        copy.wait()
    mixed = []
    for head in range(0, HEADS, quad):
        left = mixed_rows_ref[head : head + quad].reshape(quad * total, width)
        start = 2 * width + head * head_dim
        both = dot(left.astype(jnp.bfloat16), qkv_ref[:, start : start + span])
        head_at = lax.broadcasted_iota(jnp.int32, (total, span), 1) // head_dim
        piece = jnp.zeros((total, span), jnp.float32)
        for place in range(quad):
            piece = jnp.where(head_at == place, both[place * total : (place + 1) * total], piece)
        mixed.append(piece)
    mixed_mean = jnp.concatenate(mixed, axis=1) * (1.0 / tokens)
    hidden = sums_ref[...].reshape(total, width) * (1.0 / tokens)
    hidden += dot_split(mixed_mean, out_ref[...])
    pooled = layer_norm(hidden).astype(jnp.bfloat16)
    first, second = pooled[:, : width // 2], pooled[:, width // 2 :]
    keep_ref[...] = jnp.where(core_ref[0] == 0, first, second)
    send_ref[...] = jnp.where(core_ref[0] == 0, second, first)
    embedded_ref[...] = dot(pooled, proj_ref[...]).astype(jnp.bfloat16)


def in_hbm(*arrays):
    return [pltpu.with_memory_space_constraint(array, pltpu.HBM) for array in arrays]


def encode_block(core, frames, qkv_weight, out_weight, proj_weight):
    cand_count, tokens, width = frames.shape
    key_width = proj_weight.shape[1]
    groups = 2
    rows = cand_count * tokens // groups
    lanes = 2 * width // HEADS
    patches = tokens // FRAMES
    flat = frames.reshape(cand_count * tokens, width)
    whole = pl.BlockSpec(memory_space=pltpu.VMEM)
    return pl.pallas_call(
        functools.partial(encode_kernel, tokens),
        in_specs=[pl.BlockSpec(memory_space=pltpu.SMEM)]
        + [pl.BlockSpec(memory_space=pltpu.HBM)] * 4,
        out_specs=[whole] * 3,
        out_shape=[
            jax.ShapeDtypeStruct((cand_count, width // 2), jnp.bfloat16),
            jax.ShapeDtypeStruct((cand_count, width // 2), jnp.bfloat16),
            jax.ShapeDtypeStruct((cand_count, key_width), jnp.bfloat16),
        ],
        scratch_shapes=[
            pltpu.VMEM(flat.shape, jnp.bfloat16),
            pltpu.VMEM(qkv_weight.shape, jnp.bfloat16),
            pltpu.VMEM(out_weight.shape, jnp.bfloat16),
            pltpu.VMEM(proj_weight.shape, jnp.bfloat16),
            pltpu.SemaphoreType.DMA((groups + 6,)),
            pltpu.VMEM(flat.shape, jnp.bfloat16),
            pltpu.VMEM((rows, 2 * width), jnp.bfloat16),
            pltpu.VMEM((rows // lanes, HEADS // 2, patches, 2 * lanes), jnp.float32),
            pltpu.VMEM((HEADS, cand_count, width), jnp.float32),
            pltpu.VMEM((cand_count, 1, width), jnp.float32),
        ],
        compiler_params=pltpu.CompilerParams(vmem_limit_bytes=44 * MIB),
        cost_estimate=pl.CostEstimate(
            flops=5 * cand_count * tokens * width * width, bytes_accessed=1 << 24, transcendentals=0
        ),
        name="encode",
    )(core, *in_hbm(flat, qkv_weight, out_weight, proj_weight))


def attend_kernel(
    inv_ref,
    slots_ref,
    near_ref,
    far_ref,
    usable_ref,
    history_hbm,
    mlp_hbm,
    queries_ref,
    attended_ref,
    slope_ref,
    mlp_ref,
    history_ref,
    sems,
):
    users, events, _ = history_ref.shape
    chunk = math.gcd(events, 2048)
    copies = [
        pltpu.make_async_copy(history_hbm.at[user], history_ref.at[user], sems.at[user])
        for user in range(users)
    ]
    copies.append(pltpu.make_async_copy(mlp_hbm, mlp_ref, sems.at[users]))
    copies[0].start()
    slots = slots_ref[...]
    half, key_width = near_ref.shape
    places = lax.broadcasted_iota(jnp.int32, (slots.shape[0], half), 1)
    queries = dot((slots == places).astype(jnp.bfloat16), near_ref[...])
    copies[1].start()
    queries += dot((slots == places + half).astype(jnp.bfloat16), far_ref[...])
    queries_ref[...] = queries.astype(jnp.bfloat16)
    per_user = slots.shape[0] // users
    for user in range(users):
        copies[user].wait()
        if user + 2 < len(copies):
            copies[user + 2].start()
        rows = slice(user * per_user, (user + 1) * per_user)
        attended = jnp.zeros((per_user, key_width), jnp.float32)
        for at in range(0, events, chunk):
            keys = history_ref[user, at : at + chunk, :]
            usable = usable_ref[user, :, at : at + chunk]
            scores = dot_rows(queries_ref[rows, :], keys)
            half_gate = 0.5 * jnp.tanh(scores * (0.5 / math.sqrt(key_width)))
            weights = (0.5 + half_gate) * usable
            slope_ref[rows, at : at + chunk] = (weights * (0.5 - half_gate)).astype(jnp.bfloat16)
            attended += dot(weights.astype(jnp.bfloat16), keys)
        attended_ref[rows, :] = attended * inv_ref[user]
    copies[users].wait()


def attend(inv_count, slots, near, far, history, usable, mlp_weight):
    users, events, key_width = history.shape
    requests = slots.shape[0]
    whole = pl.BlockSpec(memory_space=pltpu.VMEM)
    return pl.pallas_call(
        attend_kernel,
        in_specs=[pl.BlockSpec(memory_space=pltpu.SMEM)]
        + [whole] * 4
        + [pl.BlockSpec(memory_space=pltpu.HBM)] * 2,
        out_specs=[whole] * 4,
        out_shape=[
            jax.ShapeDtypeStruct((requests, key_width), jnp.bfloat16),
            jax.ShapeDtypeStruct((requests, key_width), jnp.float32),
            jax.ShapeDtypeStruct((requests, events), jnp.bfloat16),
            pltpu.VMEM(mlp_weight.shape, mlp_weight.dtype),
        ],
        scratch_shapes=[
            pltpu.VMEM(history.shape, history.dtype),
            pltpu.SemaphoreType.DMA((users + 1,)),
        ],
        compiler_params=pltpu.CompilerParams(vmem_limit_bytes=32 * MIB),
        cost_estimate=pl.CostEstimate(
            flops=4 * requests * events * key_width, bytes_accessed=1 << 24, transcendentals=0
        ),
        name="attend",
    )(inv_count, slots, near, far, usable, *in_hbm(history, mlp_weight))


def score_kernel(
    inv_ref,
    queries_ref,
    attended_ref,
    labels_ref,
    mlp_ref,
    logit_weight_ref,
    logits_ref,
    grad_att_ref,
    direct_ref,
    grad_pre_ref,
):
    users = inv_ref.shape[0]
    per_user = queries_ref.shape[0] // users
    step_users = math.gcd(users, 2)
    step_rows = step_users * per_user
    key_width = queries_ref.shape[1]
    weight = logit_weight_ref[...].astype(jnp.float32)
    for first in range(0, users, step_users):
        at = slice(first * per_user, first * per_user + step_rows)
        query_b = queries_ref[at, :]
        query_f = query_b.astype(jnp.float32)
        attended = attended_ref[at, :]
        joined = jnp.concatenate(
            [query_b, attended.astype(jnp.bfloat16), (query_f * attended).astype(jnp.bfloat16)],
            axis=1,
        )
        pre_act = dot(joined, mlp_ref[...])
        act_sig = 0.5 * jnp.tanh(0.5 * pre_act) + 0.5
        hidden_units = (pre_act * act_sig).astype(jnp.bfloat16)
        logits = jnp.sum(hidden_units.astype(jnp.float32) * weight, axis=1, keepdims=True)
        logits_ref[at, :] = logits
        dlogit = (0.5 * jnp.tanh(0.5 * logits) + 0.5) - labels_ref[at, :].astype(jnp.float32)
        slope = act_sig * (1.0 + pre_act * (1.0 - act_sig))
        grad_pre = (dlogit * weight * slope).astype(jnp.bfloat16)
        grad_pre_ref[at, :] = grad_pre
    djoined = dot_rows(grad_pre_ref[...], mlp_ref[...])
    part_att = djoined[:, key_width : 2 * key_width]
    part_prod = djoined[:, 2 * key_width :]
    for user in range(users):
        at = slice(user * per_user, (user + 1) * per_user)
        grad_att = part_att[at] + part_prod[at] * queries_ref[at, :].astype(jnp.float32)
        grad_att_ref[at, :] = (grad_att * inv_ref[user]).astype(jnp.bfloat16)
    direct_ref[...] = djoined[:, :key_width] + part_prod * attended_ref[...]


def score(inv_count, queries, attended, labels, mlp_weight, logit_weight):
    requests, key_width = queries.shape
    whole = pl.BlockSpec(memory_space=pltpu.VMEM)
    return pl.pallas_call(
        score_kernel,
        in_specs=[pl.BlockSpec(memory_space=pltpu.SMEM)] + [whole] * 5,
        out_specs=[whole] * 3,
        out_shape=[
            jax.ShapeDtypeStruct((requests, 1), jnp.float32),
            jax.ShapeDtypeStruct((requests, key_width), jnp.bfloat16),
            jax.ShapeDtypeStruct((requests, key_width), jnp.float32),
        ],
        scratch_shapes=[pltpu.VMEM((requests, mlp_weight.shape[1]), jnp.bfloat16)],
        compiler_params=pltpu.CompilerParams(vmem_limit_bytes=32 * MIB),
        cost_estimate=pl.CostEstimate(
            flops=4 * requests * mlp_weight.shape[0] * mlp_weight.shape[1],
            bytes_accessed=1 << 23,
            transcendentals=0,
        ),
        name="score",
    )(inv_count, queries, attended, labels, mlp_weight, logit_weight)


def attend_back_kernel(first, grad_att_ref, direct_ref, slope_ref, history_ref, grad_rows_ref):
    users, events, key_width = history_ref.shape
    per_user = grad_att_ref.shape[0] // users
    chunk = math.gcd(events, 2048)
    for user in range(grad_rows_ref.shape[0] // per_user):
        rows = slice((first + user) * per_user, (first + user + 1) * per_user)
        back = jnp.zeros((per_user, key_width), jnp.float32)
        for at in range(0, events, chunk):
            keys = history_ref[first + user, at : at + chunk, :]
            slope = slope_ref[rows, at : at + chunk].astype(jnp.float32)
            grad_sig = (dot_rows(grad_att_ref[rows, :], keys) * slope).astype(jnp.bfloat16)
            back += dot(grad_sig, keys)
        grad_rows = direct_ref[rows, :] + back * (1.0 / math.sqrt(key_width))
        grad_rows_ref[user * per_user : (user + 1) * per_user, :] = grad_rows.astype(jnp.bfloat16)


def attend_back(first, count, grad_att, direct, slope, history):
    users, events, key_width = history.shape
    per_user = grad_att.shape[0] // users
    whole = pl.BlockSpec(memory_space=pltpu.VMEM)
    return pl.pallas_call(
        functools.partial(attend_back_kernel, first),
        in_specs=[whole] * 4,
        out_specs=whole,
        out_shape=jax.ShapeDtypeStruct((count * per_user, key_width), jnp.bfloat16),
        compiler_params=pltpu.CompilerParams(vmem_limit_bytes=20 * MIB),
        cost_estimate=pl.CostEstimate(
            flops=4 * count * per_user * events * key_width,
            bytes_accessed=1 << 23,
            transcendentals=0,
        ),
        name="attend_back",
    )(grad_att, direct, slope, history)


def join_rows(parts, joined_ref):
    at = 0
    for part in parts:
        joined_ref[at : at + part.shape[0], :] = part[...]
        at += part.shape[0]


def sum_rows(cands, at, slots_ref, grad_rows_ref):
    places = lax.broadcasted_iota(jnp.int32, (cands, slots_ref.shape[1]), 0) + at
    return dot((places == slots_ref[...]).astype(jnp.bfloat16), grad_rows_ref[...])


def cand_grad_kernel(slots_ref, first_ref, second_ref, cand_grad_ref, grad_rows_ref):
    join_rows((first_ref, second_ref), grad_rows_ref)
    cands = cand_grad_ref.shape[0]
    chunk = math.gcd(cands, 512)
    for at in range(0, cands, chunk):
        cand_grad_ref[at : at + chunk, :] = sum_rows(chunk, at, slots_ref, grad_rows_ref)


def own_cand_grad(cands, slots, grad_parts):
    requests, key_width = slots.shape[1], grad_parts[0].shape[1]
    whole = pl.BlockSpec(memory_space=pltpu.VMEM)
    return pl.pallas_call(
        cand_grad_kernel,
        in_specs=[whole] * 3,
        out_specs=whole,
        out_shape=jax.ShapeDtypeStruct((cands, key_width), jnp.float32),
        scratch_shapes=[pltpu.VMEM((requests, key_width), jnp.bfloat16)],
        compiler_params=pltpu.CompilerParams(vmem_limit_bytes=20 * MIB),
        cost_estimate=pl.CostEstimate(
            flops=2 * cands * key_width * requests, bytes_accessed=1 << 22, transcendentals=0
        ),
        name="own_cand_grad",
    )(slots, *grad_parts)


def terms_kernel(
    origins,
    wide_ref,
    cand_grad_ref,
    slots_ref,
    first_ref,
    second_ref,
    pooled_ref,
    out_ref,
    grad_rows_ref,
    terms_ref,
):
    join_rows((first_ref, second_ref), grad_rows_ref)
    cands = pooled_ref.shape[0]
    chunk = math.gcd(cands, 512)
    for at in range(0, cands, chunk):
        cand_grad = cand_grad_ref[at : at + chunk, :] + sum_rows(
            chunk, at, slots_ref, grad_rows_ref
        )
        term = dot_columns(pooled_ref[at : at + chunk, :], cand_grad.astype(jnp.bfloat16))
        if at == 0:
            terms_ref[...] = term
        else:
            terms_ref[...] += term
    rows = terms_ref.shape[0] // len(origins)
    wide = wide_ref[0]
    batch = max(1, 32 // rows)
    for slot in range(0, len(origins), batch):
        found = [
            terms_ref[pl.ds(pl.multiple_of((wide ^ origins[slot + i]) * rows, rows), rows), :]
            for i in range(batch)
        ]
        found = found[0] if batch == 1 else jnp.concatenate(found, axis=0)
        out_ref[slot * rows : (slot + batch) * rows, :] = found.astype(jnp.bfloat16)


def chip_terms(origins, wide, cand_grad, far_slots, far_parts, pooled):
    cands, width = pooled.shape
    requests, key_width = far_slots.shape[1], cand_grad.shape[1]
    whole = pl.BlockSpec(memory_space=pltpu.VMEM)
    return pl.pallas_call(
        functools.partial(terms_kernel, origins),
        in_specs=[pl.BlockSpec(memory_space=pltpu.SMEM)] + [whole] * 5,
        out_specs=whole,
        out_shape=jax.ShapeDtypeStruct((width, key_width), jnp.bfloat16),
        scratch_shapes=[
            pltpu.VMEM((requests, key_width), jnp.bfloat16),
            pltpu.VMEM((width, key_width), jnp.float32),
        ],
        compiler_params=pltpu.CompilerParams(vmem_limit_bytes=20 * MIB),
        cost_estimate=pl.CostEstimate(
            flops=2 * cands * key_width * (width + requests),
            bytes_accessed=1 << 22,
            transcendentals=0,
        ),
        name="chip_terms",
    )(wide, cand_grad, far_slots, *far_parts, pooled)


def bit_groups(size):
    groups = []
    bit = 0
    while (1 << bit) < size:
        values = min(4, size >> bit)
        groups.append((bit, values))
        bit += values.bit_length() - 1
    return groups


def exchange(values, axis_name, size, distance):
    return lax.ppermute(values, axis_name, [(i, i ^ distance) for i in range(size)])


def send_stage(rows, wides, bit, values):
    found = [exchange(rows, "wide", wides, step << bit) for step in reversed(range(1, values))]
    return found[::-1]


def after(values, *others):
    return lax.optimization_barrier((tuple(values),) + others)[0]


def slot_of(distance, wides):
    slot = 0
    for bit, values in bit_groups(wides):
        slot = slot * values + ((distance >> bit) & (values - 1))
    return slot


def sum_blocks(blocks, wides, logits):
    total = blocks
    for bit, values in bit_groups(wides):
        if bit > 0:
            total, logits = lax.optimization_barrier((total, logits))
        parts = total.astype(jnp.bfloat16).reshape((values, -1) + blocks.shape[1:])
        found = [
            exchange(parts[step], "wide", wides, step << bit).astype(jnp.float32)
            for step in reversed(range(1, values))
        ]
        total = sum(found, parts[0].astype(jnp.float32))
    return total, logits


def body(
    frames,
    qkv_weight,
    out_weight,
    proj_weight,
    mlp_weight,
    logit_weight,
    history,
    hist_len,
    hist_mask,
    req_owner,
    req_local,
    labels,
):
    wides = lax.axis_size("wide")
    core, wide = lax.axis_index("section"), lax.axis_index("wide")
    cand_count = frames.shape[0]
    requests = req_local.shape[0]
    users, events, _ = history.shape
    keep, send, embedded = encode_block(
        core.reshape(1), frames, qkv_weight, out_weight, proj_weight
    )
    positions = jnp.arange(events, dtype=jnp.int32)[None, :]
    usable = (
        (positions < hist_len[:, None]) & ((hist_mask == 1) | (positions == 0))
    ).astype(jnp.float32)
    inv_count = lax.rsqrt(jnp.sum(usable, axis=1))
    usable = usable.reshape(users, 1, events)
    owner_core = req_owner[:, 0] // wides
    owner_slot = slot_of((req_owner[:, 0] % wides) ^ wide, wides)
    slots = ((owner_core ^ core) * wides + owner_slot) * cand_count + req_local
    pooled_slots = (owner_slot * 2 + owner_core) * cand_count + req_local
    stages = list(reversed(bit_groups(wides)))
    near, pooled = embedded, None
    for place, stage in enumerate(stages):
        found = send_stage(near, wides, *stage)
        if place == 0:
            got = exchange(send, "section", 2, 1)
            far_slots = exchange(pooled_slots, "section", 2, 1)
            found, keep, got, far_slots = lax.optimization_barrier((found[::-1], keep, got, far_slots))
            found = found[::-1]
            pooled = jnp.where(
                core == 0,
                jnp.concatenate([keep, got], axis=0),
                jnp.concatenate([got, keep], axis=0),
            )
        else:
            bit, values = stages[place - 1]
            paired = exchange(pooled, "wide", wides, 1 << bit)
            found, paired = lax.optimization_barrier((found[::-1], paired))
            found = found[::-1]
            pooled_parts = [jnp.concatenate([pooled, paired], axis=0)]
            if values > 2:
                pooled_parts.append(exchange(pooled_parts[0], "wide", wides, 2 << bit))
            if place + 1 < len(stages):
                pooled = jnp.concatenate(pooled_parts, axis=0)
        near = jnp.concatenate([near] + found, axis=0)
    far = exchange(near, "section", 2, 1)
    queries, attended, slope, mlp_weight = attend(
        inv_count, slots.reshape(requests, 1), near, far, history, usable, mlp_weight
    )
    pooled = jnp.concatenate(after(pooled_parts, attended), axis=0)
    found_pooled = send_stage(pooled, wides, *stages[-1])
    logits, grad_att, direct = score(
        inv_count,
        queries,
        attended,
        labels.reshape(requests, 1),
        mlp_weight,
        logit_weight.reshape(1, -1),
    )
    half = max(1, users - 1)
    first_rows = attend_back(0, half, grad_att, direct, slope, history)
    found_pooled, grad_att, first_rows = lax.optimization_barrier(
        (found_pooled[::-1], grad_att, first_rows)
    )
    pooled = jnp.concatenate([pooled] + found_pooled[::-1], axis=0)
    grad_parts = [first_rows, attend_back(half, users - half, grad_att, direct, slope, history)]
    far_parts = [exchange(part, "section", 2, 1) for part in grad_parts]
    cand_grad = own_cand_grad(pooled.shape[0], pooled_slots.reshape(1, requests), grad_parts)
    origins = [0] * wides
    for distance in range(wides):
        origins[slot_of(distance, wides)] = distance
    terms = chip_terms(
        origins,
        wide.reshape(1),
        cand_grad,
        far_slots.reshape(1, requests),
        far_parts,
        pooled,
    )
    grad_proj, logits = sum_blocks(terms, wides, logits.reshape(requests))
    return (logits, grad_proj)


def solution(mesh):
    in_specs = (
        P(("section", "wide"), None, None),
        P(),
        P(),
        P(),
        P(),
        P(),
        P(("section", "wide"), None, None),
        P(("section", "wide")),
        P(("section", "wide"), None),
        P(("section", "wide"), None),
        P(("section", "wide")),
        P(("section", "wide")),
    )
    out_specs = (P(("section", "wide")), P(("section", "wide"), None))
    return jax.shard_map(body, mesh=mesh, in_specs=in_specs, out_specs=out_specs, check_vma=False)
```
